128 devices in a mesh: seq: 8 (over x_hi, z), res: 16 (over y, x_lo, core).
Axes of the slice: x: 4 (x_hi: 2, x_lo: 2; x = x_hi * 2 + x_lo), y: 4, z: 4, core: 2. Of those that a mesh axis runs over, the one named last changes fastest.
Arguments:
- multiple_alignment_rep: bfloat16 [256, 512, 256], P('seq', 'res'), may hold values from -6 to 6
- pair_rep: bfloat16 [512, 512, 128], P('res'), may hold values from -6 to 6
- aligned_member_valid: int32 [256], replicated, may hold values from 0 to 1
- chain_position_valid: int32 [512], replicated, may hold values from 0 to 1
- horizontal_entry_matrices: bfloat16 [256, 1024], replicated, may hold values from -4 to 4
- horizontal_exit_matrix: bfloat16 [256, 256], replicated, may hold values from -0.375 to 0.375
- bias_proj: bfloat16 [128, 8], replicated, may hold values from -0.5 to 0.5
- vertical_entry_matrices: bfloat16 [256, 1024], replicated, may hold values from -4 to 4
- vertical_exit_matrix: bfloat16 [256, 256], replicated, may hold values from -0.375 to 0.375
- dyadic_projection_matrices: bfloat16 [256, 64], replicated, may hold values from -0.375 to 0.375
- outer_out: bfloat16 [1024, 128], replicated, may hold values from -2.5 to 2.5
- pair_grad: bfloat16 [512, 512, 128], P('res'), may hold values from -6 to 6
Outputs:
- alignment_refreshed: bfloat16 [256, 512, 256], P('seq', 'res')
- couple_delta: bfloat16 [512, 512, 128], P('res')
- refreshed_alignment_cotangent: bfloat16 [256, 512, 256], P('seq', 'res')
The draws below stay inside these ranges and needn't reach their ends.
All inputs are finite; a program needn't handle non-finite values.
Results may differ from the reference program's by a relative error of at most 0.03.
Values may be sent and summed in bfloat16 or wider, within the bound.
No kernel may reach another device: no remote copies, remote signals or barrier semaphores. Data moves between devices by JAX's collectives and lax.ppermute only.
A program may use at most 256 MiB of HBM per device.

```python
import jax
import jax.numpy as jnp
from jax import lax

FEATURE_DEPTH = 256
CZ = 128
FACTOR_WIDTH = 32
H = 8
HEAD_SIZE = 32
RES_DEV = 32
ALIGNED_TOTAL = 256
CHAIN_LENGTH = 512


def draw_aligned_member_valid(key, part):
    key = jax.random.fold_in(key, 17)
    levels = jax.random.randint(key, (ALIGNED_TOTAL,), 0, 4)
    first = jnp.arange(ALIGNED_TOTAL) == 0
    return jnp.where(first | (levels > 0), 1, 0).astype(jnp.int32)


def draw_chain_position_valid(key, part):
    key = jax.random.fold_in(key, 29)
    levels = jax.random.randint(key, (CHAIN_LENGTH,), 0, 4)
    first = jnp.arange(CHAIN_LENGTH) == 0
    return jnp.where(first | (levels > 0), 1, 0).astype(jnp.int32)


def draw_horizontal_entry_matrices(key, part):
    key = jax.random.fold_in(key, 41)
    coefficient = jax.random.normal(jax.random.fold_in(key, 1), (FEATURE_DEPTH, 4 * FEATURE_DEPTH), jnp.float32) * FEATURE_DEPTH ** (-0.5)
    return jnp.clip(coefficient, -4.0, 4.0).astype(jnp.bfloat16)


def draw_vertical_entry_matrices(key, part):
    key = jax.random.fold_in(key, 53)
    coefficient = jax.random.normal(jax.random.fold_in(key, 1), (FEATURE_DEPTH, 4 * FEATURE_DEPTH), jnp.float32) * FEATURE_DEPTH ** (-0.5)
    return jnp.clip(coefficient, -4.0, 4.0).astype(jnp.bfloat16)


def shard_levels(key, shape, cuts, smallest, top_value):
    def one(axis_at, parts):
        draws = jax.random.uniform(jax.random.fold_in(jax.random.fold_in(key, 6), axis_at), (parts,), jnp.float32, smallest / len(cuts), top_value / len(cuts))
        return jnp.repeat(jnp.exp(draws), shape[axis_at] // parts).reshape((-1,) + (1,) * (len(shape) - axis_at - 1))

    level = one(*cuts[0])
    for cut in cuts[1:]:
        level = level * one(*cut)
    return level


def normal_values(rng, dims, width, reach, split=(), dtype=jnp.bfloat16):
    loudness = shard_levels(rng, dims, split, -0.22, 0.18) if split else 1.0
    entries = jax.random.normal(rng, dims, jnp.float32) * width * loudness
    return jnp.minimum(jnp.maximum(entries, -reach), reach).astype(dtype)


def setup_inputs(seed: int = 0) -> dict:
    key_list = jax.random.split(jax.random.key(seed), 13)
    return {
        "multiple_alignment_rep": normal_values(key_list[0], (ALIGNED_TOTAL, CHAIN_LENGTH, FEATURE_DEPTH), 1.0, 6.0, ((0, 8), (1, 16))),
        "pair_rep": normal_values(key_list[1], (CHAIN_LENGTH, CHAIN_LENGTH, CZ), 1.0, 6.0, ((0, 16),)),
        "aligned_member_valid": draw_aligned_member_valid(jax.random.fold_in(key_list[12], 71), 0),
        "chain_position_valid": draw_chain_position_valid(jax.random.fold_in(key_list[12], 71), 0),
        "horizontal_entry_matrices": draw_horizontal_entry_matrices(jax.random.fold_in(key_list[12], 71), 0),
        "horizontal_exit_matrix": normal_values(key_list[5], (FEATURE_DEPTH, FEATURE_DEPTH), FEATURE_DEPTH ** -0.5, 0.375),
        "bias_proj": normal_values(key_list[6], (CZ, H), CZ ** -0.5, 0.5),
        "vertical_entry_matrices": draw_vertical_entry_matrices(jax.random.fold_in(key_list[12], 71), 0),
        "vertical_exit_matrix": normal_values(key_list[8], (FEATURE_DEPTH, FEATURE_DEPTH), FEATURE_DEPTH ** -0.5, 0.375),
        "dyadic_projection_matrices": normal_values(key_list[9], (FEATURE_DEPTH, 2 * FACTOR_WIDTH), FEATURE_DEPTH ** -0.5, 0.375),
        "outer_out": normal_values(key_list[10], (FACTOR_WIDTH * FACTOR_WIDTH, CZ), (max(1, FACTOR_WIDTH * FACTOR_WIDTH * 4 // (3 * ALIGNED_TOTAL))) ** -0.5, 2.5),
        "pair_grad": normal_values(key_list[11], (CHAIN_LENGTH, CHAIN_LENGTH, CZ), 1.0, 6.0, ((0, 16),)),
    }


def standardize_features(values):
    values = values.astype(jnp.float32)
    center = values - lax.optimization_barrier(jnp.mean(values, -1, keepdims=True))
    spread = lax.optimization_barrier(jnp.mean(center * center, -1, keepdims=True))
    return center * lax.rsqrt(spread + 1e-05)

def standardize_reverse(values, upstream):
    values = values.astype(jnp.float32)
    center = values - lax.optimization_barrier(jnp.mean(values, -1, keepdims=True))
    inverse = lax.rsqrt(lax.optimization_barrier(jnp.mean(center * center, -1, keepdims=True)) + 1e-05)
    scaled = center * inverse
    return inverse * (upstream - lax.optimization_barrier(jnp.mean(upstream, -1, keepdims=True)) - scaled * lax.optimization_barrier(jnp.mean(upstream * scaled, -1, keepdims=True)))

def reduced_accuracy(values):
    return lax.optimization_barrier(values.astype(jnp.bfloat16)).astype(jnp.float32)

def project(portion, coefficient):
    return reduced_accuracy(jnp.einsum('mkz,zc->mkc', reduced_accuracy(standardize_features(portion)), coefficient.astype(jnp.float32)))

def split_heads(values):
    return values.reshape(values.shape[:-1] + (H, values.shape[-1] // H))

def attend(scores, value_heads, value_form, order_axes, gate_rows, portion, out_weight):
    peak = lax.optimization_barrier(jnp.max(scores, -1))
    weights = jnp.exp(scores - peak[..., None])
    total = lax.optimization_barrier(jnp.sum(weights, -1))
    summed = jnp.einsum(value_form, reduced_accuracy(weights), value_heads)
    output = summed / jnp.transpose(total, order_axes)[..., None]
    output = output.reshape(output.shape[:-2] + (-1,))
    gated = reduced_accuracy(jax.nn.sigmoid(gate_rows) * output)
    update = jnp.einsum('mkz,zc->mkc', gated, out_weight.astype(jnp.float32))
    return (portion.astype(jnp.float32) + update).astype(jnp.bfloat16)

def reference(multiple_alignment_rep, pair_rep, aligned_member_valid, chain_position_valid, horizontal_entry_matrices, horizontal_exit_matrix, bias_proj, vertical_entry_matrices, vertical_exit_matrix, dyadic_projection_matrices, outer_out, pair_grad):
    breadth = FEATURE_DEPTH
    scale = HEAD_SIZE ** (-0.5)
    bias = reduced_accuracy(jnp.einsum('ijz,zh->hij', reduced_accuracy(standardize_features(pair_rep)), bias_proj.astype(jnp.float32)))

    def horizontal_portion(portion):
        mixed = project(portion, horizontal_entry_matrices)
        query_heads = split_heads(mixed[..., :breadth])
        key_heads = split_heads(mixed[..., breadth:2 * breadth])
        value_heads = split_heads(mixed[..., 2 * breadth:3 * breadth])
        scores = jnp.einsum('bihd,bjhd->bhij', query_heads, key_heads) * scale + bias[None]
        scores = jnp.where(chain_position_valid[None, None, None, :] > 0, scores, -1000000000.0)
        return attend(scores, value_heads, 'bhij,bjhd->bihd', (0, 2, 1), mixed[..., 3 * breadth:], portion, horizontal_exit_matrix)
    alignment_horizontal_done = lax.map(horizontal_portion, multiple_alignment_rep.reshape(ALIGNED_TOTAL // 8, 8, CHAIN_LENGTH, FEATURE_DEPTH)).reshape(ALIGNED_TOTAL, CHAIN_LENGTH, FEATURE_DEPTH)

    def vertical_patch(portion):
        mixed = project(portion, vertical_entry_matrices)
        query_heads = split_heads(mixed[..., :breadth])
        key_heads = split_heads(mixed[..., breadth:2 * breadth])
        value_heads = split_heads(mixed[..., 2 * breadth:3 * breadth])
        scores = jnp.einsum('sihd,tihd->ihst', query_heads, key_heads) * scale
        scores = jnp.where(aligned_member_valid[None, None, None, :] > 0, scores, -1000000000.0)
        return attend(scores, value_heads, 'ihst,tihd->sihd', (2, 0, 1), mixed[..., 3 * breadth:], portion, vertical_exit_matrix)
    heaped_portions = jnp.moveaxis(alignment_horizontal_done.reshape(ALIGNED_TOTAL, CHAIN_LENGTH // 8, 8, FEATURE_DEPTH), 1, 0)
    alignment_refreshed = jnp.moveaxis(lax.map(vertical_patch, heaped_portions), 0, 1).reshape(ALIGNED_TOTAL, CHAIN_LENGTH, FEATURE_DEPTH)
    member_validity_scale = (aligned_member_valid[:, None] * chain_position_valid[None, :]).astype(jnp.float32)
    dyadic_operands = reduced_accuracy(jnp.einsum('mkz,zc->mkc', reduced_accuracy(standardize_features(alignment_refreshed)), dyadic_projection_matrices.astype(jnp.float32)) * member_validity_scale[..., None])
    factor_a = dyadic_operands[..., :FACTOR_WIDTH]
    factor_b = dyadic_operands[..., FACTOR_WIDTH:]
    count = jnp.sum(aligned_member_valid).astype(jnp.float32)
    cube = outer_out.astype(jnp.float32).reshape(FACTOR_WIDTH, FACTOR_WIDTH, CZ)
    left_blocks = jnp.moveaxis(factor_a.reshape(ALIGNED_TOTAL, CHAIN_LENGTH // RES_DEV, RES_DEV, FACTOR_WIDTH), 1, 0)

    def pair_block(left_part):
        mixed = reduced_accuracy(jnp.einsum('sic,cdz->sidz', left_part, cube))
        return (jnp.einsum('sidz,sjd->ijz', mixed, factor_b) / count).astype(jnp.bfloat16)
    couple_delta = lax.map(pair_block, left_blocks).reshape(CHAIN_LENGTH, CHAIN_LENGTH, CZ)
    grad_blocks = pair_grad.reshape(CHAIN_LENGTH // RES_DEV, RES_DEV, CHAIN_LENGTH, CZ)

    def grad_step(accum, pieces):
        grad_part, left_part = pieces
        spread = reduced_accuracy(jnp.einsum('ijz,fz->ijf', grad_part.astype(jnp.float32), outer_out.astype(jnp.float32)) / count)
        spread = spread.reshape(RES_DEV, CHAIN_LENGTH, FACTOR_WIDTH, FACTOR_WIDTH)
        grad_left = jnp.einsum('ijcd,sjd->sic', spread, factor_b)
        return (accum + jnp.einsum('ijcd,sic->sjd', spread, left_part), grad_left)
    grad_b, grad_lefts = lax.scan(grad_step, jnp.zeros((ALIGNED_TOTAL, CHAIN_LENGTH, FACTOR_WIDTH), jnp.float32), (grad_blocks, left_blocks))
    grad_a = jnp.moveaxis(grad_lefts, 0, 1).reshape(ALIGNED_TOTAL, CHAIN_LENGTH, FACTOR_WIDTH)
    grad_factors = reduced_accuracy(jnp.concatenate([grad_a, grad_b], -1) * member_validity_scale[..., None])
    standardized_cotangent = jnp.einsum('sif,cf->sic', grad_factors, dyadic_projection_matrices.astype(jnp.float32))
    refreshed_alignment_cotangent = standardize_reverse(alignment_refreshed, standardized_cotangent).astype(jnp.bfloat16)
    return (alignment_refreshed, couple_delta, refreshed_alignment_cotangent)
```

```python
import jax
import jax.numpy as jnp
from jax import lax
from jax.experimental import pallas as pl
from jax.experimental.pallas import tpu as pltpu
from jax.sharding import PartitionSpec as P

FACTOR_WIDTH = 32
H = 8
HEAD_SIZE = 32
LOG2E = 1.4426950408889634
MASKED = -1000000000.0 * LOG2E
BF16 = jnp.bfloat16
F32 = jnp.float32
NT = (((1,), (1,)), ((), ()))

VMEM = pl.BlockSpec(memory_space=pltpu.VMEM)
SMEM = pl.BlockSpec(memory_space=pltpu.SMEM)
ROOM = pltpu.CompilerParams(vmem_limit_bytes=56 * 1024 * 1024)


def nn(left, right):
    return jnp.dot(left, right, preferred_element_type=F32)


def nt(left, right):
    return lax.dot_general(left, right, NT, preferred_element_type=F32)


def standardize(values):
    center = values - jnp.mean(values, -1, keepdims=True)
    spread = jnp.mean(center * center, -1, keepdims=True)
    return center * lax.rsqrt(spread + 1e-05)


def put(ref, rows, values):
    for half in range(2):
        ref[half, rows, :] = values[:, 128 * half : 128 * half + 128]


def take(ref, rows):
    return jnp.concatenate([ref[0, rows, :], ref[1, rows, :]], 1)


def bias_kernel(pair_ref, proj_ref, valid_ref, out_ref):
    rows = pair_ref.shape[0]
    ones = jnp.full((128, 128), 1.0 / 128, BF16)
    live = valid_ref[...] > 0
    pieces = []
    for at in range(rows):
        lines = pair_ref[at]
        center = lines.astype(F32) - nn(lines, ones)
        spread = nn((center * center).astype(BF16), ones)
        normed = (center * lax.rsqrt(spread + 1e-05)).astype(BF16)
        bias = nt(proj_ref[...], normed) * LOG2E
        pieces.append(jnp.where(live, bias, MASKED))
    out_ref[...] = jnp.concatenate(pieces, 0).astype(BF16)


def pair_bias(pair, proj, valid):
    rows, residues, depth = pair.shape
    step = 4
    return pl.pallas_call(
        bias_kernel,
        grid=(rows // step,),
        in_specs=[
            pl.BlockSpec((step, residues, depth), lambda g: (g, 0, 0)),
            pl.BlockSpec((H, depth), lambda g: (0, 0)),
            pl.BlockSpec((1, residues), lambda g: (0, 0)),
        ],
        out_specs=pl.BlockSpec((step * H, residues), lambda g: (g, 0)),
        out_shape=jax.ShapeDtypeStruct((rows * H, residues), BF16),
        compiler_params=ROOM,
        name="pair_bias",
    )(pair, proj, valid)


def head_mask():
    lane = lax.broadcasted_iota(jnp.int32, (H, H * HEAD_SIZE), 1)
    row = lax.broadcasted_iota(jnp.int32, (H, H * HEAD_SIZE), 0)
    return jnp.where(lane // HEAD_SIZE == row, 1.0, 0.0).astype(F32)


def spread_heads(query, mask):
    rows, depth = query.shape
    return (query[:, None, :] * mask[None]).reshape(rows * H, depth).astype(BF16)


def attend(query, keys, values, offset, mask):
    rows, depth = query.shape
    scores = nt(spread_heads(query, mask), keys) + offset
    weights = jnp.exp2(scores - jnp.max(scores, -1, keepdims=True))
    total = jnp.sum(weights, -1, keepdims=True)
    summed = nn(weights.astype(BF16), values) * (1.0 / total)
    return jnp.sum(summed.reshape(rows, H, depth) * mask[None], 1)


def row_kernel(x_ref, bias_ref, valid_ref, w_ref, wo_ref, out_ref, q_s, k_s, v_s, g_s):
    blocks, seqs, rows, depth = x_ref.shape
    residues = blocks * rows
    mask = head_mask()
    live = valid_ref[...]
    for s in range(seqs):
        x = x_ref[:, s].reshape(residues, depth)
        mixed = nn(standardize(x.astype(F32)).astype(BF16), w_ref[...])
        q_s[s] = mixed[:, :depth] * (HEAD_SIZE**-0.5 * LOG2E)
        k_s[s] = (mixed[:, depth : 2 * depth] * live).astype(BF16)
        v_s[s] = mixed[:, 2 * depth : 3 * depth].astype(BF16)
        g_s[s] = jax.nn.sigmoid(mixed[:, 3 * depth :])

    upper = lax.broadcasted_iota(jnp.int32, (rows // 8, 8, depth), 1) < 4

    def block(at, carry):
        here = pl.ds(pl.multiple_of(at * rows, rows), rows)
        offset = bias_ref[at].astype(F32)
        done = []
        for s in range(seqs):
            output = attend(q_s[s, here, :], k_s[s], v_s[s], offset, mask)
            gated = (g_s[s, here, :] * output).astype(BF16)
            after = x_ref[at, s].astype(F32) + nn(gated, wo_ref[...])
            done.append(after.reshape(rows // 8, 8, depth))
        first, second = done
        even = jnp.where(upper, first, pltpu.roll(second, 4, 1)).astype(BF16)
        odd = jnp.where(upper, pltpu.roll(first, 4, 1), second).astype(BF16)
        for pair in range(rows // 8):
            out_ref[2 * pair, at] = even[pair]
            out_ref[2 * pair + 1, at] = odd[pair]
        return carry

    lax.fori_loop(0, blocks, block, 0)


def row_attention(x, bias, valid, w, wo):
    blocks, seqs, rows, depth = x.shape
    residues = blocks * rows
    return pl.pallas_call(
        row_kernel,
        in_specs=[VMEM] * 5,
        out_specs=VMEM,
        out_shape=jax.ShapeDtypeStruct((rows // 4, blocks, 4 * seqs, depth), BF16),
        scratch_shapes=[
            pltpu.VMEM((seqs, residues, depth), F32),
            pltpu.VMEM((seqs, residues, depth), BF16),
            pltpu.VMEM((seqs, residues, depth), BF16),
            pltpu.VMEM((seqs, residues, depth), F32),
        ],
        compiler_params=ROOM,
        name="row_attention",
    )(x, bias, valid, w, wo)


def col_kernel(
    y_ref, valid_col_ref, valid_row_ref, chain_ref, w_ref, wo_ref, dyadic_ref,
    out_ref, a_ref, b_ref, y_s, q_s, k_s, v_s, g_s, o_s,
):
    tokens, depth = y_s.shape[1], 2 * y_s.shape[2]
    seqs = tokens // 4
    mask = head_mask()
    live = valid_row_ref[...]
    offset = jnp.where(live > 0, 0.0, MASKED)
    put(y_s, slice(None), y_ref[...].reshape(tokens, depth).astype(F32))
    step = 32
    for at in range(4):
        y = take(y_s, pl.ds(at, seqs, stride=4))
        mixed = nn(standardize(y).astype(BF16), w_ref[...])
        q_s[...] = mixed[:, :depth] * (HEAD_SIZE**-0.5 * LOG2E)
        k_s[...] = (mixed[:, depth : 2 * depth] * valid_col_ref[...]).astype(BF16)
        v_s[...] = mixed[:, 2 * depth : 3 * depth].astype(BF16)
        g_s[...] = jax.nn.sigmoid(mixed[:, 3 * depth :])

        def block(part, carry):
            here = pl.ds(pl.multiple_of(part * step, step), step)
            output = attend(q_s[here, :], k_s[...], v_s[...], offset, mask)
            o_s[here, :] = (g_s[here, :] * output).astype(BF16)
            return carry

        lax.fori_loop(0, seqs // step, block, 0)
        done = (y + nn(o_s[...], wo_ref[...])).astype(BF16)
        out_ref[:, at] = done.reshape(out_ref.shape[0], out_ref.shape[2], depth)
        normed = standardize(done.astype(F32)).astype(BF16)
        factors = nt(dyadic_ref[...], normed) * (live * chain_ref[at])
        a_ref[pl.ds(32 * at, 32), :] = factors[:32].astype(BF16)
        b_ref[pl.ds(32 * at, 32), :] = factors[32:].astype(BF16)


def col_attention(y, valid_col, valid_row, chain, w, wo, dyadic_t, groups):
    sources, eight, depth = y.shape
    tokens = sources * eight
    seqs = tokens // 4
    return pl.pallas_call(
        col_kernel,
        in_specs=[VMEM] * 3 + [SMEM] + [VMEM] * 3,
        out_specs=[VMEM] * 3,
        out_shape=[
            jax.ShapeDtypeStruct((groups, 4, seqs // groups, depth), BF16),
            jax.ShapeDtypeStruct((4 * FACTOR_WIDTH, seqs), BF16),
            jax.ShapeDtypeStruct((4 * FACTOR_WIDTH, seqs), BF16),
        ],
        scratch_shapes=[
            pltpu.VMEM((2, tokens, depth // 2), F32),
            pltpu.VMEM((seqs, depth), F32),
            pltpu.VMEM((seqs, depth), BF16),
            pltpu.VMEM((seqs, depth), BF16),
            pltpu.VMEM((seqs, depth), F32),
            pltpu.VMEM((seqs, depth), BF16),
        ],
        compiler_params=ROOM,
        name="col_attention",
    )(y, valid_col, valid_row, chain, w, wo, dyadic_t)


def couple_kernel(a_ref, b_ref, w_ref, count_ref, out_ref, bd_ref, b_s):
    width = FACTOR_WIDTH
    columns = b_s.shape[1] // width
    put(b_s, slice(None), b_ref[...].astype(F32))

    def turn(at, carry):
        here = pl.ds(pl.multiple_of(at * columns, columns), columns)
        bd_ref[here, :] = take(b_s, pl.ds(at, columns, stride=width)).astype(BF16)
        return carry

    lax.fori_loop(0, width, turn, 0)
    scale = 1.0 / count_ref[0]
    low = lax.broadcasted_iota(jnp.int32, (128, 128), 1) < 64

    def group(at, carry):
        left = a_ref[pl.ds(pl.multiple_of(at * 256, 256), 256), :]
        outer = nt(left, bd_ref[...]).astype(BF16)
        for pair in range(4):
            stacks = []
            for one in (2 * pair, 2 * pair + 1):
                part = outer[width * one : width * one + width]
                stacks.append(
                    jnp.concatenate([part[:, 128 * e : 128 * e + 128] for e in range(16)], 0)
                )
            both = nn(w_ref[...], jnp.concatenate(stacks, 1))
            top = jnp.where(low, both[:128, :128], pltpu.roll(both[:128, 128:], 64, 1))
            bottom = jnp.where(low, pltpu.roll(both[128:, :128], 64, 1), both[128:, 128:])
            delta = ((top + bottom) * scale).T
            out_ref[pl.ds(at * 8 + 2 * pair, 2)] = delta.reshape(2, 64, 128).astype(BF16)
        return carry

    lax.fori_loop(0, 4, group, 0)


def couple(a_all, b_all, w, count):
    rows, seqs = a_all.shape
    columns = b_all.shape[0]
    return pl.pallas_call(
        couple_kernel,
        in_specs=[VMEM] * 3 + [SMEM],
        out_specs=[VMEM] * 2,
        out_shape=[
            jax.ShapeDtypeStruct((rows // FACTOR_WIDTH, columns // FACTOR_WIDTH, 128), BF16),
            jax.ShapeDtypeStruct((columns, seqs), BF16),
        ],
        scratch_shapes=[pltpu.VMEM((2, columns, seqs // 2), F32)],
        compiler_params=ROOM,
        name="couple",
    )(a_all, b_all, w, count)


def grad_kernel(a_ref, bd_ref, g_ref, w_ref, count_ref, ga_ref, gb_ref, s_s, gb_s, turned_s):
    width = FACTOR_WIDTH
    columns = bd_ref.shape[0] // width
    scale = 1.0 / count_ref[0]
    gb_s[...] = jnp.zeros_like(gb_s)
    blank = jnp.zeros((64, 128), BF16)

    def group(at, carry):
        here = pl.ds(pl.multiple_of(at * 256, 256), 256)
        for pair in range(4):
            parts = []
            for one in (2 * pair, 2 * pair + 1):
                given = g_ref[at * 8 + one]
                parts.append(jnp.concatenate([given, blank], 1))
                parts.append(jnp.concatenate([blank, given], 1))
            both = (nt(w_ref[...], jnp.concatenate(parts, 0)) * scale).astype(BF16)
            for half, one in enumerate((2 * pair, 2 * pair + 1)):
                s_s[width * one : width * one + width, :] = jnp.concatenate(
                    [
                        both[width * e : width * e + width, 128 * half : 128 * half + 128]
                        for e in range(16)
                    ],
                    1,
                )
        spread = s_s[...]
        ga_ref[here, :] = nn(spread, bd_ref[...]).astype(BF16)
        left = a_ref[here, :].astype(F32).T.astype(BF16)
        gb_s[...] += nn(left, spread)
        return carry

    lax.fori_loop(0, 4, group, 0)
    put(turned_s, slice(None), gb_s[...].T)

    def turn(at, carry):
        to = pl.ds(pl.multiple_of(at * width, width), width)
        gb_ref[to, :] = take(turned_s, pl.ds(at, width, stride=columns)).astype(BF16)
        return carry

    lax.fori_loop(0, columns, turn, 0)


def factor_grads(a_all, bd, given, w, count):
    rows, seqs = a_all.shape
    columns = bd.shape[0]
    return pl.pallas_call(
        grad_kernel,
        in_specs=[VMEM] * 4 + [SMEM],
        out_specs=[VMEM] * 2,
        out_shape=[
            jax.ShapeDtypeStruct((rows, seqs), BF16),
            jax.ShapeDtypeStruct((columns, seqs), BF16),
        ],
        scratch_shapes=[
            pltpu.VMEM((256, columns), BF16),
            pltpu.VMEM((seqs, columns), F32),
            pltpu.VMEM((2, columns, seqs // 2), F32),
        ],
        compiler_params=ROOM,
        name="factor_grads",
    )(a_all, bd, given, w, count)


def total_kernel(ga_ref, gb_ref, valid_ref, chain_ref, out_ref):
    sums = []
    for part in (ga_ref, gb_ref):
        total = part[0].astype(F32)
        for at in range(1, part.shape[0]):
            total = total + part[at].astype(F32)
        sums.append(total)
    both = jnp.concatenate(sums, 0) * valid_ref[...] * chain_ref[...]
    out_ref[...] = both.T.astype(BF16)


def total_grads(ga, gb, valid_row, chain_col):
    return pl.pallas_call(
        total_kernel,
        in_specs=[VMEM] * 4,
        out_specs=VMEM,
        out_shape=jax.ShapeDtypeStruct((ga.shape[2], 2 * ga.shape[1]), BF16),
        compiler_params=ROOM,
        name="total_grads",
    )(ga, gb, valid_row, chain_col)


def home_kernel(gf_ref, w_ref, x_ref, x_out_ref, ct_ref, x_s, ct_s):
    groups, parts, seqs, depth = x_ref.shape
    residues = groups * parts
    given = gf_ref[...].reshape(groups * seqs, depth)
    for at in range(parts):
        upstream = nn(given, w_ref[at])
        x = x_ref[:, at].reshape(groups * seqs, depth).astype(F32)
        center = x - jnp.mean(x, -1, keepdims=True)
        inverse = lax.rsqrt(jnp.mean(center * center, -1, keepdims=True) + 1e-05)
        scaled = center * inverse
        cotangent = inverse * (
            upstream
            - jnp.mean(upstream, -1, keepdims=True)
            - scaled * jnp.mean(upstream * scaled, -1, keepdims=True)
        )
        for group in range(groups):
            here = pl.ds(group * parts + at, seqs, stride=residues)
            put(x_s, here, x[group * seqs : group * seqs + seqs])
            put(ct_s, here, cotangent[group * seqs : group * seqs + seqs])
    x_out_ref[...] = take(x_s, slice(None)).reshape(seqs, residues, depth).astype(BF16)
    ct_ref[...] = take(ct_s, slice(None)).reshape(seqs, residues, depth).astype(BF16)


def finish_home(gf, w, x):
    groups, parts, seqs, depth = x.shape
    shape = (seqs, groups * parts, depth)
    return pl.pallas_call(
        home_kernel,
        in_specs=[VMEM] * 3,
        out_specs=[VMEM] * 2,
        out_shape=[jax.ShapeDtypeStruct(shape, BF16)] * 2,
        scratch_shapes=[pltpu.VMEM((2, seqs * groups * parts, depth // 2), F32)] * 2,
        compiler_params=ROOM,
        name="finish_home",
    )(gf, w, x)


def ring(x, axis, along, across):
    half = x.shape[0] // 2

    def move(values, pairs):
        return lax.ppermute(values, axis, pairs)

    partner = move(x, across)
    below = move(x, along(1))
    above = move(x, along(3))
    far_low = move(below[:half], along(1))
    far_high = move(above[half:], along(3))
    partner_below = move(partner, along(1))
    partner_above = move(partner, along(3))
    partner_far_low = move(far_low, across)
    partner_far_high = move(far_high, across)
    far = jnp.concatenate([far_low, far_high], 0)
    partner_far = jnp.concatenate([partner_far_low, partner_far_high], 0)
    return [x, above, far, below, partner, partner_above, partner_far, partner_below]


def seq_along(k):
    return [(x * 4 + z, x * 4 + (z + k) % 4) for x in range(2) for z in range(4)]


SEQ_ACROSS = [(x * 4 + z, (1 - x) * 4 + z) for x in range(2) for z in range(4)]


def res_at(y, x, core):
    return (y * 2 + x) * 2 + core


RES = [(y, x, core) for y in range(4) for x in range(2) for core in range(2)]
RES_ACROSS = [(res_at(y, x, c), res_at(y, 1 - x, c)) for y, x, c in RES]
RES_CORE = [(res_at(y, x, c), res_at(y, x, 1 - c)) for y, x, c in RES]


def res_along(k):
    return [(res_at(y, x, c), res_at((y + k) % 4, x, c)) for y, x, c in RES]


def gather_seq(x):
    q = lax.axis_index("seq")
    z, cross = q % 4, q // 4
    blocks = ring(x, "seq", seq_along, SEQ_ACROSS)
    stacked = jnp.stack(blocks).reshape((2, 4) + x.shape)
    stacked = jnp.roll(jnp.roll(stacked, z, 1), cross, 0)
    return stacked.reshape((8,) + x.shape)


def gather_res(x):
    return lax.all_gather(x, "res", axis=0)


def per_device(
    multiple_alignment_rep,
    pair_rep,
    aligned_member_valid,
    chain_position_valid,
    horizontal_entry_matrices,
    horizontal_exit_matrix,
    bias_proj,
    vertical_entry_matrices,
    vertical_exit_matrix,
    dyadic_projection_matrices,
    outer_out,
    pair_grad,
):
    seqs_here, res_here, depth = multiple_alignment_rep.shape
    residues = pair_rep.shape[1]
    pair_width = outer_out.shape[1]
    q_at, r_at = lax.axis_index("seq"), lax.axis_index("res")
    q_size, r_size = lax.axis_size("seq"), lax.axis_size("res")
    width = FACTOR_WIDTH
    member = aligned_member_valid.astype(F32)
    chain = chain_position_valid.astype(F32)
    count = jnp.sum(member).reshape(1)
    chain_here = lax.dynamic_slice_in_dim(chain, r_at * res_here + 4 * q_at, 4)

    dyadic_t = dyadic_projection_matrices.T
    cube = outer_out.reshape(width, width // 2, 2, pair_width)
    w_out = cube.transpose(2, 3, 1, 0).reshape(2 * pair_width, 16 * width)
    w_spread = cube.transpose(1, 0, 2, 3).reshape(16 * width, 2 * pair_width)
    halves = dyadic_t.reshape(2, 1, width, depth)
    place = jnp.eye(4, dtype=BF16).reshape(4, 1, 4, 1, 1)
    w_back = (place * halves[None]).reshape(4, 8 * width, depth)
    grad_here = lax.dynamic_index_in_dim(
        pair_grad.reshape(res_here, r_size, q_size, 4, pair_width), q_at, 2, keepdims=False
    ).reshape(res_here, r_size * 4, pair_width)

    x_rows = lax.all_to_all(
        multiple_alignment_rep.reshape(r_size, seqs_here // r_size, res_here, depth),
        "res", 0, 0, tiled=True,
    )
    bias = pair_bias(pair_rep, bias_proj.T, chain_position_valid.reshape(1, residues))
    bias_all = gather_res(bias)
    after_row = row_attention(
        x_rows, bias_all, chain.reshape(residues, 1),
        horizontal_entry_matrices, horizontal_exit_matrix,
    )

    columns = lax.all_to_all(
        after_row.reshape(q_size * r_size, 8, depth), ("seq", "res"), 0, 0, tiled=True
    )
    refreshed, factor_a, factor_b = col_attention(
        columns, member.reshape(-1, 1), member.reshape(1, -1), chain_here,
        vertical_entry_matrices, vertical_exit_matrix, dyadic_t, q_size,
    )
    a_all = gather_seq(factor_a).reshape(res_here * width, -1)
    b_all = gather_res(factor_b).reshape(r_size * 4 * width, -1)
    refreshed = lax.all_to_all(refreshed, "seq", 0, 0, tiled=True)

    delta, bd = couple(a_all, b_all, w_out, count)
    deltas = gather_seq(delta)
    couple_delta = (
        deltas.reshape(q_size, res_here, r_size, 4, pair_width)
        .transpose(1, 2, 0, 3, 4)
        .reshape(res_here, residues, pair_width)
    )

    ga, gb = factor_grads(a_all, bd, grad_here, w_spread, count)
    ga = lax.all_to_all(ga.reshape(q_size, 4 * width, -1), "seq", 0, 0, tiled=True)
    gb = lax.all_to_all(gb.reshape(r_size, 4 * width, -1), "res", 0, 0, tiled=True)
    chain_col = jnp.tile(jnp.repeat(chain_here, width), 2).reshape(-1, 1)
    factors = total_grads(ga, gb, member.reshape(1, -1), chain_col)
    factors = lax.all_to_all(
        factors.reshape(q_size, seqs_here, 8 * width), "seq", 0, 0, tiled=True
    )
    alignment_refreshed, cotangent = finish_home(factors, w_back, refreshed)
    return (alignment_refreshed, couple_delta, cotangent)


def solution(mesh):
    placed = (
        P("seq", "res", None),
        P("res", None, None),
        P(),
        P(),
        P(),
        P(),
        P(),
        P(),
        P(),
        P(),
        P(),
        P("res", None, None),
    )
    return jax.shard_map(
        per_device,
        mesh=mesh,
        in_specs=placed,
        out_specs=(P("seq", "res", None), P("res", None, None), P("seq", "res", None)),
        check_vma=False,
    )
```

```python
import jax
import jax.numpy as jnp
from jax import lax
from jax.experimental import pallas as pl
from jax.experimental.pallas import tpu as pltpu
from jax.sharding import PartitionSpec as P

FACTOR_WIDTH = 32
H = 8
HEAD_SIZE = 32
LOG2E = 1.4426950408889634
MASKED = -1000000000.0 * LOG2E
BF16 = jnp.bfloat16
F32 = jnp.float32
NT = (((1,), (1,)), ((), ()))
ROW_UNROLL = 1
COL_STEP = 64
PAIR_UNROLL = 2

VMEM = pl.BlockSpec(memory_space=pltpu.VMEM)
SMEM = pl.BlockSpec(memory_space=pltpu.SMEM)
ORDER = pl.BlockSpec(memory_space=pl.ANY)
ROOM = pltpu.CompilerParams(vmem_limit_bytes=56 * 1024 * 1024)


def lasting(microseconds):
    return pl.CostEstimate(
        flops=0, bytes_accessed=int(microseconds * 3.69e6), transcendentals=0
    )


def nn(left, right):
    return jnp.dot(left, right, preferred_element_type=F32)


def nt(left, right):
    return lax.dot_general(left, right, NT, preferred_element_type=F32)


def standardize(values):
    center = values - jnp.mean(values, -1, keepdims=True)
    spread = jnp.mean(center * center, -1, keepdims=True)
    return center * lax.rsqrt(spread + 1e-05)


def put(ref, rows, values):
    for half in range(2):
        ref[half, rows, :] = values[:, 128 * half : 128 * half + 128]


def take(ref, rows):
    return jnp.concatenate([ref[0, rows, :], ref[1, rows, :]], 1)


def column_of(row):
    return jnp.broadcast_to(row.astype(F32), (8, row.shape[1])).T[:, :1]


def seq_index():
    return lax.axis_index("x_hi"), lax.axis_index("z")


def res_index():
    return lax.axis_index("x_lo"), lax.axis_index("y")


def scale_of(member):
    return 1.0 / jnp.sum(member.astype(F32), keepdims=True)


def bias_kernel(pair_ref, proj_ref, valid_ref, out_ref, turn_s):
    at = pl.program_id(0)
    rows, residues, depth = pair_ref.shape
    line = lax.broadcasted_iota(jnp.int32, (depth, depth), 0)
    lane = lax.broadcasted_iota(jnp.int32, (depth, depth), 1)
    centering = (jnp.where(line == lane, 1.0, 0.0) - 1.0 / depth).astype(BF16)
    live = valid_ref[...] > 0
    proj = proj_ref[...]
    blank = jnp.zeros_like(proj)
    mean = jnp.full_like(proj, 1.0 / depth)
    sides = jnp.concatenate(
        [jnp.concatenate([proj, blank], 1), jnp.concatenate([blank, mean], 1)], 0
    ).astype(BF16)
    center = nn(pair_ref[...].reshape(rows * residues, depth), centering)
    both = jnp.concatenate([center.astype(BF16), (center * center).astype(BF16)], 1)
    for one in range(rows):
        sums = nt(sides, both[one * residues : one * residues + residues])
        bias = sums[:H] * lax.rsqrt(sums[H:] + 1e-05) * LOG2E
        bias = jnp.where(live, bias, MASKED)
        here = pl.ds(pl.multiple_of((at * rows + one) * H, H), H)
        for part in range(residues // 128):
            turn_s[part, here, :] = bias[:, 128 * part : 128 * part + 128]

    @pl.when(at == pl.num_programs(0) - 1)
    def _():
        total = out_ref.shape[0] // H
        for head in range(H):
            for part in range(residues // 128):
                out_ref[total * head : total * head + total, 128 * part : 128 * part + 128] = (
                    turn_s[part, pl.ds(head, total, stride=H), :].astype(BF16)
                )


def pair_bias(pair, proj, valid):
    rows, residues, depth = pair.shape
    step = 4
    return pl.pallas_call(
        bias_kernel,
        grid=(rows // step,),
        in_specs=[
            pl.BlockSpec((step, residues, depth), lambda g: (g, 0, 0)),
            pl.BlockSpec((H, depth), lambda g: (0, 0)),
            pl.BlockSpec((1, residues), lambda g: (0, 0)),
        ],
        out_specs=pl.BlockSpec((rows * H, residues), lambda g: (0, 0)),
        out_shape=jax.ShapeDtypeStruct((rows * H, residues), BF16),
        scratch_shapes=[pltpu.VMEM((residues // 128, rows * H, 128), F32)],
        compiler_params=ROOM,
        cost_estimate=lasting(9),
        name="pair_bias",
    )(pair, proj, valid)


def scores_of(query, keys, side):
    lanes = slice(128 * side, 128 * side + 128)
    lane = lax.broadcasted_iota(jnp.int32, (1, 128), 1) // HEAD_SIZE
    part = query[:, lanes]
    spread = [jnp.where(lane == head, part, 0.0).astype(BF16) for head in range(4)]
    return nt(jnp.concatenate(spread, 0), keys[:, lanes])


def weigh(scores, values, side):
    rows = scores.shape[0] // 4
    lane = lax.broadcasted_iota(jnp.int32, (1, 128), 1) // HEAD_SIZE
    weights = jnp.exp2(scores - jnp.max(scores, -1, keepdims=True))
    scale = 1.0 / jnp.sum(weights, -1, keepdims=True)
    summed = nn(weights.astype(BF16), values[:, 128 * side : 128 * side + 128])
    output = summed[:rows] * scale[:rows]
    for head in range(1, 4):
        here = slice(rows * head, rows * head + rows)
        output = jnp.where(lane == head, summed[here] * scale[here], output)
    return output


def entry_kernel(x_ref, other_ref, valid_ref, w_ref, q_ref, k_ref, v_ref, g_ref, live_s):
    blocks, seqs, rows, depth = x_ref.shape
    core = lax.axis_index("core")
    live_s[...] = jnp.broadcast_to(column_of(valid_ref[...]), live_s.shape)
    for s in range(seqs):
        for other in range(2):
            source = other_ref if other else x_ref
            x = source[:, s].reshape(blocks * rows, depth)
            normed = standardize(x.astype(F32)).astype(BF16)
            pair = nn(normed, w_ref[:, depth : 3 * depth])
            side = 1 - core if other else core
            for at in range(blocks):
                here = slice(rows * at, rows * at + rows)
                to = pl.ds(pl.multiple_of((2 * at + side) * rows, rows), rows)
                k_ref[s, to, :] = (pair[here, :depth] * live_s[to, :1]).astype(BF16)
                v_ref[s, to, :] = pair[here, depth:].astype(BF16)
            if not other:
                query = nn(normed, w_ref[:, :depth]) * (HEAD_SIZE**-0.5 * LOG2E)
                q_ref[s] = query.astype(BF16)
                g_ref[s] = jax.nn.sigmoid(nn(normed, w_ref[:, 3 * depth :])).astype(BF16)


def row_entry(x, other, valid, w):
    blocks, seqs, rows, depth = x.shape
    here = jax.ShapeDtypeStruct((seqs, blocks * rows, depth), BF16)
    full = jax.ShapeDtypeStruct((seqs, 2 * blocks * rows, depth), BF16)
    return pl.pallas_call(
        entry_kernel,
        in_specs=[VMEM] * 4,
        out_specs=[VMEM] * 4,
        out_shape=[here, full, full, here],
        scratch_shapes=[pltpu.VMEM((2 * blocks * rows, 128), F32)],
        compiler_params=ROOM,
        cost_estimate=lasting(5),
        name="row_entry",
    )(x, other, valid, w)


def place(index, pieces, size, store):
    across, along = index
    pieces = list(pieces)
    for block in range(8):
        at = (across ^ (block // 4)) * 4 + ((along + block) & 3)
        parts = 2 if block % 4 == 2 else 1
        for part in range(parts):
            store(at, size // parts * part, size // parts, pieces.pop(0))


def place_pairs(index, pieces, size, store):
    across, along = index
    pieces = list(pieces)
    for ahead in range(4):
        for other in range(2):
            at = (across ^ other) * 4 + ((along + ahead) & 3)
            if ahead == 2:
                store(at, 0, size, pieces[2 + other], 0)
            else:
                store(at, 0, size, pieces[(0, 1, None, 4)[ahead]], size * other)


def row_kernel(q_ref, k_ref, v_ref, g_ref, x_ref, wo_ref, *refs):
    pieces, (out_ref, bias_s) = refs[:10], refs[10:]
    blocks, seqs, rows, depth = x_ref.shape

    def store(block, start, size, piece):
        bias_s[(block % 4) * 2 + block // 4, start : start + size, :] = piece[...]

    place(res_index(), pieces, bias_s.shape[1], store)
    upper = lax.broadcasted_iota(jnp.int32, (rows // 8, 8, depth), 1) < 4

    def block(at, carry):
        here = pl.ds(pl.multiple_of(at * rows, rows), rows)
        scores = {}
        for side in range(2):
            offset = bias_s[at, 4 * rows * side : 4 * rows * side + 4 * rows, :].astype(F32)
            for s in range(seqs):
                scores[s, side] = scores_of(q_ref[s, here, :], k_ref.at[s], side) + offset
        done = []
        for s in range(seqs):
            output = jnp.concatenate(
                [weigh(scores[s, side], v_ref.at[s], side) for side in range(2)], 1
            )
            gated = (g_ref[s, here, :].astype(F32) * output).astype(BF16)
            after = x_ref[at, s].astype(F32) + nn(gated, wo_ref[...])
            done.append(after.reshape(rows // 8, 8, depth))
        even, odd = [], []
        for first, second in zip(done[::2], done[1::2]):
            even.append(jnp.where(upper, first, pltpu.roll(second, 4, 1)))
            odd.append(jnp.where(upper, pltpu.roll(first, 4, 1), second))
        even = jnp.concatenate(even, 1).astype(BF16)
        odd = jnp.concatenate(odd, 1).astype(BF16)
        for pair in range(rows // 8):
            out_ref[2 * pair, at] = even[pair]
            out_ref[2 * pair + 1, at] = odd[pair]
        return carry

    lax.fori_loop(0, blocks, block, 0, unroll=ROW_UNROLL)


def row_attention(q, k, v, g, x, wo, bias):
    blocks, seqs, rows, depth = x.shape
    return pl.pallas_call(
        row_kernel,
        in_specs=[VMEM] * (6 + len(bias)),
        out_specs=VMEM,
        out_shape=jax.ShapeDtypeStruct((rows // 4, blocks, 4 * seqs, depth), BF16),
        scratch_shapes=[pltpu.VMEM((blocks,) + bias[0].shape, BF16)],
        compiler_params=ROOM,
        cost_estimate=lasting(14),
        name="row_attention",
    )(q, k, v, g, x, wo, *bias)


def col_kernel(
    y_ref, valid_ref, chain_ref, w_ref, wo_ref, dyadic_ref, _,
    out_ref, a_ref, b_ref, y_s, q_s, k_s, v_s, g_s, o_s,
):
    tokens, depth = y_s.shape[1], 2 * y_s.shape[2]
    parts = q_s.shape[0]
    seqs = tokens // parts
    live = valid_ref[...].astype(F32)
    live_column = column_of(live)
    offset = jnp.where(live > 0, 0.0, MASKED)
    x_hi, z = seq_index()
    x_lo, y_at = res_index()
    first = ((y_at * 2 + x_lo) * 2 + lax.axis_index("core")) * 32 + (x_hi * 4 + z) * parts
    put(y_s, slice(None), y_ref[...].reshape(tokens, depth).astype(F32))
    for at in range(parts):
        y = take(y_s, pl.ds(at, seqs, stride=parts))
        mixed = nn(standardize(y).astype(BF16), w_ref[...])
        q_s[at] = mixed[:, :depth] * (HEAD_SIZE**-0.5 * LOG2E)
        k_s[at] = (mixed[:, depth : 2 * depth] * live_column).astype(BF16)
        v_s[at] = mixed[:, 2 * depth : 3 * depth].astype(BF16)
        g_s[at] = jax.nn.sigmoid(mixed[:, 3 * depth :])
    step = COL_STEP

    def block(part, carry):
        here = pl.ds(pl.multiple_of(part * step, step), step)
        scores = [
            [scores_of(q_s[at, here, :], k_s[at], side) + offset for side in range(2)]
            for at in range(parts)
        ]
        for at in range(parts):
            output = jnp.concatenate(
                [weigh(scores[at][side], v_s[at], side) for side in range(2)], 1
            )
            o_s[at, here, :] = (g_s[at, here, :] * output).astype(BF16)
        return carry

    lax.fori_loop(0, seqs // step, block, 0)
    for at in range(parts):
        y = take(y_s, pl.ds(at, seqs, stride=parts))
        done = (y + nn(o_s[at], wo_ref[...])).astype(BF16)
        out_ref[:, at] = done.reshape(out_ref.shape[0], out_ref.shape[2], depth)
        normed = standardize(done.astype(F32)).astype(BF16)
        factors = nt(dyadic_ref[...], normed) * (live * chain_ref[first + at].astype(F32))
        a_ref[pl.ds(32 * at, 32), :] = factors[:32].astype(BF16)
        b_ref[pl.ds(32 * at, 32), :] = factors[32:].astype(BF16)


def col_attention(y, valid, chain, w, wo, dyadic_t, groups, after):
    sources, eight, depth = y.shape
    tokens = sources * eight
    seqs = tokens // 4
    return pl.pallas_call(
        col_kernel,
        in_specs=[VMEM] * 2 + [SMEM] + [VMEM] * 3 + [ORDER],
        out_specs=[VMEM] * 3,
        out_shape=[
            jax.ShapeDtypeStruct((groups, 4, seqs // groups, depth), BF16),
            jax.ShapeDtypeStruct((4 * FACTOR_WIDTH, seqs), BF16),
            jax.ShapeDtypeStruct((4 * FACTOR_WIDTH, seqs), BF16),
        ],
        scratch_shapes=[
            pltpu.VMEM((2, tokens, depth // 2), F32),
            pltpu.VMEM((4, seqs, depth), F32),
            pltpu.VMEM((4, seqs, depth), BF16),
            pltpu.VMEM((4, seqs, depth), BF16),
            pltpu.VMEM((4, seqs, depth), F32),
            pltpu.VMEM((4, seqs, depth), BF16),
        ],
        compiler_params=ROOM,
        cost_estimate=lasting(8),
        name="col_attention",
    )(y, valid, chain, w, wo, dyadic_t, after)


def couple_kernel(a_ref, bd_ref, w_ref, member_ref, _, out_ref, o_s):
    width = FACTOR_WIDTH
    rows, columns = o_s.shape
    for at in range(columns // 256):
        here = slice(256 * at, 256 * at + 256)
        o_s[:, here] = nt(a_ref[...], bd_ref[here, :]).astype(BF16)
    scale = scale_of(member_ref[...])
    w = w_ref[...].astype(F32).T.astype(BF16)
    low = lax.broadcasted_iota(jnp.int32, (128, 128), 1) < 64

    def pair(at, carry):
        outer = o_s[pl.ds(pl.multiple_of(at * 2 * width, 2 * width), 2 * width), :]
        stacks = []
        for one in range(2):
            part = outer[width * one : width * one + width]
            stacks.append(
                jnp.concatenate([part[:, 128 * e : 128 * e + 128] for e in range(16)], 0)
            )
        both = nn(w, jnp.concatenate(stacks, 1))
        top = jnp.where(low, both[:128, :128], pltpu.roll(both[:128, 128:], 64, 1))
        bottom = jnp.where(low, pltpu.roll(both[128:, :128], 64, 1), both[128:, 128:])
        delta = ((top + bottom) * scale).T
        out_ref[pl.ds(at * 2, 2)] = delta.reshape(2, 64, 128).astype(BF16)
        return carry

    lax.fori_loop(0, rows // (2 * width), pair, 0, unroll=PAIR_UNROLL)


def couple(a_all, bd, w, member, after):
    rows, columns = a_all.shape[0], bd.shape[0]
    return pl.pallas_call(
        couple_kernel,
        in_specs=[VMEM] * 4 + [ORDER],
        out_specs=VMEM,
        out_shape=jax.ShapeDtypeStruct(
            (rows // FACTOR_WIDTH, columns // FACTOR_WIDTH, 128), BF16
        ),
        scratch_shapes=[pltpu.VMEM((rows, columns), BF16)],
        compiler_params=ROOM,
        cost_estimate=lasting(8),
        name="couple",
    )(a_all, bd, w, member, after)


def assemble_kernel(*refs):
    pieces, (out_ref, d_s) = refs[:10], refs[10:]
    step = out_ref.shape[0]
    at = pl.program_id(0)

    def store(block, start, size, piece):
        d_s[block, start : start + size] = piece[...]

    @pl.when(at == 0)
    def _():
        place(seq_index(), pieces, d_s.shape[1], store)

    upper = lax.broadcasted_iota(jnp.int32, (8, 8, 128), 1) < 4

    def line(one, carry):
        even, odd = [], []
        for pair in range(4):
            first = d_s[2 * pair, at * step + one].astype(F32).reshape(8, 8, 128)
            second = d_s[2 * pair + 1, at * step + one].astype(F32).reshape(8, 8, 128)
            even.append(jnp.where(upper, first, pltpu.roll(second, 4, 1)))
            odd.append(jnp.where(upper, pltpu.roll(first, 4, 1), second))
        both = jnp.stack([jnp.stack(even, 1), jnp.stack(odd, 1)], 1)
        out_ref[one] = both.reshape(512, 128).astype(BF16)
        return carry

    lax.fori_loop(0, step, line, 0, unroll=2)


def assemble(pieces):
    rows, columns, depth = pieces[0].shape
    step = 8
    return pl.pallas_call(
        assemble_kernel,
        grid=(rows // step,),
        in_specs=[VMEM] * len(pieces),
        out_specs=pl.BlockSpec((step, 8 * columns, depth), lambda g: (g, 0, 0)),
        out_shape=jax.ShapeDtypeStruct((rows, 8 * columns, depth), BF16),
        scratch_shapes=[pltpu.VMEM((8, rows, columns, depth), BF16)],
        compiler_params=ROOM,
        cost_estimate=lasting(5),
        name="assemble",
    )(*pieces)


def spread_kernel(g_ref, w_ref, member_ref, _, out_ref):
    width = FACTOR_WIDTH
    scale = scale_of(member_ref[...])
    blank = jnp.zeros((64, 128), BF16)

    def pair(at, carry):
        parts = []
        for one in range(2):
            given = g_ref[2 * at + one]
            parts.append(jnp.concatenate([given, blank], 1))
            parts.append(jnp.concatenate([blank, given], 1))
        both = (nt(w_ref[...], jnp.concatenate(parts, 0)) * scale).astype(BF16)
        for one in range(2):
            here = pl.ds(pl.multiple_of((2 * at + one) * width, width), width)
            out_ref[here, :] = jnp.concatenate(
                [
                    both[width * e : width * e + width, 128 * one : 128 * one + 128]
                    for e in range(16)
                ],
                1,
            )
        return carry

    lax.fori_loop(0, g_ref.shape[0] // 2, pair, 0)


def spread_of(given, w, member, after):
    rows, columns, _ = given.shape
    return pl.pallas_call(
        spread_kernel,
        in_specs=[VMEM] * 3 + [ORDER],
        out_specs=VMEM,
        out_shape=jax.ShapeDtypeStruct((rows * FACTOR_WIDTH, columns * FACTOR_WIDTH), BF16),
        compiler_params=ROOM,
        cost_estimate=lasting(8),
        name="spread",
    )(given, w, member, after)


def grad_a_kernel(s_ref, x_ref, *refs):
    a_pieces, b_pieces = refs[:5], refs[5:10]
    a_ref, bd_ref, out_ref, turned_s = refs[10:]
    width = FACTOR_WIDTH
    rows = a_ref.shape[0]
    columns = bd_ref.shape[0] // width
    core = lax.axis_index("core")
    blocks, seqs = out_ref.shape[0], out_ref.shape[1] // 2

    def store_a(block, start, size, piece, source):
        to = pl.ds(pl.multiple_of(block * size, size), size)
        a_ref[to, :] = piece[source : source + size, :]

    def store_b(block, start, size, piece, source):
        at = ((block % 4) * 2 + block // 4) * 2
        half = size // 2
        for other in range(2):
            side = 1 - core if other else core
            to = pl.ds(pl.multiple_of((at + side) * half, half), half)
            part = slice(source + half * other, source + half * other + half)
            put(turned_s, to, piece[part, :].astype(F32))

    place_pairs(seq_index(), a_pieces, 128, store_a)
    place_pairs(res_index(), b_pieces, 256, store_b)
    for at in range(width):
        here = slice(at * columns, at * columns + columns)
        bd_ref[here, :] = take(turned_s, pl.ds(at, columns, stride=width)).astype(BF16)
    grad = nn(s_ref[...], bd_ref[...]).astype(BF16)
    out_ref[:, :seqs] = grad.reshape(blocks, seqs, grad.shape[1])
    out_ref[:, seqs:] = x_ref[...].reshape(blocks, seqs, grad.shape[1])


def grad_a_of(spread, refreshed, a_pieces, b_pieces):
    seqs = a_pieces[0].shape[1]
    rows, columns = 4 * a_pieces[1].shape[0], 4 * b_pieces[1].shape[0]
    groups, parts, members, depth = refreshed.shape
    return pl.pallas_call(
        grad_a_kernel,
        in_specs=[VMEM] * 12,
        out_specs=[VMEM] * 3,
        out_shape=[
            jax.ShapeDtypeStruct((rows, seqs), BF16),
            jax.ShapeDtypeStruct((columns, seqs), BF16),
            jax.ShapeDtypeStruct((groups, 2 * parts * members, depth), BF16),
        ],
        scratch_shapes=[pltpu.VMEM((2, columns, seqs // 2), F32)],
        compiler_params=ROOM,
        cost_estimate=lasting(6),
        name="grad_a",
    )(spread, refreshed, *a_pieces, *b_pieces)


def grad_b_kernel(a_ref, s_ref, _, out_ref, turned_s):
    width = FACTOR_WIDTH
    columns = out_ref.shape[0] // width
    left = a_ref[...].astype(F32).T.astype(BF16)
    for at in range(columns * width // 256):
        here = slice(256 * at, 256 * at + 256)
        put(turned_s, here, nn(left, s_ref[:, here]).T)
    for at in range(columns):
        to = slice(at * width, at * width + width)
        out_ref[to, :] = take(turned_s, pl.ds(at, width, stride=columns)).astype(BF16)


def grad_b_of(a_all, spread, after):
    seqs, columns = a_all.shape[1], spread.shape[1]
    return pl.pallas_call(
        grad_b_kernel,
        in_specs=[VMEM] * 2 + [ORDER],
        out_specs=VMEM,
        out_shape=jax.ShapeDtypeStruct((columns, seqs), BF16),
        scratch_shapes=[pltpu.VMEM((2, columns, seqs // 2), F32)],
        compiler_params=ROOM,
        cost_estimate=lasting(5),
        name="grad_b",
    )(a_all, spread, after)


def total_kernel(ga_ref, gb_ref, valid_ref, chain_ref, out_ref):
    width = FACTOR_WIDTH
    rows, seqs = gb_ref.shape[1:]
    x_hi, z = seq_index()
    x_lo, y = res_index()
    first = ((y * 2 + x_lo) * 2 + lax.axis_index("core")) * 32 + (x_hi * 4 + z) * 4
    part = lax.broadcasted_iota(jnp.int32, (rows, 1), 0) // width
    live = jnp.zeros((rows, 1), F32)
    for at in range(4):
        live = jnp.where(part == at, chain_ref[first + at].astype(F32), live)
    live = live * valid_ref[...].astype(F32)
    sums = []
    for source in (ga_ref, gb_ref):
        total = source[0, :rows].astype(F32)
        for at in range(1, source.shape[0]):
            total = total + source[at, :rows].astype(F32)
        sums.append(total * live)
    out_ref[...] = jnp.concatenate(sums, 0).T.astype(BF16)


def total_grads(ga, gb, valid, chain):
    return pl.pallas_call(
        total_kernel,
        in_specs=[VMEM] * 3 + [SMEM],
        out_specs=VMEM,
        out_shape=jax.ShapeDtypeStruct((gb.shape[2], 2 * gb.shape[1]), BF16),
        compiler_params=ROOM,
        cost_estimate=lasting(2),
        name="total_grads",
    )(ga, gb, valid, chain)


def home_kernel(gf_ref, w_ref, x_ref, x_out_ref, ct_ref, x_s, ct_s):
    width = FACTOR_WIDTH
    groups, rows, depth = x_ref.shape
    parts = 4
    rows = rows // 2
    seqs = rows // parts
    residues = groups * parts
    given = gf_ref[...].reshape(groups * seqs, depth)
    lane = lax.broadcasted_iota(jnp.int32, (1, depth), 1) // width % parts
    back = jnp.concatenate([w_ref[:width, :]] * parts + [w_ref[width:, :]] * parts, 0)
    for at in range(parts):
        upstream = nn(jnp.where(lane == at, given.astype(F32), 0.0).astype(BF16), back)
        x = x_ref[:, rows + seqs * at : rows + seqs * at + seqs]
        x = x.reshape(groups * seqs, depth).astype(F32)
        center = x - jnp.mean(x, -1, keepdims=True)
        inverse = lax.rsqrt(jnp.mean(center * center, -1, keepdims=True) + 1e-05)
        scaled = center * inverse
        cotangent = inverse * (
            upstream
            - jnp.mean(upstream, -1, keepdims=True)
            - scaled * jnp.mean(upstream * scaled, -1, keepdims=True)
        )
        for group in range(groups):
            here = pl.ds(group * parts + at, seqs, stride=residues)
            put(x_s, here, x[group * seqs : group * seqs + seqs])
            put(ct_s, here, cotangent[group * seqs : group * seqs + seqs])
    x_out_ref[...] = take(x_s, slice(None)).reshape(seqs, residues, depth).astype(BF16)
    ct_ref[...] = take(ct_s, slice(None)).reshape(seqs, residues, depth).astype(BF16)


def finish_home(gf, w, both):
    groups, rows, depth = both.shape
    seqs, residues = rows // 8, groups * 4
    shape = (seqs, residues, depth)
    return pl.pallas_call(
        home_kernel,
        in_specs=[VMEM] * 3,
        out_specs=[VMEM] * 2,
        out_shape=[jax.ShapeDtypeStruct(shape, BF16)] * 2,
        scratch_shapes=[pltpu.VMEM((2, seqs * residues, depth // 2), F32)] * 2,
        compiler_params=ROOM,
        cost_estimate=lasting(5),
        name="finish_home",
    )(gf, w, both)


def hold_kernel(*refs):
    pass


def hold(first, second, after):
    return pl.pallas_call(
        hold_kernel,
        in_specs=[ORDER] * 3,
        out_specs=[ORDER] * 2,
        out_shape=[jax.ShapeDtypeStruct(one.shape, one.dtype) for one in (first, second)],
        input_output_aliases={0: 0, 1: 1},
        cost_estimate=lasting(0.1),
        name="hold",
    )(first, second, after)


def turn_by(steps):
    return [(at, (at + steps) % 4) for at in range(4)]


SWAP = [(0, 1), (1, 0)]


def ring(x, along, across, after=None):
    half = x.shape[0] // 2
    partner = lax.ppermute(x, across, SWAP)
    below = lax.ppermute(x, along, turn_by(1))
    above = lax.ppermute(x, along, turn_by(3))
    far_low = lax.ppermute(below[:half], along, turn_by(1))
    far_high = lax.ppermute(above[half:], along, turn_by(3))
    partner_below = lax.ppermute(partner, along, turn_by(1))
    partner_above = lax.ppermute(partner, along, turn_by(3))
    if after is not None:
        far_low, far_high = hold(far_low, far_high, after)
    partner_low = lax.ppermute(far_low, across, SWAP)
    partner_high = lax.ppermute(far_high, across, SWAP)
    return [
        x, above, far_low, far_high, below,
        partner, partner_above, partner_low, partner_high, partner_below,
    ]


def ring_pairs(x, along, across):
    partner = lax.ppermute(x, across, SWAP)
    pair = jnp.concatenate([x, partner], 0)
    half = x.shape[0]
    below = lax.ppermute(pair, along, turn_by(1))
    above = lax.ppermute(pair, along, turn_by(3))
    far = lax.ppermute(below[:half], along, turn_by(1))
    far_partner = lax.ppermute(above[half:], along, turn_by(3))
    return [pair, above, far, far_partner, below]


def per_device(
    multiple_alignment_rep,
    pair_rep,
    aligned_member_valid,
    chain_position_valid,
    horizontal_entry_matrices,
    horizontal_exit_matrix,
    bias_proj,
    vertical_entry_matrices,
    vertical_exit_matrix,
    dyadic_projection_matrices,
    outer_out,
    pair_grad,
):
    seqs_here, res_here, depth = multiple_alignment_rep.shape
    residues = pair_rep.shape[1]
    pair_width = outer_out.shape[1]
    q_size, b_size, r_size = 8, 8, 16
    width = FACTOR_WIDTH
    q_at = lax.axis_index("x_hi") * 4 + lax.axis_index("z")
    member = aligned_member_valid.reshape(1, -1)
    chain_row = chain_position_valid.reshape(1, residues)

    dyadic_t = dyadic_projection_matrices.T
    cube = outer_out.reshape(width, width // 2, 2, pair_width)
    w_outer = cube.transpose(1, 0, 2, 3).reshape(16 * width, 2 * pair_width)
    grad_here = lax.dynamic_index_in_dim(
        pair_grad.reshape(res_here, r_size, q_size, 4, pair_width), q_at, 2, keepdims=False
    ).reshape(res_here, r_size * 4, pair_width)

    bias = pair_bias(pair_rep, bias_proj.astype(F32).T, chain_row)
    x_rows = lax.all_to_all(
        multiple_alignment_rep.reshape(b_size, seqs_here // b_size, res_here, depth),
        ("y", "x_lo"), 0, 0, tiled=True,
    )
    x_other = lax.ppermute(x_rows, "core", SWAP)
    q, k, v, g = row_entry(x_rows, x_other, chain_row, horizontal_entry_matrices)
    bias_pieces = ring(bias, "y", "x_lo", after=q)
    after_row = row_attention(q, k, v, g, x_rows, horizontal_exit_matrix, bias_pieces)

    spread = spread_of(grad_here, w_outer, member, after_row)
    columns = lax.all_to_all(
        after_row.reshape(q_size * b_size, 16, depth),
        ("x_hi", "z", "y", "x_lo"), 0, 0, tiled=True,
    )
    refreshed, factor_a, factor_b = col_attention(
        columns, member, chain_position_valid,
        vertical_entry_matrices, vertical_exit_matrix, dyadic_t, q_size, spread,
    )
    b_other = lax.ppermute(factor_b, "core", SWAP)
    a_pieces = ring_pairs(factor_a, "z", "x_hi")
    b_pieces = ring_pairs(jnp.concatenate([factor_b, b_other], 0), "y", "x_lo")

    a_all, bd, going = grad_a_of(spread, refreshed, a_pieces, b_pieces)
    back = lax.all_to_all(going, ("x_hi", "z"), 0, 0, tiled=True)
    delta = couple(a_all, bd, w_outer, member, going)
    gb = grad_b_of(a_all, spread, delta)
    gb = lax.all_to_all(
        gb.reshape(r_size, 4 * width, -1), ("y", "x_lo", "core"), 0, 0, tiled=True
    )
    couple_delta = assemble(ring(delta, "z", "x_hi"))
    factors = total_grads(back, gb, member, chain_position_valid)
    factors = lax.all_to_all(
        factors.reshape(q_size, seqs_here, 8 * width), ("x_hi", "z"), 0, 0, tiled=True
    )
    alignment_refreshed, cotangent = finish_home(factors, dyadic_t, back)
    return (alignment_refreshed, couple_delta, cotangent)


def solution(mesh):
    torus = jax.sharding.Mesh(
        mesh.devices.reshape(2, 4, 4, 2, 2), ("x_hi", "z", "y", "x_lo", "core")
    )
    seq, res = ("x_hi", "z"), ("y", "x_lo", "core")
    placed = (
        P(seq, res, None),
        P(res, None, None),
        P(),
        P(),
        P(),
        P(),
        P(),
        P(),
        P(),
        P(),
        P(),
        P(res, None, None),
    )
    return jax.shard_map(
        per_device,
        mesh=torus,
        in_specs=placed,
        out_specs=(P(seq, res, None), P(res, None, None), P(seq, res, None)),
        check_vma=False,
    )
```

```python
import jax
import jax.numpy as jnp
from jax import lax
from jax.experimental import pallas as pl
from jax.experimental.pallas import tpu as pltpu
from jax.sharding import PartitionSpec as P

FACTOR_WIDTH = 32
H = 8
HEAD_SIZE = 32
LOG2E = 1.4426950408889634
MASKED = -1000000000.0 * LOG2E
BF16 = jnp.bfloat16
F32 = jnp.float32
NT = (((1,), (1,)), ((), ()))
ROW_UNROLL = 1
COL_STEP = 64
PAIR_UNROLL = 2

VMEM = pl.BlockSpec(memory_space=pltpu.VMEM)
SMEM = pl.BlockSpec(memory_space=pltpu.SMEM)
ORDER = pl.BlockSpec(memory_space=pl.ANY)
ROOM = pltpu.CompilerParams(vmem_limit_bytes=56 * 1024 * 1024)


def lasting(microseconds):
    return pl.CostEstimate(
        flops=0, bytes_accessed=int(microseconds * 3.69e6), transcendentals=0
    )


def nn(left, right):
    return jnp.dot(left, right, preferred_element_type=F32)


def nt(left, right):
    return lax.dot_general(left, right, NT, preferred_element_type=F32)


def standardize(values):
    center = values - jnp.mean(values, -1, keepdims=True)
    spread = jnp.mean(center * center, -1, keepdims=True)
    return center * lax.rsqrt(spread + 1e-05)


def put(ref, rows, values):
    for half in range(2):
        ref[half, rows, :] = values[:, 128 * half : 128 * half + 128]


def take(ref, rows):
    return jnp.concatenate([ref[0, rows, :], ref[1, rows, :]], 1)


def column_of(row):
    return jnp.broadcast_to(row.astype(F32), (8, row.shape[1])).T[:, :1]


def seq_index():
    return lax.axis_index("x_hi"), lax.axis_index("z")


def res_index():
    return lax.axis_index("x_lo"), lax.axis_index("y")


def scale_of(member):
    return 1.0 / jnp.sum(member.astype(F32), keepdims=True)


def bias_kernel(pair_ref, proj_ref, valid_ref, out_ref, turn_s):
    at = pl.program_id(0)
    rows, residues, depth = pair_ref.shape
    line = lax.broadcasted_iota(jnp.int32, (depth, depth), 0)
    lane = lax.broadcasted_iota(jnp.int32, (depth, depth), 1)
    centering = (jnp.where(line == lane, 1.0, 0.0) - 1.0 / depth).astype(BF16)
    live = valid_ref[...] > 0
    proj = proj_ref[...]
    blank = jnp.zeros_like(proj)
    mean = jnp.full_like(proj, 1.0 / depth)
    sides = jnp.concatenate(
        [jnp.concatenate([proj, blank], 1), jnp.concatenate([blank, mean], 1)], 0
    ).astype(BF16)
    center = nn(pair_ref[...].reshape(rows * residues, depth), centering)
    both = jnp.concatenate([center.astype(BF16), (center * center).astype(BF16)], 1)
    for one in range(rows):
        sums = nt(sides, both[one * residues : one * residues + residues])
        bias = sums[:H] * lax.rsqrt(sums[H:] + 1e-05) * LOG2E
        bias = jnp.where(live, bias, MASKED)
        here = pl.ds(pl.multiple_of((at * rows + one) * H, H), H)
        for part in range(residues // 128):
            turn_s[part, here, :] = bias[:, 128 * part : 128 * part + 128]

    @pl.when(at == pl.num_programs(0) - 1)
    def _():
        total = out_ref.shape[0] // H
        for head in range(H):
            for part in range(residues // 128):
                out_ref[total * head : total * head + total, 128 * part : 128 * part + 128] = (
                    turn_s[part, pl.ds(head, total, stride=H), :].astype(BF16)
                )


def pair_bias(pair, proj, valid):
    rows, residues, depth = pair.shape
    step = 4
    return pl.pallas_call(
        bias_kernel,
        grid=(rows // step,),
        in_specs=[
            pl.BlockSpec((step, residues, depth), lambda g: (g, 0, 0)),
            pl.BlockSpec((H, depth), lambda g: (0, 0)),
            pl.BlockSpec((1, residues), lambda g: (0, 0)),
        ],
        out_specs=pl.BlockSpec((rows * H, residues), lambda g: (0, 0)),
        out_shape=jax.ShapeDtypeStruct((rows * H, residues), BF16),
        scratch_shapes=[pltpu.VMEM((residues // 128, rows * H, 128), F32)],
        compiler_params=ROOM,
        cost_estimate=lasting(9),
        name="pair_bias",
    )(pair, proj, valid)


def scores_of(query, keys, side):
    lanes = slice(128 * side, 128 * side + 128)
    lane = lax.broadcasted_iota(jnp.int32, (1, 128), 1) // HEAD_SIZE
    part = query[:, lanes]
    spread = [jnp.where(lane == head, part, 0.0).astype(BF16) for head in range(4)]
    return nt(jnp.concatenate(spread, 0), keys[:, lanes])


def weigh(scores, values, side):
    rows = scores.shape[0] // 4
    lane = lax.broadcasted_iota(jnp.int32, (1, 128), 1) // HEAD_SIZE
    weights = jnp.exp2(scores - jnp.max(scores, -1, keepdims=True))
    scale = 1.0 / jnp.sum(weights, -1, keepdims=True)
    summed = nn(weights.astype(BF16), values[:, 128 * side : 128 * side + 128])
    output = summed[:rows] * scale[:rows]
    for head in range(1, 4):
        here = slice(rows * head, rows * head + rows)
        output = jnp.where(lane == head, summed[here] * scale[here], output)
    return output


def entry_kernel(x_ref, other_ref, valid_ref, w_ref, q_ref, k_ref, v_ref, g_ref, live_s):
    blocks, seqs, rows, depth = x_ref.shape
    core = lax.axis_index("core")
    live_s[...] = jnp.broadcast_to(column_of(valid_ref[...]), live_s.shape)
    for s in range(seqs):
        for other in range(2):
            source = other_ref if other else x_ref
            x = source[:, s].reshape(blocks * rows, depth)
            normed = standardize(x.astype(F32)).astype(BF16)
            pair = nn(normed, w_ref[:, depth : 3 * depth])
            side = 1 - core if other else core
            for at in range(blocks):
                here = slice(rows * at, rows * at + rows)
                to = pl.ds(pl.multiple_of((2 * at + side) * rows, rows), rows)
                k_ref[s, to, :] = (pair[here, :depth] * live_s[to, :1]).astype(BF16)
                v_ref[s, to, :] = pair[here, depth:].astype(BF16)
            if not other:
                query = nn(normed, w_ref[:, :depth]) * (HEAD_SIZE**-0.5 * LOG2E)
                q_ref[s] = query.astype(BF16)
                g_ref[s] = jax.nn.sigmoid(nn(normed, w_ref[:, 3 * depth :])).astype(BF16)


def row_entry(x, other, valid, w):
    blocks, seqs, rows, depth = x.shape
    here = jax.ShapeDtypeStruct((seqs, blocks * rows, depth), BF16)
    full = jax.ShapeDtypeStruct((seqs, 2 * blocks * rows, depth), BF16)
    return pl.pallas_call(
        entry_kernel,
        in_specs=[VMEM] * 4,
        out_specs=[VMEM] * 4,
        out_shape=[here, full, full, here],
        scratch_shapes=[pltpu.VMEM((2 * blocks * rows, 128), F32)],
        compiler_params=ROOM,
        cost_estimate=lasting(5),
        name="row_entry",
    )(x, other, valid, w)


def place(index, pieces, store):
    across, along = index
    for block, piece in enumerate(pieces):
        store((across ^ (block // 4)) * 4 + ((along + block) & 3), piece)


def place_halves(index, pieces, size, store):
    across, along = index
    pieces = list(pieces)
    for block in range(8):
        parts = 2 if block % 4 == 2 else 1
        for part in range(parts):
            at = (across ^ (block // 4)) * 4 + ((along + block) & 3)
            store(at, size // parts * part, size // parts, pieces.pop(0))


def row_kernel(q_ref, k_ref, v_ref, g_ref, x_ref, wo_ref, *refs):
    pieces, (out_ref, bias_s) = refs[:8], refs[8:]
    blocks, seqs, rows, depth = x_ref.shape

    def store(block, piece):
        bias_s[(block % 4) * 2 + block // 4] = piece[...]

    place(res_index(), pieces, store)
    upper = lax.broadcasted_iota(jnp.int32, (rows // 8, 8, depth), 1) < 4

    def block(at, carry):
        here = pl.ds(pl.multiple_of(at * rows, rows), rows)
        scores = {}
        for side in range(2):
            offset = bias_s[at, 4 * rows * side : 4 * rows * side + 4 * rows, :].astype(F32)
            for s in range(seqs):
                scores[s, side] = scores_of(q_ref[s, here, :], k_ref.at[s], side) + offset
        done = []
        for s in range(seqs):
            output = jnp.concatenate(
                [weigh(scores[s, side], v_ref.at[s], side) for side in range(2)], 1
            )
            gated = (g_ref[s, here, :].astype(F32) * output).astype(BF16)
            after = x_ref[at, s].astype(F32) + nn(gated, wo_ref[...])
            done.append(after.reshape(rows // 8, 8, depth))
        even, odd = [], []
        for first, second in zip(done[::2], done[1::2]):
            even.append(jnp.where(upper, first, pltpu.roll(second, 4, 1)))
            odd.append(jnp.where(upper, pltpu.roll(first, 4, 1), second))
        even = jnp.concatenate(even, 1).astype(BF16)
        odd = jnp.concatenate(odd, 1).astype(BF16)
        for pair in range(rows // 8):
            out_ref[2 * pair, at] = even[pair]
            out_ref[2 * pair + 1, at] = odd[pair]
        return carry

    lax.fori_loop(0, blocks, block, 0, unroll=ROW_UNROLL)


def row_attention(q, k, v, g, x, wo, bias):
    blocks, seqs, rows, depth = x.shape
    return pl.pallas_call(
        row_kernel,
        in_specs=[VMEM] * (6 + len(bias)),
        out_specs=VMEM,
        out_shape=jax.ShapeDtypeStruct((rows // 4, blocks, 4 * seqs, depth), BF16),
        scratch_shapes=[pltpu.VMEM((blocks,) + bias[0].shape, BF16)],
        compiler_params=ROOM,
        cost_estimate=lasting(14),
        name="row_attention",
    )(q, k, v, g, x, wo, *bias)


def col_kernel(
    y_ref, valid_ref, chain_ref, w_ref, wo_ref, dyadic_ref, _,
    out_ref, b_ref, y_s, q_s, k_s, v_s, g_s, o_s,
):
    tokens, depth = y_s.shape[1], 2 * y_s.shape[2]
    parts = q_s.shape[0]
    seqs = tokens // parts
    live = valid_ref[...].astype(F32)
    live_column = column_of(live)
    offset = jnp.where(live > 0, 0.0, MASKED)
    x_hi, z = seq_index()
    x_lo, y_at = res_index()
    first = ((y_at * 2 + x_lo) * 2 + lax.axis_index("core")) * 32 + (x_hi * 4 + z) * parts
    put(y_s, slice(None), y_ref[...].reshape(tokens, depth).astype(F32))
    for at in range(parts):
        y = take(y_s, pl.ds(at, seqs, stride=parts))
        mixed = nn(standardize(y).astype(BF16), w_ref[...])
        q_s[at] = mixed[:, :depth] * (HEAD_SIZE**-0.5 * LOG2E)
        k_s[at] = (mixed[:, depth : 2 * depth] * live_column).astype(BF16)
        v_s[at] = mixed[:, 2 * depth : 3 * depth].astype(BF16)
        g_s[at] = jax.nn.sigmoid(mixed[:, 3 * depth :])
    step = COL_STEP

    def block(part, carry):
        here = pl.ds(pl.multiple_of(part * step, step), step)
        scores = [
            [scores_of(q_s[at, here, :], k_s[at], side) + offset for side in range(2)]
            for at in range(parts)
        ]
        for at in range(parts):
            output = jnp.concatenate(
                [weigh(scores[at][side], v_s[at], side) for side in range(2)], 1
            )
            o_s[at, here, :] = (g_s[at, here, :] * output).astype(BF16)
        return carry

    lax.fori_loop(0, seqs // step, block, 0)
    for at in range(parts):
        y = take(y_s, pl.ds(at, seqs, stride=parts))
        done = (y + nn(o_s[at], wo_ref[...])).astype(BF16)
        groups = out_ref.shape[0]
        here = slice(seqs // groups * at, seqs // groups * at + seqs // groups)
        out_ref[:, here, :] = done.reshape(groups, seqs // groups, depth)
        normed = standardize(done.astype(F32)).astype(BF16)
        factors = nt(dyadic_ref[...], normed) * (live * chain_ref[first + at].astype(F32))
        for group in range(groups):
            to = slice(128 + 32 * at, 160 + 32 * at)
            out_ref[group, to, :] = factors[:32].astype(BF16)
        b_ref[pl.ds(32 * at, 32), :] = factors[32:].astype(BF16)


def col_attention(y, valid, chain, w, wo, dyadic_t, groups, after):
    sources, eight, depth = y.shape
    tokens = sources * eight
    seqs = tokens // 4
    return pl.pallas_call(
        col_kernel,
        in_specs=[VMEM] * 2 + [SMEM] + [VMEM] * 3 + [ORDER],
        out_specs=[VMEM] * 2,
        out_shape=[
            jax.ShapeDtypeStruct((groups, 2 * 4 * FACTOR_WIDTH, seqs), BF16),
            jax.ShapeDtypeStruct((4 * FACTOR_WIDTH, seqs), BF16),
        ],
        scratch_shapes=[
            pltpu.VMEM((2, tokens, depth // 2), F32),
            pltpu.VMEM((4, seqs, depth), F32),
            pltpu.VMEM((4, seqs, depth), BF16),
            pltpu.VMEM((4, seqs, depth), BF16),
            pltpu.VMEM((4, seqs, depth), F32),
            pltpu.VMEM((4, seqs, depth), BF16),
        ],
        compiler_params=ROOM,
        cost_estimate=lasting(8),
        name="col_attention",
    )(y, valid, chain, w, wo, dyadic_t, after)


def assemble_kernel(*refs):
    pieces, (out_ref, d_s) = refs[:10], refs[10:]
    step = out_ref.shape[0]
    at = pl.program_id(0)

    def store(block, start, size, piece):
        d_s[block, start : start + size] = piece[...]

    @pl.when(at == 0)
    def _():
        place_halves(seq_index(), pieces, d_s.shape[1], store)

    upper = lax.broadcasted_iota(jnp.int32, (8, 8, 128), 1) < 4

    def line(one, carry):
        even, odd = [], []
        for pair in range(4):
            first = d_s[2 * pair, at * step + one].astype(F32).reshape(8, 8, 128)
            second = d_s[2 * pair + 1, at * step + one].astype(F32).reshape(8, 8, 128)
            even.append(jnp.where(upper, first, pltpu.roll(second, 4, 1)))
            odd.append(jnp.where(upper, pltpu.roll(first, 4, 1), second))
        both = jnp.stack([jnp.stack(even, 1), jnp.stack(odd, 1)], 1)
        out_ref[one] = both.reshape(512, 128).astype(BF16)
        return carry

    lax.fori_loop(0, step, line, 0, unroll=2)


def assemble(pieces):
    rows, columns, depth = pieces[0].shape
    step = 8
    return pl.pallas_call(
        assemble_kernel,
        grid=(rows // step,),
        in_specs=[VMEM] * len(pieces),
        out_specs=pl.BlockSpec((step, 8 * columns, depth), lambda g: (g, 0, 0)),
        out_shape=jax.ShapeDtypeStruct((rows, 8 * columns, depth), BF16),
        scratch_shapes=[pltpu.VMEM((8, rows, columns, depth), BF16)],
        compiler_params=ROOM,
        cost_estimate=lasting(5),
        name="assemble",
    )(*pieces)


def spread_kernel(g_ref, w_ref, member_ref, _, out_ref):
    width = FACTOR_WIDTH
    scale = scale_of(member_ref[...])
    blank = jnp.zeros((64, 128), BF16)

    def pair(at, carry):
        parts = []
        for one in range(2):
            given = g_ref[2 * at + one]
            parts.append(jnp.concatenate([given, blank], 1))
            parts.append(jnp.concatenate([blank, given], 1))
        both = (nt(w_ref[...], jnp.concatenate(parts, 0)) * scale).astype(BF16)
        for one in range(2):
            here = pl.ds(pl.multiple_of((2 * at + one) * width, width), width)
            out_ref[here, :] = jnp.concatenate(
                [
                    both[width * e : width * e + width, 128 * one : 128 * one + 128]
                    for e in range(16)
                ],
                1,
            )
        return carry

    lax.fori_loop(0, g_ref.shape[0] // 2, pair, 0)


def spread_of(given, w, member, after):
    rows, columns, _ = given.shape
    return pl.pallas_call(
        spread_kernel,
        in_specs=[VMEM] * 3 + [ORDER],
        out_specs=VMEM,
        out_shape=jax.ShapeDtypeStruct((rows * FACTOR_WIDTH, columns * FACTOR_WIDTH), BF16),
        compiler_params=ROOM,
        cost_estimate=lasting(8),
        name="spread",
    )(given, w, member, after)


def couple_kernel(both_ref, w_ref, member_ref, b_ref, out_ref, a_ref, bd_ref, o_s, b_s):
    width = FACTOR_WIDTH
    rows, columns = o_s.shape
    put(b_s, slice(None), b_ref[...].reshape(columns, b_ref.shape[2]).astype(F32))
    count = columns // width
    for at in range(width):
        here = slice(at * count, at * count + count)
        bd_ref[here, :] = take(b_s, pl.ds(at, count, stride=width)).astype(BF16)
    a_ref[...] = both_ref[:, 128:].reshape(a_ref.shape)
    for at in range(columns // 256):
        here = slice(256 * at, 256 * at + 256)
        o_s[:, here] = nt(a_ref[...], bd_ref[here, :]).astype(BF16)
    scale = scale_of(member_ref[...])
    w = w_ref[...].astype(F32).T.astype(BF16)
    low = lax.broadcasted_iota(jnp.int32, (128, 128), 1) < 64

    def pair(at, carry):
        outer = o_s[pl.ds(pl.multiple_of(at * 2 * width, 2 * width), 2 * width), :]
        stacks = []
        for one in range(2):
            part = outer[width * one : width * one + width]
            stacks.append(
                jnp.concatenate([part[:, 128 * e : 128 * e + 128] for e in range(16)], 0)
            )
        both = nn(w, jnp.concatenate(stacks, 1))
        top = jnp.where(low, both[:128, :128], pltpu.roll(both[:128, 128:], 64, 1))
        bottom = jnp.where(low, pltpu.roll(both[128:, :128], 64, 1), both[128:, 128:])
        delta = ((top + bottom) * scale).T
        out_ref[pl.ds(at * 2, 2)] = delta.reshape(2, 64, 128).astype(BF16)
        return carry

    lax.fori_loop(0, rows // (2 * width), pair, 0, unroll=PAIR_UNROLL)


def couple(both, w, member, b_all):
    seqs = both.shape[2]
    rows, columns = both.shape[0] * 128, b_all.shape[0] * 128
    return pl.pallas_call(
        couple_kernel,
        in_specs=[VMEM] * 4,
        out_specs=[VMEM] * 3,
        out_shape=[
            jax.ShapeDtypeStruct((rows // FACTOR_WIDTH, columns // FACTOR_WIDTH, 128), BF16),
            jax.ShapeDtypeStruct((rows, seqs), BF16),
            jax.ShapeDtypeStruct((columns, seqs), BF16),
        ],
        scratch_shapes=[
            pltpu.VMEM((rows, columns), BF16),
            pltpu.VMEM((2, columns, seqs // 2), F32),
        ],
        compiler_params=ROOM,
        cost_estimate=lasting(9),
        name="couple",
    )(both, w, member, b_all)


def grad_a_kernel(bd_ref, s_ref, *refs):
    out_ref = refs[-1]
    for at in range(4):
        here = slice(256 * at, 256 * at + 256)
        out_ref[:, here] = nn(s_ref[here, :], bd_ref[...]).T.astype(BF16)


def grad_a_of(bd, spread, after):
    return pl.pallas_call(
        grad_a_kernel,
        in_specs=[VMEM] * 2 + [ORDER] * len(after),
        out_specs=VMEM,
        out_shape=jax.ShapeDtypeStruct((bd.shape[1], spread.shape[0]), BF16),
        compiler_params=ROOM,
        cost_estimate=lasting(4),
        name="grad_a",
    )(bd, spread, *after)


def grad_b_kernel(a_ref, s_ref, *refs):
    out_ref, turned_s = refs[-2:]
    width = FACTOR_WIDTH
    columns = out_ref.shape[0] // width
    left = a_ref[...].astype(F32).T.astype(BF16)
    for at in range(columns * width // 256):
        here = slice(256 * at, 256 * at + 256)
        put(turned_s, here, nn(left, s_ref[:, here]).T)
    for at in range(columns):
        to = slice(at * width, at * width + width)
        out_ref[to, :] = take(turned_s, pl.ds(at, width, stride=columns)).astype(BF16)


def grad_b_of(a_all, spread, after):
    seqs, columns = a_all.shape[1], spread.shape[1]
    return pl.pallas_call(
        grad_b_kernel,
        in_specs=[VMEM] * 2 + [ORDER] * len(after),
        out_specs=VMEM,
        out_shape=jax.ShapeDtypeStruct((columns, seqs), BF16),
        scratch_shapes=[pltpu.VMEM((2, columns, seqs // 2), F32)],
        compiler_params=ROOM,
        cost_estimate=lasting(5),
        name="grad_b",
    )(a_all, spread, *after)


def pack_kernel(ga_ref, gb_ref, out_ref):
    groups, members, _ = out_ref.shape
    wide = ga_ref.shape[1]
    total = gb_ref[0].astype(F32)
    for at in range(1, gb_ref.shape[0]):
        total = total + gb_ref[at].astype(F32)
    out_ref[:, :, :wide] = ga_ref[...].reshape(groups, members, wide)
    out_ref[:, :, wide:] = total.T.reshape(groups, members, total.shape[0]).astype(BF16)


def pack_grads(ga, gb, groups):
    seqs, wide = ga.shape
    return pl.pallas_call(
        pack_kernel,
        in_specs=[VMEM] * 2,
        out_specs=VMEM,
        out_shape=jax.ShapeDtypeStruct((groups, seqs // groups, wide + gb.shape[1]), BF16),
        compiler_params=ROOM,
        cost_estimate=lasting(3),
        name="pack_grads",
    )(ga, gb)


def home_kernel(gf_ref, w_ref, x_ref, member_ref, chain_ref, x_out_ref, ct_ref, x_s, ct_s):
    width = FACTOR_WIDTH
    groups, rows, depth = x_ref.shape
    parts = 4
    seqs = rows // 2 // parts
    residues = groups * parts
    wide = residues * width
    x_hi, z = seq_index()
    x_lo, y = res_index()
    first = ((y * 2 + x_lo) * 2 + lax.axis_index("core")) * residues
    member = member_ref[pl.ds(x_hi * 4 + z, 1), :]
    member = jnp.broadcast_to(member.astype(F32), (8, member.shape[1])).T[:seqs, :1]
    total = gf_ref[0, :, :wide].astype(F32)
    for at in range(1, groups):
        total = total + gf_ref[at, :, :wide].astype(F32)
    lane = lax.broadcasted_iota(jnp.int32, (1, 128), 1) // width
    lines = []
    for group in range(groups):
        live = jnp.zeros((1, 128), F32)
        for at in range(parts):
            here = chain_ref[first + group * parts + at].astype(F32)
            live = jnp.where(lane == at, here, live)
        live = live * member
        left = total[:, 128 * group : 128 * group + 128] * live
        right = gf_ref[group, :, wide:].astype(F32) * live
        lines.append(jnp.concatenate([left, right], 1))
    given = jnp.concatenate(lines, 0)
    lane = lax.broadcasted_iota(jnp.int32, (1, depth), 1) // width % parts
    back = jnp.concatenate([w_ref[:width, :]] * parts + [w_ref[width:, :]] * parts, 0)
    for at in range(parts):
        upstream = nn(jnp.where(lane == at, given, 0.0).astype(BF16), back)
        x = x_ref[:, seqs * at : seqs * at + seqs]
        x = x.reshape(groups * seqs, depth).astype(F32)
        center = x - jnp.mean(x, -1, keepdims=True)
        inverse = lax.rsqrt(jnp.mean(center * center, -1, keepdims=True) + 1e-05)
        scaled = center * inverse
        cotangent = inverse * (
            upstream
            - jnp.mean(upstream, -1, keepdims=True)
            - scaled * jnp.mean(upstream * scaled, -1, keepdims=True)
        )
        for group in range(groups):
            here = pl.ds(group * parts + at, seqs, stride=residues)
            put(x_s, here, x[group * seqs : group * seqs + seqs])
            put(ct_s, here, cotangent[group * seqs : group * seqs + seqs])
    x_out_ref[...] = take(x_s, slice(None)).reshape(seqs, residues, depth).astype(BF16)
    ct_ref[...] = take(ct_s, slice(None)).reshape(seqs, residues, depth).astype(BF16)


def finish_home(gf, w, both, member, chain):
    groups, rows, depth = both.shape
    seqs, residues = rows // 8, groups * 4
    shape = (seqs, residues, depth)
    return pl.pallas_call(
        home_kernel,
        in_specs=[VMEM] * 4 + [SMEM],
        out_specs=[VMEM] * 2,
        out_shape=[jax.ShapeDtypeStruct(shape, BF16)] * 2,
        scratch_shapes=[pltpu.VMEM((2, seqs * residues, depth // 2), F32)] * 2,
        compiler_params=ROOM,
        cost_estimate=lasting(6),
        name="finish_home",
    )(gf, w, both, member, chain)


def hold_kernel(*refs):
    pass


def hold(arrays, after):
    count = len(arrays)
    return pl.pallas_call(
        hold_kernel,
        in_specs=[ORDER] * (count + 1),
        out_specs=[ORDER] * count,
        out_shape=[jax.ShapeDtypeStruct(one.shape, one.dtype) for one in arrays],
        input_output_aliases={at: at for at in range(count)},
        cost_estimate=lasting(0.1),
        name="hold",
    )(*arrays, after)


def turn_by(steps):
    return [(at, (at + steps) % 4) for at in range(4)]


SWAP = [(0, 1), (1, 0)]


def ring(x, along, across, after=None):
    partner = lax.ppermute(x, across, SWAP)
    below = lax.ppermute(x, along, turn_by(1))
    above = lax.ppermute(x, along, turn_by(3))
    far = lax.ppermute(x, along, turn_by(2))
    if after is not None:
        partner, far = hold([partner, far], after)
    partner_below = lax.ppermute(partner, along, turn_by(1))
    partner_above = lax.ppermute(partner, along, turn_by(3))
    partner_far = lax.ppermute(far, across, SWAP)
    return [x, above, far, below, partner, partner_above, partner_far, partner_below]


def ring_halves(x, along, across):
    half = x.shape[0] // 2
    partner = lax.ppermute(x, across, SWAP)
    below = lax.ppermute(x, along, turn_by(1))
    above = lax.ppermute(x, along, turn_by(3))
    far_low = lax.ppermute(below[:half], along, turn_by(1))
    far_high = lax.ppermute(above[half:], along, turn_by(3))
    partner_below = lax.ppermute(partner, along, turn_by(1))
    partner_above = lax.ppermute(partner, along, turn_by(3))
    partner_low = lax.ppermute(far_low, across, SWAP)
    partner_high = lax.ppermute(far_high, across, SWAP)
    return [
        x, above, far_low, far_high, below,
        partner, partner_above, partner_low, partner_high, partner_below,
    ]


def per_device(
    multiple_alignment_rep,
    pair_rep,
    aligned_member_valid,
    chain_position_valid,
    horizontal_entry_matrices,
    horizontal_exit_matrix,
    bias_proj,
    vertical_entry_matrices,
    vertical_exit_matrix,
    dyadic_projection_matrices,
    outer_out,
    pair_grad,
):
    seqs_here, res_here, depth = multiple_alignment_rep.shape
    residues = pair_rep.shape[1]
    pair_width = outer_out.shape[1]
    q_size, b_size, r_size = 8, 8, 16
    width = FACTOR_WIDTH
    q_at = lax.axis_index("x_hi") * 4 + lax.axis_index("z")
    member = aligned_member_valid.reshape(1, -1)
    chain_row = chain_position_valid.reshape(1, residues)

    dyadic_t = dyadic_projection_matrices.T
    cube = outer_out.reshape(width, width // 2, 2, pair_width)
    w_outer = cube.transpose(1, 0, 2, 3).reshape(16 * width, 2 * pair_width)
    grad_here = lax.dynamic_index_in_dim(
        pair_grad.reshape(res_here, r_size, q_size, 4, pair_width), q_at, 2, keepdims=False
    ).reshape(res_here, r_size * 4, pair_width)

    bias = pair_bias(pair_rep, bias_proj.astype(F32).T, chain_row)
    x_rows = lax.all_to_all(
        multiple_alignment_rep.reshape(b_size, seqs_here // b_size, res_here, depth),
        ("y", "x_lo"), 0, 0, tiled=True,
    )
    (x_rows,) = hold([x_rows], bias)
    x_other = lax.ppermute(x_rows, "core", SWAP)
    q, k, v, g = row_entry(x_rows, x_other, chain_row, horizontal_entry_matrices)
    bias_pieces = ring(bias, "y", "x_lo", after=q)
    after_row = row_attention(q, k, v, g, x_rows, horizontal_exit_matrix, bias_pieces)

    spread = spread_of(grad_here, w_outer, member, after_row)
    columns = lax.all_to_all(
        after_row.reshape(q_size * b_size, 16, depth),
        ("x_hi", "z", "y", "x_lo"), 0, 0, tiled=True,
    )
    going, factor_b = col_attention(
        columns, member, chain_position_valid,
        vertical_entry_matrices, vertical_exit_matrix, dyadic_t, q_size, spread,
    )
    b_all = lax.all_gather(factor_b, ("y", "x_lo", "core"), axis=0)
    back = lax.all_to_all(going, ("x_hi", "z"), 0, 0, tiled=True)

    delta, a_all, bd = couple(back, w_outer, member, b_all)
    deltas = ring_halves(delta, "z", "x_hi")
    gb = grad_b_of(a_all, spread, [delta])
    gb = lax.all_to_all(
        gb.reshape(r_size, 4 * width, -1), ("y", "x_lo", "core"), 0, 0, tiled=True
    )
    ga = grad_a_of(bd, spread, [deltas[1], deltas[4], deltas[5]])
    couple_delta = assemble(deltas)
    factors = lax.all_to_all(pack_grads(ga, gb, q_size), ("x_hi", "z"), 0, 0, tiled=True)
    alignment_refreshed, cotangent = finish_home(
        factors, dyadic_t, back, member.reshape(q_size, seqs_here), chain_position_valid
    )
    return (alignment_refreshed, couple_delta, cotangent)


def solution(mesh):
    torus = jax.sharding.Mesh(
        mesh.devices.reshape(2, 4, 4, 2, 2), ("x_hi", "z", "y", "x_lo", "core")
    )
    seq, res = ("x_hi", "z"), ("y", "x_lo", "core")
    placed = (
        P(seq, res, None),
        P(res, None, None),
        P(),
        P(),
        P(),
        P(),
        P(),
        P(),
        P(),
        P(),
        P(),
        P(res, None, None),
    )
    return jax.shard_map(
        per_device,
        mesh=torus,
        in_specs=placed,
        out_specs=(P(seq, res, None), P(res, None, None), P(seq, res, None)),
        check_vma=False,
    )
```

```python
import functools

import jax
import jax.numpy as jnp
from jax import lax
from jax.experimental import pallas as pl
from jax.experimental.pallas import tpu as pltpu
from jax.sharding import PartitionSpec as P

FACTOR_WIDTH = 32
H = 8
HEAD_SIZE = 32
LOG2E = 1.4426950408889634
MASKED = -1000000000.0 * LOG2E
BF16 = jnp.bfloat16
F32 = jnp.float32
NT = (((1,), (1,)), ((), ()))
ROW_UNROLL = 1
COL_STEP = 64
PAIR_UNROLL = 2

VMEM = pl.BlockSpec(memory_space=pltpu.VMEM)
SMEM = pl.BlockSpec(memory_space=pltpu.SMEM)
ORDER = pl.BlockSpec(memory_space=pl.ANY)
ROOM = pltpu.CompilerParams(vmem_limit_bytes=56 * 1024 * 1024)


def lasting(microseconds):
    return pl.CostEstimate(
        flops=0, bytes_accessed=int(microseconds * 3.69e6), transcendentals=0
    )


def nn(left, right):
    return jnp.dot(left, right, preferred_element_type=F32)


def nt(left, right):
    return lax.dot_general(left, right, NT, preferred_element_type=F32)


def standardize(values):
    center = values - jnp.mean(values, -1, keepdims=True)
    spread = jnp.mean(center * center, -1, keepdims=True)
    return center * lax.rsqrt(spread + 1e-05)


def put(ref, rows, values):
    for half in range(2):
        ref[half, rows, :] = values[:, 128 * half : 128 * half + 128]


def take(ref, rows):
    return jnp.concatenate([ref[0, rows, :], ref[1, rows, :]], 1)


def column_of(row):
    return jnp.broadcast_to(row.astype(F32), (8, row.shape[1])).T[:, :1]


def seq_index():
    return lax.axis_index("x_hi"), lax.axis_index("z")


def res_index():
    return lax.axis_index("x_lo"), lax.axis_index("y")


def scale_of(member):
    return 1.0 / jnp.sum(member.astype(F32), keepdims=True)


def bias_kernel(pair_ref, proj_ref, valid_ref, out_ref, turn_s):
    at = pl.program_id(0)
    rows, residues, depth = pair_ref.shape
    line = lax.broadcasted_iota(jnp.int32, (depth, depth), 0)
    lane = lax.broadcasted_iota(jnp.int32, (depth, depth), 1)
    centering = (jnp.where(line == lane, 1.0, 0.0) - 1.0 / depth).astype(BF16)
    live = valid_ref[...] > 0
    proj = proj_ref[...].astype(F32).T
    blank = jnp.zeros_like(proj)
    mean = jnp.full_like(proj, 1.0 / depth)
    sides = jnp.concatenate(
        [jnp.concatenate([proj, blank], 1), jnp.concatenate([blank, mean], 1)], 0
    ).astype(BF16)
    center = nn(pair_ref[...].reshape(rows * residues, depth), centering)
    both = jnp.concatenate([center.astype(BF16), (center * center).astype(BF16)], 1)
    for one in range(rows):
        sums = nt(sides, both[one * residues : one * residues + residues])
        bias = sums[:H] * lax.rsqrt(sums[H:] + 1e-05) * LOG2E
        bias = jnp.where(live, bias, MASKED)
        here = pl.ds(pl.multiple_of((at * rows + one) * H, H), H)
        for part in range(residues // 128):
            turn_s[part, here, :] = bias[:, 128 * part : 128 * part + 128]

    @pl.when(at == pl.num_programs(0) - 1)
    def _():
        total = out_ref.shape[0] // H
        for head in range(H):
            for part in range(residues // 128):
                out_ref[total * head : total * head + total, 128 * part : 128 * part + 128] = (
                    turn_s[part, pl.ds(head, total, stride=H), :].astype(BF16)
                )


def pair_bias(pair, proj, valid):
    rows, residues, depth = pair.shape
    step = 4
    return pl.pallas_call(
        bias_kernel,
        grid=(rows // step,),
        in_specs=[
            pl.BlockSpec((step, residues, depth), lambda g: (g, 0, 0)),
            pl.BlockSpec((depth, H), lambda g: (0, 0)),
            pl.BlockSpec((1, residues), lambda g: (0, 0)),
        ],
        out_specs=pl.BlockSpec((rows * H, residues), lambda g: (0, 0)),
        out_shape=jax.ShapeDtypeStruct((rows * H, residues), BF16),
        scratch_shapes=[pltpu.VMEM((residues // 128, rows * H, 128), F32)],
        compiler_params=ROOM,
        cost_estimate=lasting(9),
        name="pair_bias",
    )(pair, proj, valid)


def scores_of(query, keys, side):
    lanes = slice(128 * side, 128 * side + 128)
    lane = lax.broadcasted_iota(jnp.int32, (1, 128), 1) // HEAD_SIZE
    part = query[:, lanes]
    spread = [jnp.where(lane == head, part, 0.0).astype(BF16) for head in range(4)]
    return nt(jnp.concatenate(spread, 0), keys[:, lanes])


def weigh(scores, values):
    rows = scores.shape[0] // 4
    lane = lax.broadcasted_iota(jnp.int32, (1, 128), 1) // HEAD_SIZE
    weights = jnp.exp2(scores - jnp.max(scores, -1, keepdims=True)).astype(BF16)
    both = nn(weights, values)
    summed, total = both[:rows, :128], both[:rows, 128:]
    for head in range(1, 4):
        here = slice(rows * head, rows * head + rows)
        summed = jnp.where(lane == head, both[here, :128], summed)
        total = jnp.where(lane == head, both[here, 128:], total)
    return summed / total


def entry_kernel(x_ref, other_ref, valid_ref, w_ref, q_ref, k_ref, v_ref, g_ref, live_s):
    blocks, seqs, rows, depth = x_ref.shape
    core = lax.axis_index("core")
    v_ref[:, :, :, 128:] = jnp.ones(v_ref.shape[:3] + (128,), BF16)
    live_s[...] = jnp.broadcast_to(column_of(valid_ref[...]), live_s.shape)
    for s in range(seqs):
        for other in range(2):
            source = other_ref if other else x_ref
            x = source[:, s].reshape(blocks * rows, depth)
            normed = standardize(x.astype(F32)).astype(BF16)
            pair = nn(normed, w_ref[:, depth : 3 * depth])
            side = 1 - core if other else core
            for at in range(blocks):
                here = slice(rows * at, rows * at + rows)
                to = pl.ds(pl.multiple_of((2 * at + side) * rows, rows), rows)
                k_ref[s, to, :] = (pair[here, :depth] * live_s[to, :1]).astype(BF16)
                for part in range(2):
                    lanes = slice(depth + 128 * part, depth + 128 * part + 128)
                    v_ref[s, part, to, :128] = pair[here, lanes].astype(BF16)
            if not other:
                query = nn(normed, w_ref[:, :depth]) * (HEAD_SIZE**-0.5 * LOG2E)
                q_ref[s] = query.astype(BF16)
                g_ref[s] = jax.nn.sigmoid(nn(normed, w_ref[:, 3 * depth :])).astype(BF16)


def row_entry(x, other, valid, w):
    blocks, seqs, rows, depth = x.shape
    here = jax.ShapeDtypeStruct((seqs, blocks * rows, depth), BF16)
    full = jax.ShapeDtypeStruct((seqs, 2 * blocks * rows, depth), BF16)
    sides = jax.ShapeDtypeStruct((seqs, 2, 2 * blocks * rows, 256), BF16)
    return pl.pallas_call(
        entry_kernel,
        in_specs=[VMEM] * 4,
        out_specs=[VMEM] * 4,
        out_shape=[here, full, sides, here],
        scratch_shapes=[pltpu.VMEM((2 * blocks * rows, 128), F32)],
        compiler_params=ROOM,
        cost_estimate=lasting(5),
        name="row_entry",
    )(x, other, valid, w)


def place(index, pieces, store):
    across, along = index
    for block, piece in enumerate(pieces):
        store((across ^ (block // 4)) * 4 + ((along + block) & 3), piece)


def place_halves(index, pieces, size, store):
    across, along = index
    pieces = list(pieces)
    for block in range(8):
        parts = 2 if block % 4 == 2 else 1
        for part in range(parts):
            at = (across ^ (block // 4)) * 4 + ((along + block) & 3)
            store(at, size // parts * part, size // parts, pieces.pop(0))


def row_kernel(steps, q_ref, k_ref, v_ref, g_ref, x_ref, wo_ref, *refs):
    count = len(steps)
    pieces, (out_ref, bias_s) = refs[:count], refs[-2:]
    blocks, seqs, rows, depth = x_ref.shape
    for at, piece in enumerate(pieces):
        bias_s[at] = piece[...]
    for before in refs[count:-2]:
        out_ref[...] = before[...]
    x_lo, y = res_index()

    upper = lax.broadcasted_iota(jnp.int32, (rows // 8, 8, depth), 1) < 4

    def block(step, carry):
        across, ahead = jnp.int32(0), jnp.int32(0)
        for one, (far_across, far_ahead) in enumerate(steps):
            across = jnp.where(step == one, far_across, across)
            ahead = jnp.where(step == one, far_ahead, ahead)
        at = ((y + ahead) & 3) * 2 + (x_lo ^ across)
        here = pl.ds(pl.multiple_of(at * rows, rows), rows)
        scores = {}
        for side in range(2):
            offset = bias_s[step, 4 * rows * side : 4 * rows * side + 4 * rows, :].astype(F32)
            for s in range(seqs):
                scores[s, side] = scores_of(q_ref[s, here, :], k_ref.at[s], side) + offset
        done = []
        for s in range(seqs):
            output = jnp.concatenate(
                [weigh(scores[s, side], v_ref[s, side]) for side in range(2)], 1
            )
            gated = (g_ref[s, here, :].astype(F32) * output).astype(BF16)
            after = x_ref[at, s].astype(F32) + nn(gated, wo_ref[...])
            done.append(after.reshape(rows // 8, 8, depth))
        even, odd = [], []
        for first, second in zip(done[::2], done[1::2]):
            even.append(jnp.where(upper, first, pltpu.roll(second, 4, 1)))
            odd.append(jnp.where(upper, pltpu.roll(first, 4, 1), second))
        even = jnp.concatenate(even, 1).astype(BF16)
        odd = jnp.concatenate(odd, 1).astype(BF16)
        for pair in range(rows // 8):
            out_ref[2 * pair, at] = even[pair]
            out_ref[2 * pair + 1, at] = odd[pair]
        return carry

    lax.fori_loop(0, count, block, 0, unroll=ROW_UNROLL)


def row_attention(steps, q, k, v, g, x, wo, bias, before=()):
    blocks, seqs, rows, depth = x.shape
    return pl.pallas_call(
        functools.partial(row_kernel, steps),
        in_specs=[VMEM] * (6 + len(bias) + len(before)),
        out_specs=VMEM,
        out_shape=jax.ShapeDtypeStruct((rows // 4, blocks, 4 * seqs, depth), BF16),
        scratch_shapes=[pltpu.VMEM((len(bias),) + bias[0].shape, BF16)],
        compiler_params=ROOM,
        cost_estimate=lasting(8),
        name="row_attention",
    )(q, k, v, g, x, wo, *bias, *before)


def col_kernel(
    y_ref, valid_ref, chain_ref, w_ref, wo_ref, dyadic_ref, _,
    out_ref, b_ref, y_s, q_s, k_s, v_s, g_s, o_s,
):
    tokens, depth = y_s.shape[1], 2 * y_s.shape[2]
    parts = q_s.shape[0]
    seqs = tokens // parts
    live = valid_ref[...].astype(F32)
    live_column = column_of(live)
    offset = jnp.where(live > 0, 0.0, MASKED)
    x_hi, z = seq_index()
    x_lo, y_at = res_index()
    first = ((y_at * 2 + x_lo) * 2 + lax.axis_index("core")) * 32 + (x_hi * 4 + z) * parts
    put(y_s, slice(None), y_ref[...].reshape(tokens, depth).astype(F32))
    for at in range(parts):
        y = take(y_s, pl.ds(at, seqs, stride=parts))
        mixed = nn(standardize(y).astype(BF16), w_ref[...])
        q_s[at] = mixed[:, :depth] * (HEAD_SIZE**-0.5 * LOG2E)
        k_s[at] = (mixed[:, depth : 2 * depth] * live_column).astype(BF16)
        for part in range(2):
            lanes = slice(2 * depth + 128 * part, 2 * depth + 128 * part + 128)
            v_s[at, part, :, :128] = mixed[:, lanes].astype(BF16)
        g_s[at] = jax.nn.sigmoid(mixed[:, 3 * depth :])
    step = COL_STEP
    v_s[:, :, :, 128:] = jnp.ones(v_s.shape[:3] + (128,), BF16)

    def block(part, carry):
        here = pl.ds(pl.multiple_of(part * step, step), step)
        scores = [
            [scores_of(q_s[at, here, :], k_s[at], side) + offset for side in range(2)]
            for at in range(parts)
        ]
        for at in range(parts):
            output = jnp.concatenate(
                [weigh(scores[at][side], v_s[at, side]) for side in range(2)], 1
            )
            o_s[at, here, :] = (g_s[at, here, :] * output).astype(BF16)
        return carry

    lax.fori_loop(0, seqs // step, block, 0)
    for at in range(parts):
        y = take(y_s, pl.ds(at, seqs, stride=parts))
        done = (y + nn(o_s[at], wo_ref[...])).astype(BF16)
        groups = out_ref.shape[0]
        here = slice(seqs // groups * at, seqs // groups * at + seqs // groups)
        out_ref[:, here, :] = done.reshape(groups, seqs // groups, depth)
        normed = standardize(done.astype(F32)).astype(BF16)
        factors = nt(dyadic_ref[...], normed) * (live * chain_ref[first + at].astype(F32))
        for group in range(groups):
            to = slice(128 + 32 * at, 160 + 32 * at)
            out_ref[group, to, :] = factors[:32].astype(BF16)
        b_ref[pl.ds(32 * at, 32), :] = factors[32:].astype(BF16)


def col_attention(y, valid, chain, w, wo, dyadic_t, groups, after):
    sources, eight, depth = y.shape
    tokens = sources * eight
    seqs = tokens // 4
    return pl.pallas_call(
        col_kernel,
        in_specs=[VMEM] * 2 + [SMEM] + [VMEM] * 3 + [ORDER],
        out_specs=[VMEM] * 2,
        out_shape=[
            jax.ShapeDtypeStruct((groups, 2 * 4 * FACTOR_WIDTH, seqs), BF16),
            jax.ShapeDtypeStruct((4 * FACTOR_WIDTH, seqs), BF16),
        ],
        scratch_shapes=[
            pltpu.VMEM((2, tokens, depth // 2), F32),
            pltpu.VMEM((4, seqs, depth), F32),
            pltpu.VMEM((4, seqs, depth), BF16),
            pltpu.VMEM((4, 2, seqs, 256), BF16),
            pltpu.VMEM((4, seqs, depth), F32),
            pltpu.VMEM((4, seqs, depth), BF16),
        ],
        compiler_params=ROOM,
        cost_estimate=lasting(8),
        name="col_attention",
    )(y, valid, chain, w, wo, dyadic_t, after)


def assemble_kernel(*refs):
    pieces, (out_ref, d_s) = refs[:10], refs[10:]
    step = out_ref.shape[0]
    at = pl.program_id(0)

    def store(block, start, size, piece):
        d_s[block, start : start + size] = piece[...]

    @pl.when(at == 0)
    def _():
        place_halves(seq_index(), pieces, d_s.shape[1], store)

    upper = lax.broadcasted_iota(jnp.int32, (8, 8, 128), 1) < 4

    def line(one, carry):
        even, odd = [], []
        for pair in range(4):
            first = d_s[2 * pair, at * step + one].astype(F32).reshape(8, 8, 128)
            second = d_s[2 * pair + 1, at * step + one].astype(F32).reshape(8, 8, 128)
            even.append(jnp.where(upper, first, pltpu.roll(second, 4, 1)))
            odd.append(jnp.where(upper, pltpu.roll(first, 4, 1), second))
        both = jnp.stack([jnp.stack(even, 1), jnp.stack(odd, 1)], 1)
        out_ref[one] = both.reshape(512, 128).astype(BF16)
        return carry

    lax.fori_loop(0, step, line, 0, unroll=2)


def assemble(pieces):
    rows, columns, depth = pieces[0].shape
    step = 8
    return pl.pallas_call(
        assemble_kernel,
        grid=(rows // step,),
        in_specs=[VMEM] * len(pieces),
        out_specs=pl.BlockSpec((step, 8 * columns, depth), lambda g: (g, 0, 0)),
        out_shape=jax.ShapeDtypeStruct((rows, 8 * columns, depth), BF16),
        scratch_shapes=[pltpu.VMEM((8, rows, columns, depth), BF16)],
        compiler_params=ROOM,
        cost_estimate=lasting(5),
        name="assemble",
    )(*pieces)


def spread_kernel(g_ref, w_ref, member_ref, _, out_ref):
    width = FACTOR_WIDTH
    scale = scale_of(member_ref[...])
    blank = jnp.zeros((64, 128), BF16)

    def pair(at, carry):
        parts = []
        for one in range(2):
            given = g_ref[2 * at + one]
            parts.append(jnp.concatenate([given, blank], 1))
            parts.append(jnp.concatenate([blank, given], 1))
        both = (nt(w_ref[...], jnp.concatenate(parts, 0)) * scale).astype(BF16)
        for one in range(2):
            here = pl.ds(pl.multiple_of((2 * at + one) * width, width), width)
            out_ref[here, :] = jnp.concatenate(
                [
                    both[width * e : width * e + width, 128 * one : 128 * one + 128]
                    for e in range(16)
                ],
                1,
            )
        return carry

    lax.fori_loop(0, g_ref.shape[0] // 2, pair, 0)


def spread_of(given, w, member, after):
    rows, columns, _ = given.shape
    return pl.pallas_call(
        spread_kernel,
        in_specs=[VMEM] * 3 + [ORDER],
        out_specs=VMEM,
        out_shape=jax.ShapeDtypeStruct((rows * FACTOR_WIDTH, columns * FACTOR_WIDTH), BF16),
        compiler_params=ROOM,
        cost_estimate=lasting(8),
        name="spread",
    )(given, w, member, after)


def couple_kernel(both_ref, w_ref, member_ref, *refs):
    b_pieces, (out_ref, a_ref, bd_ref, o_s, b_s) = refs[:-5], refs[-5:]
    width = FACTOR_WIDTH
    rows, columns = o_s.shape
    core = lax.axis_index("core")
    x_lo, y = res_index()
    near, far = (0, 1, 3, 4), (2, 5, 6, 7)
    for other in range(2):
        for part, piece in zip((near, far), b_pieces[2 * other : 2 * other + 2]):
            for at, block in enumerate(part):
                to = ((y + block) & 3) * 2 + (x_lo ^ (block // 4))
                to = pl.multiple_of((to * 2 + (core ^ other)) * 128, 128)
                put(b_s, pl.ds(to, 128), piece[128 * at : 128 * at + 128, :].astype(F32))
    count = columns // width
    for at in range(width):
        here = slice(at * count, at * count + count)
        bd_ref[here, :] = take(b_s, pl.ds(at, count, stride=width)).astype(BF16)
    a_ref[...] = both_ref[:, 128:].reshape(a_ref.shape)
    for at in range(columns // 256):
        here = slice(256 * at, 256 * at + 256)
        o_s[:, here] = nt(a_ref[...], bd_ref[here, :]).astype(BF16)
    scale = scale_of(member_ref[...])
    w = w_ref[...].astype(F32).T.astype(BF16)
    low = lax.broadcasted_iota(jnp.int32, (128, 128), 1) < 64

    def pair(at, carry):
        outer = o_s[pl.ds(pl.multiple_of(at * 2 * width, 2 * width), 2 * width), :]
        stacks = []
        for one in range(2):
            part = outer[width * one : width * one + width]
            stacks.append(
                jnp.concatenate([part[:, 128 * e : 128 * e + 128] for e in range(16)], 0)
            )
        both = nn(w, jnp.concatenate(stacks, 1))
        top = jnp.where(low, both[:128, :128], pltpu.roll(both[:128, 128:], 64, 1))
        bottom = jnp.where(low, pltpu.roll(both[128:, :128], 64, 1), both[128:, 128:])
        delta = ((top + bottom) * scale).T
        out_ref[pl.ds(at * 2, 2)] = delta.reshape(2, 64, 128).astype(BF16)
        return carry

    lax.fori_loop(0, rows // (2 * width), pair, 0, unroll=PAIR_UNROLL)


def couple(both, w, member, b_pieces):
    seqs = both.shape[2]
    rows, columns = both.shape[0] * 128, 4 * b_pieces[0].shape[0]
    return pl.pallas_call(
        couple_kernel,
        in_specs=[VMEM] * 7,
        out_specs=[VMEM] * 3,
        out_shape=[
            jax.ShapeDtypeStruct((rows // FACTOR_WIDTH, columns // FACTOR_WIDTH, 128), BF16),
            jax.ShapeDtypeStruct((rows, seqs), BF16),
            jax.ShapeDtypeStruct((columns, seqs), BF16),
        ],
        scratch_shapes=[
            pltpu.VMEM((rows, columns), BF16),
            pltpu.VMEM((2, columns, seqs // 2), F32),
        ],
        compiler_params=ROOM,
        cost_estimate=lasting(9),
        name="couple",
    )(both, w, member, *b_pieces)


def grads_kernel(a_ref, bd_ref, s_ref, _, ga_ref, own_ref, other_ref, turned_s):
    width = FACTOR_WIDTH
    blocks = own_ref.shape[0]
    columns = turned_s.shape[1] // width
    core = lax.axis_index("core")
    left = a_ref[...].astype(F32).T.astype(BF16)
    for at in range(columns * width // 256):
        here = slice(256 * at, 256 * at + 256)
        put(turned_s, here, nn(left, s_ref[:, here]).T)
    for other, out_ref in ((1, other_ref), (0, own_ref)):
        for block in range(blocks):
            for part in range(4):
                column = (2 * block + (core ^ other)) * 4 + part
                lines = take(turned_s, pl.ds(column, width, stride=columns))
                out_ref[block, width * part : width * part + width, :] = lines.astype(BF16)
    for at in range(4):
        here = slice(256 * at, 256 * at + 256)
        ga_ref[:, here] = nn(s_ref[here, :], bd_ref[...]).T.astype(BF16)


def factor_grads(a_all, bd, spread, after):
    seqs, columns = a_all.shape[1], spread.shape[1]
    shape = jax.ShapeDtypeStruct((columns // 256, 128, seqs), BF16)
    return pl.pallas_call(
        grads_kernel,
        in_specs=[VMEM] * 3 + [ORDER],
        out_specs=[VMEM] * 3,
        out_shape=[jax.ShapeDtypeStruct((seqs, spread.shape[0]), BF16), shape, shape],
        scratch_shapes=[pltpu.VMEM((2, columns, seqs // 2), F32)],
        compiler_params=ROOM,
        cost_estimate=lasting(10),
        name="factor_grads",
    )(a_all, bd, spread, after)


def fold_kernel(own_ref, other_ref, *refs):
    refs[-1][...] = (own_ref[...].astype(F32) + other_ref[...].astype(F32)).astype(BF16)


def fold(own, other, after):
    return pl.pallas_call(
        fold_kernel,
        in_specs=[VMEM] * 2 + [ORDER] * len(after),
        out_specs=VMEM,
        out_shape=jax.ShapeDtypeStruct(own.shape, BF16),
        compiler_params=ROOM,
        cost_estimate=lasting(1),
        name="fold",
    )(own, other, *after)


def pack_kernel(ga_ref, gb_ref, out_ref):
    groups, members, _ = out_ref.shape
    wide = ga_ref.shape[1]
    total = gb_ref[0].astype(F32)
    for at in range(1, gb_ref.shape[0]):
        total = total + gb_ref[at].astype(F32)
    out_ref[:, :, :wide] = ga_ref[...].reshape(groups, members, wide)
    out_ref[:, :, wide:] = total.T.reshape(groups, members, total.shape[0]).astype(BF16)


def pack_grads(ga, gb, groups):
    seqs, wide = ga.shape
    return pl.pallas_call(
        pack_kernel,
        in_specs=[VMEM] * 2,
        out_specs=VMEM,
        out_shape=jax.ShapeDtypeStruct((groups, seqs // groups, wide + gb.shape[1]), BF16),
        compiler_params=ROOM,
        cost_estimate=lasting(3),
        name="pack_grads",
    )(ga, gb)


def home_kernel(gf_ref, w_ref, x_ref, member_ref, chain_ref, x_out_ref, ct_ref, x_s, ct_s):
    width = FACTOR_WIDTH
    groups, rows, depth = x_ref.shape
    parts = 4
    seqs = rows // 2 // parts
    residues = groups * parts
    wide = residues * width
    x_hi, z = seq_index()
    x_lo, y = res_index()
    first = ((y * 2 + x_lo) * 2 + lax.axis_index("core")) * residues
    member = member_ref[pl.ds(x_hi * 4 + z, 1), :]
    member = jnp.broadcast_to(member.astype(F32), (8, member.shape[1])).T[:seqs, :1]
    total = gf_ref[0, :, :wide].astype(F32)
    for at in range(1, groups):
        total = total + gf_ref[at, :, :wide].astype(F32)
    lane = lax.broadcasted_iota(jnp.int32, (1, 128), 1) // width
    lines = []
    for group in range(groups):
        live = jnp.zeros((1, 128), F32)
        for at in range(parts):
            here = chain_ref[first + group * parts + at].astype(F32)
            live = jnp.where(lane == at, here, live)
        live = live * member
        left = total[:, 128 * group : 128 * group + 128] * live
        right = gf_ref[group, :, wide:].astype(F32) * live
        lines.append(jnp.concatenate([left, right], 1))
    given = jnp.concatenate(lines, 0)
    lane = lax.broadcasted_iota(jnp.int32, (1, depth), 1) // width % parts
    back = jnp.concatenate([w_ref[:width, :]] * parts + [w_ref[width:, :]] * parts, 0)
    for at in range(parts):
        upstream = nn(jnp.where(lane == at, given, 0.0).astype(BF16), back)
        x = x_ref[:, seqs * at : seqs * at + seqs]
        x = x.reshape(groups * seqs, depth).astype(F32)
        center = x - jnp.mean(x, -1, keepdims=True)
        inverse = lax.rsqrt(jnp.mean(center * center, -1, keepdims=True) + 1e-05)
        scaled = center * inverse
        cotangent = inverse * (
            upstream
            - jnp.mean(upstream, -1, keepdims=True)
            - scaled * jnp.mean(upstream * scaled, -1, keepdims=True)
        )
        for group in range(groups):
            here = pl.ds(group * parts + at, seqs, stride=residues)
            put(x_s, here, x[group * seqs : group * seqs + seqs])
            put(ct_s, here, cotangent[group * seqs : group * seqs + seqs])
    x_out_ref[...] = take(x_s, slice(None)).reshape(seqs, residues, depth).astype(BF16)
    ct_ref[...] = take(ct_s, slice(None)).reshape(seqs, residues, depth).astype(BF16)


def finish_home(gf, w, both, member, chain):
    groups, rows, depth = both.shape
    seqs, residues = rows // 8, groups * 4
    shape = (seqs, residues, depth)
    return pl.pallas_call(
        home_kernel,
        in_specs=[VMEM] * 4 + [SMEM],
        out_specs=[VMEM] * 2,
        out_shape=[jax.ShapeDtypeStruct(shape, BF16)] * 2,
        scratch_shapes=[pltpu.VMEM((2, seqs * residues, depth // 2), F32)] * 2,
        compiler_params=ROOM,
        cost_estimate=lasting(6),
        name="finish_home",
    )(gf, w, both, member, chain)


def hold_kernel(*refs):
    pass


def hold(arrays, after):
    count = len(arrays)
    return pl.pallas_call(
        hold_kernel,
        in_specs=[ORDER] * (count + 1),
        out_specs=[ORDER] * count,
        out_shape=[jax.ShapeDtypeStruct(one.shape, one.dtype) for one in arrays],
        input_output_aliases={at: at for at in range(count)},
        cost_estimate=lasting(0.1),
        name="hold",
    )(*arrays, after)


def turn_by(steps):
    return [(at, (at + steps) % 4) for at in range(4)]


SWAP = [(0, 1), (1, 0)]


def ring(x, along, across, after=None):
    partner = lax.ppermute(x, across, SWAP)
    below = lax.ppermute(x, along, turn_by(1))
    above = lax.ppermute(x, along, turn_by(3))
    far = lax.ppermute(x, along, turn_by(2))
    if after is not None:
        partner, far = hold([partner, far], after)
    partner_below = lax.ppermute(partner, along, turn_by(1))
    partner_above = lax.ppermute(partner, along, turn_by(3))
    partner_far = lax.ppermute(far, across, SWAP)
    return [x, above, far, below, partner, partner_above, partner_far, partner_below]


def ring_halves(x, along, across):
    half = x.shape[0] // 2
    partner = lax.ppermute(x, across, SWAP)
    below = lax.ppermute(x, along, turn_by(1))
    above = lax.ppermute(x, along, turn_by(3))
    far_low = lax.ppermute(below[:half], along, turn_by(1))
    far_high = lax.ppermute(above[half:], along, turn_by(3))
    partner_below = lax.ppermute(partner, along, turn_by(1))
    partner_above = lax.ppermute(partner, along, turn_by(3))
    partner_low = lax.ppermute(far_low, across, SWAP)
    partner_high = lax.ppermute(far_high, across, SWAP)
    return [
        x, above, far_low, far_high, below,
        partner, partner_above, partner_low, partner_high, partner_below,
    ]


def per_device(
    multiple_alignment_rep,
    pair_rep,
    aligned_member_valid,
    chain_position_valid,
    horizontal_entry_matrices,
    horizontal_exit_matrix,
    bias_proj,
    vertical_entry_matrices,
    vertical_exit_matrix,
    dyadic_projection_matrices,
    outer_out,
    pair_grad,
):
    seqs_here, res_here, depth = multiple_alignment_rep.shape
    residues = pair_rep.shape[1]
    pair_width = outer_out.shape[1]
    q_size, b_size, r_size = 8, 8, 16
    width = FACTOR_WIDTH
    q_at = lax.axis_index("x_hi") * 4 + lax.axis_index("z")
    member = aligned_member_valid.reshape(1, -1)
    chain_row = chain_position_valid.reshape(1, residues)

    dyadic_t = dyadic_projection_matrices.T
    cube = outer_out.reshape(width, width // 2, 2, pair_width)
    w_outer = cube.transpose(1, 0, 2, 3).reshape(16 * width, 2 * pair_width)
    grad_here = lax.dynamic_index_in_dim(
        pair_grad.reshape(res_here, r_size, q_size, 4, pair_width), q_at, 2, keepdims=False
    ).reshape(res_here, r_size * 4, pair_width)

    bias = pair_bias(pair_rep, bias_proj, chain_row)
    x_rows = lax.all_to_all(
        multiple_alignment_rep.reshape(b_size, seqs_here // b_size, res_here, depth),
        ("y", "x_lo"), 0, 0, tiled=True,
    )
    (x_rows,) = hold([x_rows], bias)
    x_other = lax.ppermute(x_rows, "core", SWAP)
    q, k, v, g = row_entry(x_rows, x_other, chain_row, horizontal_entry_matrices)
    bias_pieces = ring(bias, "y", "x_lo", after=q)
    near, far = (0, 1, 3, 4), (2, 5, 6, 7)
    after_row = ()
    for part in (near, far):
        after_row = row_attention(
            [(at // 4, at % 4) for at in part], q, k, v, g, x_rows, horizontal_exit_matrix,
            [bias_pieces[at] for at in part], after_row,
        )
        after_row = [after_row]
    (after_row,) = after_row

    spread = spread_of(grad_here, w_outer, member, after_row)
    columns = lax.all_to_all(
        after_row.reshape(q_size * b_size, 16, depth),
        ("x_hi", "z", "y", "x_lo"), 0, 0, tiled=True,
    )
    going, factor_b = col_attention(
        columns, member, chain_position_valid,
        vertical_entry_matrices, vertical_exit_matrix, dyadic_t, q_size, spread,
    )
    b_ring = ring(factor_b, "y", "x_lo")
    b_pieces = [jnp.concatenate([b_ring[at] for at in part], 0) for part in (near, far)]
    b_pieces += [lax.ppermute(piece, "core", SWAP) for piece in b_pieces]
    back = lax.all_to_all(going, ("x_hi", "z"), 0, 0, tiled=True)

    delta, a_all, bd = couple(back, w_outer, member, b_pieces)
    deltas = ring_halves(delta, "z", "x_hi")
    ga, gb, gb_other = factor_grads(a_all, bd, spread, delta)
    gb_other = lax.ppermute(gb_other, "core", SWAP)
    gb = fold(gb, gb_other, [deltas[1], deltas[4], deltas[5]])
    gb = lax.all_to_all(gb, ("y", "x_lo"), 0, 0, tiled=True)
    couple_delta = assemble(deltas)
    factors = lax.all_to_all(pack_grads(ga, gb, q_size), ("x_hi", "z"), 0, 0, tiled=True)
    alignment_refreshed, cotangent = finish_home(
        factors, dyadic_t, back, member.reshape(q_size, seqs_here), chain_position_valid
    )
    return (alignment_refreshed, couple_delta, cotangent)


def solution(mesh):
    torus = jax.sharding.Mesh(
        mesh.devices.reshape(2, 4, 4, 2, 2), ("x_hi", "z", "y", "x_lo", "core")
    )
    seq, res = ("x_hi", "z"), ("y", "x_lo", "core")
    placed = (
        P(seq, res, None),
        P(res, None, None),
        P(),
        P(),
        P(),
        P(),
        P(),
        P(),
        P(),
        P(),
        P(),
        P(res, None, None),
    )
    return jax.shard_map(
        per_device,
        mesh=torus,
        in_specs=placed,
        out_specs=(P(seq, res, None), P(res, None, None), P(seq, res, None)),
        check_vma=False,
    )
```

```python
import functools

import jax
import jax.numpy as jnp
from jax import lax
from jax.experimental import pallas as pl
from jax.experimental.pallas import tpu as pltpu
from jax.sharding import PartitionSpec as P

FACTOR_WIDTH = 32
H = 8
HEAD_SIZE = 32
LOG2E = 1.4426950408889634
MASKED = -1000000000.0 * LOG2E
BF16 = jnp.bfloat16
F32 = jnp.float32
NT = (((1,), (1,)), ((), ()))
COL_STEP = 128
ROW_UNROLL = 4
PAIR_UNROLL = 8
BIAS_STEP = 8
ASSEMBLE_STEP = 8

VMEM = pl.BlockSpec(memory_space=pltpu.VMEM)
SMEM = pl.BlockSpec(memory_space=pltpu.SMEM)
ORDER = pl.BlockSpec(memory_space=pl.ANY)
ROOM = pltpu.CompilerParams(vmem_limit_bytes=56 * 1024 * 1024)


def lasting(microseconds):
    return pl.CostEstimate(
        flops=0, bytes_accessed=int(microseconds * 3.69e6), transcendentals=0
    )


def nn(left, right):
    return jnp.dot(left, right, preferred_element_type=F32)


def nt(left, right):
    return lax.dot_general(left, right, NT, preferred_element_type=F32)


def standardize(values):
    center = values - jnp.mean(values, -1, keepdims=True)
    spread = jnp.mean(center * center, -1, keepdims=True)
    return center * lax.rsqrt(spread + 1e-05)


def put(ref, rows, values):
    for half in range(2):
        ref[half, rows, :] = values[:, 128 * half : 128 * half + 128]


def take(ref, rows):
    return jnp.concatenate([ref[0, rows, :], ref[1, rows, :]], 1)


def column_of(row):
    return jnp.broadcast_to(row.astype(F32), (8, row.shape[1])).T[:, :1]


def seq_index():
    return lax.axis_index("x_hi"), lax.axis_index("z")


def res_index():
    return lax.axis_index("x_lo"), lax.axis_index("y")


def scale_of(member):
    return 1.0 / jnp.sum(member.astype(F32), keepdims=True)


def bias_kernel(pair_ref, proj_ref, valid_ref, out_ref, turn_s):
    at = pl.program_id(0)
    rows, residues, depth = pair_ref.shape
    line = lax.broadcasted_iota(jnp.int32, (depth, depth), 0)
    lane = lax.broadcasted_iota(jnp.int32, (depth, depth), 1)
    centering = (jnp.where(line == lane, 1.0, 0.0) - 1.0 / depth).astype(BF16)
    live = valid_ref[...] > 0
    proj = proj_ref[...].astype(F32).T
    blank = jnp.zeros_like(proj)
    mean = jnp.full_like(proj, 1.0 / depth)
    sides = jnp.concatenate(
        [jnp.concatenate([proj, blank], 1), jnp.concatenate([blank, mean], 1)], 0
    ).astype(BF16)
    center = nn(pair_ref[...].reshape(rows * residues, depth), centering)
    both = jnp.concatenate([center.astype(BF16), (center * center).astype(BF16)], 1)
    for one in range(rows):
        sums = nt(sides, both[one * residues : one * residues + residues])
        bias = sums[:H] * lax.rsqrt(sums[H:] + 1e-05) * LOG2E
        bias = jnp.where(live, bias, MASKED)
        here = pl.ds(pl.multiple_of((at * rows + one) * H, H), H)
        for part in range(residues // 128):
            turn_s[part, here, :] = bias[:, 128 * part : 128 * part + 128]

    @pl.when(at == pl.num_programs(0) - 1)
    def _():
        total = out_ref.shape[0] // H
        for head in range(H):
            for part in range(residues // 128):
                out_ref[total * head : total * head + total, 128 * part : 128 * part + 128] = (
                    turn_s[part, pl.ds(head, total, stride=H), :].astype(BF16)
                )


def pair_bias(pair, proj, valid):
    rows, residues, depth = pair.shape
    step = BIAS_STEP
    return pl.pallas_call(
        bias_kernel,
        grid=(rows // step,),
        in_specs=[
            pl.BlockSpec((step, residues, depth), lambda g: (g, 0, 0)),
            pl.BlockSpec((depth, H), lambda g: (0, 0)),
            pl.BlockSpec((1, residues), lambda g: (0, 0)),
        ],
        out_specs=pl.BlockSpec((rows * H, residues), lambda g: (0, 0)),
        out_shape=jax.ShapeDtypeStruct((rows * H, residues), BF16),
        scratch_shapes=[pltpu.VMEM((residues // 128, rows * H, 128), F32)],
        compiler_params=ROOM,
        cost_estimate=lasting(9),
        name="pair_bias",
    )(pair, proj, valid)


def scores_of(query, keys, side):
    lanes = slice(128 * side, 128 * side + 128)
    lane = lax.broadcasted_iota(jnp.int32, (1, 128), 1) // HEAD_SIZE
    part = query[:, lanes]
    spread = [jnp.where(lane == head, part, 0.0).astype(BF16) for head in range(4)]
    return nt(jnp.concatenate(spread, 0), keys[:, lanes])


def weigh(scores, values):
    rows = scores.shape[0] // 4
    lane = lax.broadcasted_iota(jnp.int32, (1, 128), 1) // HEAD_SIZE
    weights = jnp.exp2(scores - jnp.max(scores, -1, keepdims=True)).astype(BF16)
    both = nn(weights, values)
    summed, total = both[:rows, :128], both[:rows, 128:]
    for head in range(1, 4):
        here = slice(rows * head, rows * head + rows)
        summed = jnp.where(lane == head, both[here, :128], summed)
        total = jnp.where(lane == head, both[here, 128:], total)
    return summed / total


def entry_kernel(x_ref, other_ref, valid_ref, w_ref, q_ref, k_ref, v_ref, g_ref, live_s):
    blocks, seqs, rows, depth = x_ref.shape
    core = lax.axis_index("core")
    v_ref[:, :, :, 128:] = jnp.ones(v_ref.shape[:3] + (128,), BF16)
    live_s[...] = jnp.broadcast_to(column_of(valid_ref[...]), live_s.shape)
    for s in range(seqs):
        for other in range(2):
            source = other_ref if other else x_ref
            x = source[:, s].reshape(blocks * rows, depth)
            normed = standardize(x.astype(F32)).astype(BF16)
            pair = nn(normed, w_ref[:, depth : 3 * depth])
            side = 1 - core if other else core
            for at in range(blocks):
                here = slice(rows * at, rows * at + rows)
                to = pl.ds(pl.multiple_of((2 * at + side) * rows, rows), rows)
                k_ref[s, to, :] = (pair[here, :depth] * live_s[to, :1]).astype(BF16)
                for part in range(2):
                    lanes = slice(depth + 128 * part, depth + 128 * part + 128)
                    v_ref[s, part, to, :128] = pair[here, lanes].astype(BF16)
            if not other:
                query = nn(normed, w_ref[:, :depth]) * (HEAD_SIZE**-0.5 * LOG2E)
                q_ref[s] = query.astype(BF16)
                g_ref[s] = jax.nn.sigmoid(nn(normed, w_ref[:, 3 * depth :])).astype(BF16)


def row_entry(x, other, valid, w):
    blocks, seqs, rows, depth = x.shape
    here = jax.ShapeDtypeStruct((seqs, blocks * rows, depth), BF16)
    full = jax.ShapeDtypeStruct((seqs, 2 * blocks * rows, depth), BF16)
    sides = jax.ShapeDtypeStruct((seqs, 2, 2 * blocks * rows, 256), BF16)
    return pl.pallas_call(
        entry_kernel,
        in_specs=[VMEM] * 4,
        out_specs=[VMEM] * 4,
        out_shape=[here, full, sides, here],
        scratch_shapes=[pltpu.VMEM((2 * blocks * rows, 128), F32)],
        compiler_params=ROOM,
        cost_estimate=lasting(5),
        name="row_entry",
    )(x, other, valid, w)


def place(index, pieces, store):
    across, along = index
    for block, piece in enumerate(pieces):
        store((across ^ (block // 4)) * 4 + ((along + block) & 3), piece)


def place_halves(index, pieces, size, store):
    across, along = index
    pieces = list(pieces)
    for block in range(8):
        parts = 2 if block % 4 == 2 else 1
        for part in range(parts):
            at = (across ^ (block // 4)) * 4 + ((along + block) & 3)
            store(at, size // parts * part, size // parts, pieces.pop(0))


def row_kernel(steps, q_ref, k_ref, v_ref, g_ref, x_ref, wo_ref, *refs):
    count = len(steps)
    pieces, (out_ref, bias_s, after_s) = refs[:count], refs[-3:]
    blocks, seqs, rows, depth = x_ref.shape
    lines = count * rows
    for at, piece in enumerate(pieces):
        for head in range(H):
            to = lines * head + rows * at
            bias_s[to : to + rows, :] = piece[rows * head : rows * head + rows, :]
    for before in refs[count:-3]:
        out_ref[...] = before[...]
    x_lo, y = res_index()
    at_blocks = [((y + ahead) & 3) * 2 + (x_lo ^ across) for across, ahead in steps]
    spots = [pl.ds(pl.multiple_of(at * rows, rows), rows) for at in at_blocks]

    def sequence(s, carry):
        query = jnp.concatenate([q_ref[s, spot, :] for spot in spots], 0)
        gate = jnp.concatenate([g_ref[s, spot, :] for spot in spots], 0)
        x = jnp.concatenate([x_ref[at, s] for at in at_blocks], 0)
        sides = []
        for side in range(2):
            offset = bias_s[4 * lines * side : 4 * lines * side + 4 * lines, :].astype(F32)
            sides.append(scores_of(query, k_ref.at[s], side) + offset)
        output = jnp.concatenate([weigh(sides[side], v_ref[s, side]) for side in range(2)], 1)
        gated = (gate.astype(F32) * output).astype(BF16)
        after_s[s] = x.astype(F32) + nn(gated, wo_ref[...])
        return carry

    lax.fori_loop(0, seqs, sequence, 0, unroll=ROW_UNROLL)
    upper = lax.broadcasted_iota(jnp.int32, (rows // 8, 8, depth), 1) < 4
    for at, block in enumerate(at_blocks):
        even, odd = [], []
        for pair in range(seqs // 2):
            first, second = (
                after_s[one, rows * at : rows * at + rows, :].reshape(rows // 8, 8, depth)
                for one in (2 * pair, 2 * pair + 1)
            )
            even.append(jnp.where(upper, first, pltpu.roll(second, 4, 1)))
            odd.append(jnp.where(upper, pltpu.roll(first, 4, 1), second))
        even = jnp.concatenate(even, 1).astype(BF16)
        odd = jnp.concatenate(odd, 1).astype(BF16)
        for pair in range(rows // 8):
            out_ref[2 * pair, block] = even[pair]
            out_ref[2 * pair + 1, block] = odd[pair]


def row_attention(steps, q, k, v, g, x, wo, bias, before=()):
    blocks, seqs, rows, depth = x.shape
    return pl.pallas_call(
        functools.partial(row_kernel, steps),
        in_specs=[VMEM] * (6 + len(bias) + len(before)),
        out_specs=VMEM,
        out_shape=jax.ShapeDtypeStruct((rows // 4, blocks, 4 * seqs, depth), BF16),
        scratch_shapes=[
            pltpu.VMEM((len(bias) * bias[0].shape[0], bias[0].shape[1]), BF16),
            pltpu.VMEM((seqs, len(bias) * rows, depth), F32),
        ],
        compiler_params=ROOM,
        cost_estimate=lasting(8),
        name="row_attention",
    )(q, k, v, g, x, wo, *bias, *before)


def col_kernel(
    y_ref, valid_ref, chain_ref, w_ref, wo_ref, dyadic_ref, _,
    out_ref, b_ref, y_s, q_s, k_s, v_s, g_s, o_s,
):
    tokens, depth = y_s.shape[1], 2 * y_s.shape[2]
    parts = q_s.shape[0]
    seqs = tokens // parts
    live = valid_ref[...].astype(F32)
    live_column = column_of(live)
    offset = jnp.where(live > 0, 0.0, MASKED)
    x_hi, z = seq_index()
    x_lo, y_at = res_index()
    first = ((y_at * 2 + x_lo) * 2 + lax.axis_index("core")) * 32 + (x_hi * 4 + z) * parts
    put(y_s, slice(None), y_ref[...].reshape(tokens, depth).astype(F32))
    for at in range(parts):
        y = take(y_s, pl.ds(at, seqs, stride=parts))
        mixed = nn(standardize(y).astype(BF16), w_ref[...])
        q_s[at] = mixed[:, :depth] * (HEAD_SIZE**-0.5 * LOG2E)
        k_s[at] = (mixed[:, depth : 2 * depth] * live_column).astype(BF16)
        for part in range(2):
            lanes = slice(2 * depth + 128 * part, 2 * depth + 128 * part + 128)
            v_s[at, part, :, :128] = mixed[:, lanes].astype(BF16)
        g_s[at] = jax.nn.sigmoid(mixed[:, 3 * depth :])
    step = COL_STEP
    v_s[:, :, :, 128:] = jnp.ones(v_s.shape[:3] + (128,), BF16)

    def block(part, carry):
        here = pl.ds(pl.multiple_of(part * step, step), step)
        scores = [
            [scores_of(q_s[at, here, :], k_s[at], side) + offset for side in range(2)]
            for at in range(parts)
        ]
        for at in range(parts):
            output = jnp.concatenate(
                [weigh(scores[at][side], v_s[at, side]) for side in range(2)], 1
            )
            o_s[at, here, :] = (g_s[at, here, :] * output).astype(BF16)
        return carry

    lax.fori_loop(0, seqs // step, block, 0)
    for at in range(parts):
        y = take(y_s, pl.ds(at, seqs, stride=parts))
        done = (y + nn(o_s[at], wo_ref[...])).astype(BF16)
        groups = out_ref.shape[0]
        here = slice(seqs // groups * at, seqs // groups * at + seqs // groups)
        out_ref[:, here, :] = done.reshape(groups, seqs // groups, depth)
        normed = standardize(done.astype(F32)).astype(BF16)
        factors = nt(dyadic_ref[...], normed) * (live * chain_ref[first + at].astype(F32))
        for group in range(groups):
            to = slice(128 + 32 * at, 160 + 32 * at)
            out_ref[group, to, :] = factors[:32].astype(BF16)
        b_ref[pl.ds(32 * at, 32), :] = factors[32:].astype(BF16)


def col_attention(y, valid, chain, w, wo, dyadic_t, groups, after):
    sources, eight, depth = y.shape
    tokens = sources * eight
    seqs = tokens // 4
    return pl.pallas_call(
        col_kernel,
        in_specs=[VMEM] * 2 + [SMEM] + [VMEM] * 3 + [ORDER],
        out_specs=[VMEM] * 2,
        out_shape=[
            jax.ShapeDtypeStruct((groups, 2 * 4 * FACTOR_WIDTH, seqs), BF16),
            jax.ShapeDtypeStruct((4 * FACTOR_WIDTH, seqs), BF16),
        ],
        scratch_shapes=[
            pltpu.VMEM((2, tokens, depth // 2), F32),
            pltpu.VMEM((4, seqs, depth), F32),
            pltpu.VMEM((4, seqs, depth), BF16),
            pltpu.VMEM((4, 2, seqs, 256), BF16),
            pltpu.VMEM((4, seqs, depth), F32),
            pltpu.VMEM((4, seqs, depth), BF16),
        ],
        compiler_params=ROOM,
        cost_estimate=lasting(8),
        name="col_attention",
    )(y, valid, chain, w, wo, dyadic_t, after)


def assemble_kernel(*refs):
    pieces, (out_ref, d_s) = refs[:10], refs[10:]
    step = out_ref.shape[0]
    at = pl.program_id(0)

    def store(block, start, size, piece):
        d_s[block, start : start + size] = piece[...]

    @pl.when(at == 0)
    def _():
        place_halves(seq_index(), pieces, d_s.shape[1], store)

    upper = lax.broadcasted_iota(jnp.int32, (8, 8, 128), 1) < 4

    def line(one, carry):
        even, odd = [], []
        for pair in range(4):
            first = d_s[2 * pair, at * step + one].astype(F32).reshape(8, 8, 128)
            second = d_s[2 * pair + 1, at * step + one].astype(F32).reshape(8, 8, 128)
            even.append(jnp.where(upper, first, pltpu.roll(second, 4, 1)))
            odd.append(jnp.where(upper, pltpu.roll(first, 4, 1), second))
        both = jnp.stack([jnp.stack(even, 1), jnp.stack(odd, 1)], 1)
        out_ref[one] = both.reshape(512, 128).astype(BF16)
        return carry

    lax.fori_loop(0, step, line, 0, unroll=2)


def assemble(pieces):
    rows, columns, depth = pieces[0].shape
    step = ASSEMBLE_STEP
    return pl.pallas_call(
        assemble_kernel,
        grid=(rows // step,),
        in_specs=[VMEM] * len(pieces),
        out_specs=pl.BlockSpec((step, 8 * columns, depth), lambda g: (g, 0, 0)),
        out_shape=jax.ShapeDtypeStruct((rows, 8 * columns, depth), BF16),
        scratch_shapes=[pltpu.VMEM((8, rows, columns, depth), BF16)],
        compiler_params=ROOM,
        cost_estimate=lasting(5),
        name="assemble",
    )(*pieces)


def spread_kernel(g_ref, w_ref, member_ref, _, out_ref):
    width = FACTOR_WIDTH
    scale = scale_of(member_ref[...])
    blank = jnp.zeros((64, 128), BF16)

    def pair(at, carry):
        parts = []
        for one in range(2):
            given = g_ref[2 * at + one]
            parts.append(jnp.concatenate([given, blank], 1))
            parts.append(jnp.concatenate([blank, given], 1))
        both = (nt(w_ref[...], jnp.concatenate(parts, 0)) * scale).astype(BF16)
        for one in range(2):
            here = pl.ds(pl.multiple_of((2 * at + one) * width, width), width)
            out_ref[here, :] = jnp.concatenate(
                [
                    both[width * e : width * e + width, 128 * one : 128 * one + 128]
                    for e in range(16)
                ],
                1,
            )
        return carry

    lax.fori_loop(0, g_ref.shape[0] // 2, pair, 0)


def spread_of(given, w, member, after):
    rows, columns, _ = given.shape
    return pl.pallas_call(
        spread_kernel,
        in_specs=[VMEM] * 3 + [ORDER],
        out_specs=VMEM,
        out_shape=jax.ShapeDtypeStruct((rows * FACTOR_WIDTH, columns * FACTOR_WIDTH), BF16),
        compiler_params=ROOM,
        cost_estimate=lasting(8),
        name="spread",
    )(given, w, member, after)


def couple_kernel(both_ref, w_ref, member_ref, *refs):
    b_pieces, (out_ref, a_ref, bd_ref, o_s, b_s) = refs[:-5], refs[-5:]
    width = FACTOR_WIDTH
    rows, columns = o_s.shape
    core = lax.axis_index("core")
    x_lo, y = res_index()
    near, far = (0, 1, 3, 4), (2, 5, 6, 7)
    for other in range(2):
        for part, piece in zip((near, far), b_pieces[2 * other : 2 * other + 2]):
            for at, block in enumerate(part):
                to = ((y + block) & 3) * 2 + (x_lo ^ (block // 4))
                to = pl.multiple_of((to * 2 + (core ^ other)) * 128, 128)
                put(b_s, pl.ds(to, 128), piece[128 * at : 128 * at + 128, :].astype(F32))
    count = columns // width
    for at in range(width):
        here = slice(at * count, at * count + count)
        bd_ref[here, :] = take(b_s, pl.ds(at, count, stride=width)).astype(BF16)
    a_ref[...] = both_ref[:, 128:].reshape(a_ref.shape)
    for at in range(columns // 256):
        here = slice(256 * at, 256 * at + 256)
        o_s[:, here] = nt(a_ref[...], bd_ref[here, :]).astype(BF16)
    scale = scale_of(member_ref[...])
    w = w_ref[...].astype(F32).T.astype(BF16)
    low = lax.broadcasted_iota(jnp.int32, (128, 128), 1) < 64

    def pair(at, carry):
        outer = o_s[pl.ds(pl.multiple_of(at * 2 * width, 2 * width), 2 * width), :]
        stacks = []
        for one in range(2):
            part = outer[width * one : width * one + width]
            stacks.append(
                jnp.concatenate([part[:, 128 * e : 128 * e + 128] for e in range(16)], 0)
            )
        both = nn(w, jnp.concatenate(stacks, 1))
        top = jnp.where(low, both[:128, :128], pltpu.roll(both[:128, 128:], 64, 1))
        bottom = jnp.where(low, pltpu.roll(both[128:, :128], 64, 1), both[128:, 128:])
        delta = ((top + bottom) * scale).T
        out_ref[pl.ds(at * 2, 2)] = delta.reshape(2, 64, 128).astype(BF16)
        return carry

    lax.fori_loop(0, rows // (2 * width), pair, 0, unroll=PAIR_UNROLL)


def couple(both, w, member, b_pieces):
    seqs = both.shape[2]
    rows, columns = both.shape[0] * 128, 4 * b_pieces[0].shape[0]
    return pl.pallas_call(
        couple_kernel,
        in_specs=[VMEM] * 7,
        out_specs=[VMEM] * 3,
        out_shape=[
            jax.ShapeDtypeStruct((rows // FACTOR_WIDTH, columns // FACTOR_WIDTH, 128), BF16),
            jax.ShapeDtypeStruct((rows, seqs), BF16),
            jax.ShapeDtypeStruct((columns, seqs), BF16),
        ],
        scratch_shapes=[
            pltpu.VMEM((rows, columns), BF16),
            pltpu.VMEM((2, columns, seqs // 2), F32),
        ],
        compiler_params=ROOM,
        cost_estimate=lasting(9),
        name="couple",
    )(both, w, member, *b_pieces)


def grads_kernel(a_ref, bd_ref, s_ref, _, ga_ref, own_ref, other_ref, turned_s):
    width = FACTOR_WIDTH
    blocks = own_ref.shape[0]
    columns = turned_s.shape[1] // width
    core = lax.axis_index("core")
    left = a_ref[...].astype(F32).T.astype(BF16)
    for at in range(columns * width // 256):
        here = slice(256 * at, 256 * at + 256)
        put(turned_s, here, nn(left, s_ref[:, here]).T)
    for other, out_ref in ((1, other_ref), (0, own_ref)):
        for block in range(blocks):
            for part in range(4):
                column = (2 * block + (core ^ other)) * 4 + part
                lines = take(turned_s, pl.ds(column, width, stride=columns))
                out_ref[block, width * part : width * part + width, :] = lines.astype(BF16)
    for at in range(4):
        here = slice(256 * at, 256 * at + 256)
        ga_ref[:, here] = nn(s_ref[here, :], bd_ref[...]).T.astype(BF16)


def factor_grads(a_all, bd, spread, after):
    seqs, columns = a_all.shape[1], spread.shape[1]
    shape = jax.ShapeDtypeStruct((columns // 256, 128, seqs), BF16)
    return pl.pallas_call(
        grads_kernel,
        in_specs=[VMEM] * 3 + [ORDER],
        out_specs=[VMEM] * 3,
        out_shape=[jax.ShapeDtypeStruct((seqs, spread.shape[0]), BF16), shape, shape],
        scratch_shapes=[pltpu.VMEM((2, columns, seqs // 2), F32)],
        compiler_params=ROOM,
        cost_estimate=lasting(10),
        name="factor_grads",
    )(a_all, bd, spread, after)


def fold_kernel(own_ref, other_ref, *refs):
    refs[-1][...] = (own_ref[...].astype(F32) + other_ref[...].astype(F32)).astype(BF16)


def fold(own, other, after):
    return pl.pallas_call(
        fold_kernel,
        in_specs=[VMEM] * 2 + [ORDER] * len(after),
        out_specs=VMEM,
        out_shape=jax.ShapeDtypeStruct(own.shape, BF16),
        compiler_params=ROOM,
        cost_estimate=lasting(1),
        name="fold",
    )(own, other, *after)


def pack_kernel(ga_ref, gb_ref, out_ref):
    groups, members, _ = out_ref.shape
    wide = ga_ref.shape[1]
    total = gb_ref[0].astype(F32)
    for at in range(1, gb_ref.shape[0]):
        total = total + gb_ref[at].astype(F32)
    out_ref[:, :, :wide] = ga_ref[...].reshape(groups, members, wide)
    out_ref[:, :, wide:] = total.T.reshape(groups, members, total.shape[0]).astype(BF16)


def pack_grads(ga, gb, groups):
    seqs, wide = ga.shape
    return pl.pallas_call(
        pack_kernel,
        in_specs=[VMEM] * 2,
        out_specs=VMEM,
        out_shape=jax.ShapeDtypeStruct((groups, seqs // groups, wide + gb.shape[1]), BF16),
        compiler_params=ROOM,
        cost_estimate=lasting(3),
        name="pack_grads",
    )(ga, gb)


def home_kernel(gf_ref, w_ref, x_ref, member_ref, chain_ref, x_out_ref, ct_ref, x_s, ct_s):
    width = FACTOR_WIDTH
    groups, rows, depth = x_ref.shape
    parts = 4
    seqs = rows // 2 // parts
    residues = groups * parts
    wide = residues * width
    x_hi, z = seq_index()
    x_lo, y = res_index()
    first = ((y * 2 + x_lo) * 2 + lax.axis_index("core")) * residues
    member = member_ref[pl.ds(x_hi * 4 + z, 1), :]
    member = jnp.broadcast_to(member.astype(F32), (8, member.shape[1])).T[:seqs, :1]
    total = gf_ref[0, :, :wide].astype(F32)
    for at in range(1, groups):
        total = total + gf_ref[at, :, :wide].astype(F32)
    lane = lax.broadcasted_iota(jnp.int32, (1, 128), 1) // width
    lines = []
    for group in range(groups):
        live = jnp.zeros((1, 128), F32)
        for at in range(parts):
            here = chain_ref[first + group * parts + at].astype(F32)
            live = jnp.where(lane == at, here, live)
        live = live * member
        left = total[:, 128 * group : 128 * group + 128] * live
        right = gf_ref[group, :, wide:].astype(F32) * live
        lines.append(jnp.concatenate([left, right], 1))
    given = jnp.concatenate(lines, 0)
    lane = lax.broadcasted_iota(jnp.int32, (1, depth), 1) // width % parts
    back = jnp.concatenate([w_ref[:width, :]] * parts + [w_ref[width:, :]] * parts, 0)
    for at in range(parts):
        upstream = nn(jnp.where(lane == at, given, 0.0).astype(BF16), back)
        x = x_ref[:, seqs * at : seqs * at + seqs]
        x = x.reshape(groups * seqs, depth).astype(F32)
        center = x - jnp.mean(x, -1, keepdims=True)
        inverse = lax.rsqrt(jnp.mean(center * center, -1, keepdims=True) + 1e-05)
        scaled = center * inverse
        cotangent = inverse * (
            upstream
            - jnp.mean(upstream, -1, keepdims=True)
            - scaled * jnp.mean(upstream * scaled, -1, keepdims=True)
        )
        for group in range(groups):
            here = pl.ds(group * parts + at, seqs, stride=residues)
            put(x_s, here, x[group * seqs : group * seqs + seqs])
            put(ct_s, here, cotangent[group * seqs : group * seqs + seqs])
    x_out_ref[...] = take(x_s, slice(None)).reshape(seqs, residues, depth).astype(BF16)
    ct_ref[...] = take(ct_s, slice(None)).reshape(seqs, residues, depth).astype(BF16)


def finish_home(gf, w, both, member, chain):
    groups, rows, depth = both.shape
    seqs, residues = rows // 8, groups * 4
    shape = (seqs, residues, depth)
    return pl.pallas_call(
        home_kernel,
        in_specs=[VMEM] * 4 + [SMEM],
        out_specs=[VMEM] * 2,
        out_shape=[jax.ShapeDtypeStruct(shape, BF16)] * 2,
        scratch_shapes=[pltpu.VMEM((2, seqs * residues, depth // 2), F32)] * 2,
        compiler_params=ROOM,
        cost_estimate=lasting(6),
        name="finish_home",
    )(gf, w, both, member, chain)


def hold_kernel(*refs):
    pass


def hold(arrays, after):
    count = len(arrays)
    return pl.pallas_call(
        hold_kernel,
        in_specs=[ORDER] * (count + 1),
        out_specs=[ORDER] * count,
        out_shape=[jax.ShapeDtypeStruct(one.shape, one.dtype) for one in arrays],
        input_output_aliases={at: at for at in range(count)},
        cost_estimate=lasting(0.1),
        name="hold",
    )(*arrays, after)


def turn_by(steps):
    return [(at, (at + steps) % 4) for at in range(4)]


SWAP = [(0, 1), (1, 0)]


def ring(x, along, across, after=None):
    partner = lax.ppermute(x, across, SWAP)
    below = lax.ppermute(x, along, turn_by(1))
    above = lax.ppermute(x, along, turn_by(3))
    far = lax.ppermute(x, along, turn_by(2))
    if after is not None:
        partner, far = hold([partner, far], after)
    partner_below = lax.ppermute(partner, along, turn_by(1))
    partner_above = lax.ppermute(partner, along, turn_by(3))
    partner_far = lax.ppermute(far, across, SWAP)
    return [x, above, far, below, partner, partner_above, partner_far, partner_below]


def ring_halves(x, along, across):
    half = x.shape[0] // 2
    partner = lax.ppermute(x, across, SWAP)
    below = lax.ppermute(x, along, turn_by(1))
    above = lax.ppermute(x, along, turn_by(3))
    far_low = lax.ppermute(below[:half], along, turn_by(1))
    far_high = lax.ppermute(above[half:], along, turn_by(3))
    partner_below = lax.ppermute(partner, along, turn_by(1))
    partner_above = lax.ppermute(partner, along, turn_by(3))
    partner_low = lax.ppermute(far_low, across, SWAP)
    partner_high = lax.ppermute(far_high, across, SWAP)
    return [
        x, above, far_low, far_high, below,
        partner, partner_above, partner_low, partner_high, partner_below,
    ]


def per_device(
    multiple_alignment_rep,
    pair_rep,
    aligned_member_valid,
    chain_position_valid,
    horizontal_entry_matrices,
    horizontal_exit_matrix,
    bias_proj,
    vertical_entry_matrices,
    vertical_exit_matrix,
    dyadic_projection_matrices,
    outer_out,
    pair_grad,
):
    seqs_here, res_here, depth = multiple_alignment_rep.shape
    residues = pair_rep.shape[1]
    pair_width = outer_out.shape[1]
    q_size, b_size, r_size = 8, 8, 16
    width = FACTOR_WIDTH
    q_at = lax.axis_index("x_hi") * 4 + lax.axis_index("z")
    member = aligned_member_valid.reshape(1, -1)
    chain_row = chain_position_valid.reshape(1, residues)

    dyadic_t = dyadic_projection_matrices.T
    cube = outer_out.reshape(width, width // 2, 2, pair_width)
    w_outer = cube.transpose(1, 0, 2, 3).reshape(16 * width, 2 * pair_width)
    grad_here = lax.dynamic_index_in_dim(
        pair_grad.reshape(res_here, r_size, q_size, 4, pair_width), q_at, 2, keepdims=False
    ).reshape(res_here, r_size * 4, pair_width)

    bias = pair_bias(pair_rep, bias_proj, chain_row)
    x_rows = lax.all_to_all(
        multiple_alignment_rep.reshape(b_size, seqs_here // b_size, res_here, depth),
        ("y", "x_lo"), 0, 0, tiled=True,
    )
    (x_rows,) = hold([x_rows], bias)
    x_other = lax.ppermute(x_rows, "core", SWAP)
    q, k, v, g = row_entry(x_rows, x_other, chain_row, horizontal_entry_matrices)
    bias_pieces = ring(bias, "y", "x_lo", after=q)
    near, far = (0, 1, 3, 4), (2, 5, 6, 7)
    after_row = ()
    for part in (near, far):
        after_row = row_attention(
            [(at // 4, at % 4) for at in part], q, k, v, g, x_rows, horizontal_exit_matrix,
            [bias_pieces[at] for at in part], after_row,
        )
        after_row = [after_row]
    (after_row,) = after_row

    spread = spread_of(grad_here, w_outer, member, after_row)
    columns = lax.all_to_all(
        after_row.reshape(q_size * b_size, 16, depth),
        ("x_hi", "z", "y", "x_lo"), 0, 0, tiled=True,
    )
    going, factor_b = col_attention(
        columns, member, chain_position_valid,
        vertical_entry_matrices, vertical_exit_matrix, dyadic_t, q_size, spread,
    )
    b_ring = ring(factor_b, "y", "x_lo")
    b_pieces = [jnp.concatenate([b_ring[at] for at in part], 0) for part in (near, far)]
    b_pieces += [lax.ppermute(piece, "core", SWAP) for piece in b_pieces]
    back = lax.all_to_all(going, ("x_hi", "z"), 0, 0, tiled=True)

    delta, a_all, bd = couple(back, w_outer, member, b_pieces)
    deltas = ring_halves(delta, "z", "x_hi")
    ga, gb, gb_other = factor_grads(a_all, bd, spread, deltas[5])
    gb_other = lax.ppermute(gb_other, "core", SWAP)
    gb = fold(gb, gb_other, [deltas[1], deltas[4], deltas[5]])
    gb = lax.all_to_all(gb, ("y", "x_lo"), 0, 0, tiled=True)
    couple_delta = assemble(deltas)
    factors = lax.all_to_all(pack_grads(ga, gb, q_size), ("x_hi", "z"), 0, 0, tiled=True)
    alignment_refreshed, cotangent = finish_home(
        factors, dyadic_t, back, member.reshape(q_size, seqs_here), chain_position_valid
    )
    return (alignment_refreshed, couple_delta, cotangent)


def solution(mesh):
    torus = jax.sharding.Mesh(
        mesh.devices.reshape(2, 4, 4, 2, 2), ("x_hi", "z", "y", "x_lo", "core")
    )
    seq, res = ("x_hi", "z"), ("y", "x_lo", "core")
    placed = (
        P(seq, res, None),
        P(res, None, None),
        P(),
        P(),
        P(),
        P(),
        P(),
        P(),
        P(),
        P(),
        P(),
        P(res, None, None),
    )
    return jax.shard_map(
        per_device,
        mesh=torus,
        in_specs=placed,
        out_specs=(P(seq, res, None), P(res, None, None), P(seq, res, None)),
        check_vma=False,
    )
```

```python
import functools

import jax
import jax.numpy as jnp
from jax import lax
from jax.experimental import pallas as pl
from jax.experimental.pallas import tpu as pltpu
from jax.sharding import PartitionSpec as P

FACTOR_WIDTH = 32
H = 8
HEAD_SIZE = 32
LOG2E = 1.4426950408889634
MASKED = -1000000000.0 * LOG2E
BF16 = jnp.bfloat16
F32 = jnp.float32
NT = (((1,), (1,)), ((), ()))
COL_STEP = 128
ROW_UNROLL = 4
PAIR_UNROLL = 8
BIAS_STEP = 8
ASSEMBLE_STEP = 8

VMEM = pl.BlockSpec(memory_space=pltpu.VMEM)
SMEM = pl.BlockSpec(memory_space=pltpu.SMEM)
ORDER = pl.BlockSpec(memory_space=pl.ANY)
ROOM = pltpu.CompilerParams(vmem_limit_bytes=56 * 1024 * 1024)


def lasting(microseconds):
    return pl.CostEstimate(
        flops=0, bytes_accessed=int(microseconds * 3.69e6), transcendentals=0
    )


def nn(left, right):
    return jnp.dot(left, right, preferred_element_type=F32)


def nt(left, right):
    return lax.dot_general(left, right, NT, preferred_element_type=F32)


def standardize(values):
    center = values - jnp.mean(values, -1, keepdims=True)
    spread = jnp.mean(center * center, -1, keepdims=True)
    return center * lax.rsqrt(spread + 1e-05)


def put(ref, rows, values):
    for half in range(2):
        ref[half, rows, :] = values[:, 128 * half : 128 * half + 128]


def take(ref, rows):
    return jnp.concatenate([ref[0, rows, :], ref[1, rows, :]], 1)


def column_of(row):
    return jnp.broadcast_to(row.astype(F32), (8, row.shape[1])).T[:, :1]


def seq_index():
    return lax.axis_index("x_hi"), lax.axis_index("z")


def res_index():
    return lax.axis_index("x_lo"), lax.axis_index("y")


def scale_of(member):
    return 1.0 / jnp.sum(member.astype(F32), keepdims=True)


def bias_kernel(pair_ref, proj_ref, valid_ref, out_ref, turn_s):
    at = pl.program_id(0)
    rows, residues, depth = pair_ref.shape
    line = lax.broadcasted_iota(jnp.int32, (depth, depth), 0)
    lane = lax.broadcasted_iota(jnp.int32, (depth, depth), 1)
    centering = (jnp.where(line == lane, 1.0, 0.0) - 1.0 / depth).astype(BF16)
    live = valid_ref[...] > 0
    proj = proj_ref[...].astype(F32)
    blank = jnp.zeros_like(proj)
    mean = jnp.full_like(proj, 1.0 / depth)
    sides = jnp.concatenate(
        [jnp.concatenate([proj, blank], 1), jnp.concatenate([blank, mean], 1)], 0
    ).astype(BF16)
    center = nn(pair_ref[...].reshape(rows * residues, depth), centering)
    both = jnp.concatenate([center.astype(BF16), (center * center).astype(BF16)], 1)
    for one in range(rows):
        sums = nt(sides, both[one * residues : one * residues + residues])
        bias = sums[:H] * lax.rsqrt(sums[H:] + 1e-05) * LOG2E
        bias = jnp.where(live, bias, MASKED)
        here = pl.ds(pl.multiple_of((at * rows + one) * H, H), H)
        for part in range(residues // 128):
            turn_s[part, here, :] = bias[:, 128 * part : 128 * part + 128]

    @pl.when(at == pl.num_programs(0) - 1)
    def _():
        total = out_ref.shape[0] // H
        for head in range(H):
            for part in range(residues // 128):
                out_ref[total * head : total * head + total, 128 * part : 128 * part + 128] = (
                    turn_s[part, pl.ds(head, total, stride=H), :].astype(BF16)
                )


def pair_bias(pair, proj, valid):
    rows, residues, depth = pair.shape
    step = BIAS_STEP
    return pl.pallas_call(
        bias_kernel,
        grid=(rows // step,),
        in_specs=[
            pl.BlockSpec((step, residues, depth), lambda g: (g, 0, 0)),
            pl.BlockSpec((H, depth), lambda g: (0, 0)),
            pl.BlockSpec((1, residues), lambda g: (0, 0)),
        ],
        out_specs=pl.BlockSpec((rows * H, residues), lambda g: (0, 0)),
        out_shape=jax.ShapeDtypeStruct((rows * H, residues), BF16),
        scratch_shapes=[pltpu.VMEM((residues // 128, rows * H, 128), F32)],
        compiler_params=ROOM,
        cost_estimate=lasting(9),
        name="pair_bias",
    )(pair, proj, valid)


def scores_of(query, keys, side):
    lanes = slice(128 * side, 128 * side + 128)
    lane = lax.broadcasted_iota(jnp.int32, (1, 128), 1) // HEAD_SIZE
    part = query[:, lanes]
    spread = [jnp.where(lane == head, part, 0.0).astype(BF16) for head in range(4)]
    return nt(jnp.concatenate(spread, 0), keys[:, lanes])


def weigh(scores, values):
    rows = scores.shape[0] // 4
    lane = lax.broadcasted_iota(jnp.int32, (1, 128), 1) // HEAD_SIZE
    weights = jnp.exp2(scores - jnp.max(scores, -1, keepdims=True)).astype(BF16)
    both = nn(weights, values)
    summed, total = both[:rows, :128], both[:rows, 128:]
    for head in range(1, 4):
        here = slice(rows * head, rows * head + rows)
        summed = jnp.where(lane == head, both[here, :128], summed)
        total = jnp.where(lane == head, both[here, 128:], total)
    return summed / total


def entry_kernel(x_ref, other_ref, valid_ref, w_ref, q_ref, k_ref, v_ref, g_ref, live_s):
    blocks, seqs, rows, depth = x_ref.shape
    core = lax.axis_index("core")
    v_ref[:, :, :, 128:] = jnp.ones(v_ref.shape[:3] + (128,), BF16)
    live_s[...] = jnp.broadcast_to(column_of(valid_ref[...]), live_s.shape)
    for s in range(seqs):
        for other in range(2):
            source = other_ref if other else x_ref
            x = source[:, s].reshape(blocks * rows, depth)
            normed = standardize(x.astype(F32)).astype(BF16)
            pair = nn(normed, w_ref[:, depth : 3 * depth])
            side = 1 - core if other else core
            for at in range(blocks):
                here = slice(rows * at, rows * at + rows)
                to = pl.ds(pl.multiple_of((2 * at + side) * rows, rows), rows)
                k_ref[s, to, :] = (pair[here, :depth] * live_s[to, :1]).astype(BF16)
                for part in range(2):
                    lanes = slice(depth + 128 * part, depth + 128 * part + 128)
                    v_ref[s, part, to, :128] = pair[here, lanes].astype(BF16)
            if not other:
                query = nn(normed, w_ref[:, :depth]) * (HEAD_SIZE**-0.5 * LOG2E)
                q_ref[s] = query.astype(BF16)
                g_ref[s] = jax.nn.sigmoid(nn(normed, w_ref[:, 3 * depth :])).astype(BF16)


def row_entry(x, other, valid, w):
    blocks, seqs, rows, depth = x.shape
    here = jax.ShapeDtypeStruct((seqs, blocks * rows, depth), BF16)
    full = jax.ShapeDtypeStruct((seqs, 2 * blocks * rows, depth), BF16)
    sides = jax.ShapeDtypeStruct((seqs, 2, 2 * blocks * rows, 256), BF16)
    return pl.pallas_call(
        entry_kernel,
        in_specs=[VMEM] * 4,
        out_specs=[VMEM] * 4,
        out_shape=[here, full, sides, here],
        scratch_shapes=[pltpu.VMEM((2 * blocks * rows, 128), F32)],
        compiler_params=ROOM,
        cost_estimate=lasting(5),
        name="row_entry",
    )(x, other, valid, w)


def place(index, pieces, store):
    across, along = index
    for block, piece in enumerate(pieces):
        store((across ^ (block // 4)) * 4 + ((along + block) & 3), piece)


def place_halves(index, pieces, size, store):
    across, along = index
    pieces = list(pieces)
    for block in range(8):
        parts = 2 if block % 4 == 2 else 1
        for part in range(parts):
            at = (across ^ (block // 4)) * 4 + ((along + block) & 3)
            store(at, size // parts * part, size // parts, pieces.pop(0))


def row_kernel(steps, q_ref, k_ref, v_ref, g_ref, x_ref, wo_ref, *refs):
    count = len(steps)
    pieces, (out_ref, bias_s, after_s) = refs[:count], refs[-3:]
    blocks, seqs, rows, depth = x_ref.shape
    lines = count * rows
    for at, piece in enumerate(pieces):
        for head in range(H):
            to = lines * head + rows * at
            bias_s[to : to + rows, :] = piece[rows * head : rows * head + rows, :]
    for before in refs[count:-3]:
        out_ref[...] = before[...]
    x_lo, y = res_index()
    at_blocks = [((y + ahead) & 3) * 2 + (x_lo ^ across) for across, ahead in steps]
    spots = [pl.ds(pl.multiple_of(at * rows, rows), rows) for at in at_blocks]

    def sequence(s, carry):
        query = jnp.concatenate([q_ref[s, spot, :] for spot in spots], 0)
        gate = jnp.concatenate([g_ref[s, spot, :] for spot in spots], 0)
        x = jnp.concatenate([x_ref[at, s] for at in at_blocks], 0)
        sides = []
        for side in range(2):
            offset = bias_s[4 * lines * side : 4 * lines * side + 4 * lines, :].astype(F32)
            sides.append(scores_of(query, k_ref.at[s], side) + offset)
        output = jnp.concatenate([weigh(sides[side], v_ref[s, side]) for side in range(2)], 1)
        gated = (gate.astype(F32) * output).astype(BF16)
        after_s[s] = x.astype(F32) + nn(gated, wo_ref[...])
        return carry

    lax.fori_loop(0, seqs, sequence, 0, unroll=ROW_UNROLL)
    upper = lax.broadcasted_iota(jnp.int32, (rows // 8, 8, depth), 1) < 4
    for at, block in enumerate(at_blocks):
        even, odd = [], []
        for pair in range(seqs // 2):
            first, second = (
                after_s[one, rows * at : rows * at + rows, :].reshape(rows // 8, 8, depth)
                for one in (2 * pair, 2 * pair + 1)
            )
            even.append(jnp.where(upper, first, pltpu.roll(second, 4, 1)))
            odd.append(jnp.where(upper, pltpu.roll(first, 4, 1), second))
        even = jnp.concatenate(even, 1).astype(BF16)
        odd = jnp.concatenate(odd, 1).astype(BF16)
        for pair in range(rows // 8):
            out_ref[2 * pair, block] = even[pair]
            out_ref[2 * pair + 1, block] = odd[pair]


def row_attention(steps, q, k, v, g, x, wo, bias, before=()):
    blocks, seqs, rows, depth = x.shape
    return pl.pallas_call(
        functools.partial(row_kernel, steps),
        in_specs=[VMEM] * (6 + len(bias) + len(before)),
        out_specs=VMEM,
        out_shape=jax.ShapeDtypeStruct((rows // 4, blocks, 4 * seqs, depth), BF16),
        scratch_shapes=[
            pltpu.VMEM((len(bias) * bias[0].shape[0], bias[0].shape[1]), BF16),
            pltpu.VMEM((seqs, len(bias) * rows, depth), F32),
        ],
        compiler_params=ROOM,
        cost_estimate=lasting(8),
        name="row_attention",
    )(q, k, v, g, x, wo, *bias, *before)


def col_kernel(
    y_ref, valid_ref, chain_ref, w_ref, wo_ref, dyadic_ref, _,
    out_ref, b_ref, y_s, q_s, k_s, v_s, g_s, o_s,
):
    tokens, depth = y_s.shape[1], 2 * y_s.shape[2]
    parts = q_s.shape[0]
    seqs = tokens // parts
    live = valid_ref[...].astype(F32)
    live_column = column_of(live)
    offset = jnp.where(live > 0, 0.0, MASKED)
    x_hi, z = seq_index()
    x_lo, y_at = res_index()
    first = ((y_at * 2 + x_lo) * 2 + lax.axis_index("core")) * 32 + (x_hi * 4 + z) * parts
    put(y_s, slice(None), y_ref[...].reshape(tokens, depth).astype(F32))
    for at in range(parts):
        y = take(y_s, pl.ds(at, seqs, stride=parts))
        mixed = nn(standardize(y).astype(BF16), w_ref[...])
        q_s[at] = mixed[:, :depth] * (HEAD_SIZE**-0.5 * LOG2E)
        k_s[at] = (mixed[:, depth : 2 * depth] * live_column).astype(BF16)
        for part in range(2):
            lanes = slice(2 * depth + 128 * part, 2 * depth + 128 * part + 128)
            v_s[at, part, :, :128] = mixed[:, lanes].astype(BF16)
        g_s[at] = jax.nn.sigmoid(mixed[:, 3 * depth :])
    step = COL_STEP
    v_s[:, :, :, 128:] = jnp.ones(v_s.shape[:3] + (128,), BF16)

    def block(part, carry):
        here = pl.ds(pl.multiple_of(part * step, step), step)
        scores = [
            [scores_of(q_s[at, here, :], k_s[at], side) + offset for side in range(2)]
            for at in range(parts)
        ]
        for at in range(parts):
            output = jnp.concatenate(
                [weigh(scores[at][side], v_s[at, side]) for side in range(2)], 1
            )
            o_s[at, here, :] = (g_s[at, here, :] * output).astype(BF16)
        return carry

    lax.fori_loop(0, seqs // step, block, 0)
    for at in range(parts):
        y = take(y_s, pl.ds(at, seqs, stride=parts))
        done = (y + nn(o_s[at], wo_ref[...])).astype(BF16)
        groups = out_ref.shape[0]
        here = slice(seqs // groups * at, seqs // groups * at + seqs // groups)
        out_ref[:, here, :] = done.reshape(groups, seqs // groups, depth)
        normed = standardize(done.astype(F32)).astype(BF16)
        factors = nt(dyadic_ref[...], normed) * (live * chain_ref[first + at].astype(F32))
        for group in range(groups):
            to = slice(128 + 32 * at, 160 + 32 * at)
            out_ref[group, to, :] = factors[:32].astype(BF16)
        b_ref[pl.ds(32 * at, 32), :] = factors[32:].astype(BF16)


def col_attention(y, valid, chain, w, wo, dyadic_t, groups, after):
    sources, eight, depth = y.shape
    tokens = sources * eight
    seqs = tokens // 4
    return pl.pallas_call(
        col_kernel,
        in_specs=[VMEM] * 2 + [SMEM] + [VMEM] * 3 + [ORDER],
        out_specs=[VMEM] * 2,
        out_shape=[
            jax.ShapeDtypeStruct((groups, 2 * 4 * FACTOR_WIDTH, seqs), BF16),
            jax.ShapeDtypeStruct((4 * FACTOR_WIDTH, seqs), BF16),
        ],
        scratch_shapes=[
            pltpu.VMEM((2, tokens, depth // 2), F32),
            pltpu.VMEM((4, seqs, depth), F32),
            pltpu.VMEM((4, seqs, depth), BF16),
            pltpu.VMEM((4, 2, seqs, 256), BF16),
            pltpu.VMEM((4, seqs, depth), F32),
            pltpu.VMEM((4, seqs, depth), BF16),
        ],
        compiler_params=ROOM,
        cost_estimate=lasting(8),
        name="col_attention",
    )(y, valid, chain, w, wo, dyadic_t, after)


def assemble_kernel(*refs):
    pieces, (out_ref, d_s) = refs[:10], refs[11:]
    step = out_ref.shape[0]
    at = pl.program_id(0)

    def store(block, start, size, piece):
        d_s[block, start : start + size] = piece[...]

    @pl.when(at == 0)
    def _():
        place_halves(seq_index(), pieces, d_s.shape[1], store)

    upper = lax.broadcasted_iota(jnp.int32, (8, 8, 128), 1) < 4

    def line(one, carry):
        even, odd = [], []
        for pair in range(4):
            first = d_s[2 * pair, at * step + one].astype(F32).reshape(8, 8, 128)
            second = d_s[2 * pair + 1, at * step + one].astype(F32).reshape(8, 8, 128)
            even.append(jnp.where(upper, first, pltpu.roll(second, 4, 1)))
            odd.append(jnp.where(upper, pltpu.roll(first, 4, 1), second))
        both = jnp.stack([jnp.stack(even, 1), jnp.stack(odd, 1)], 1)
        out_ref[one] = both.reshape(512, 128).astype(BF16)
        return carry

    lax.fori_loop(0, step, line, 0, unroll=2)


def assemble(pieces, after):
    rows, columns, depth = pieces[0].shape
    step = ASSEMBLE_STEP
    return pl.pallas_call(
        assemble_kernel,
        grid=(rows // step,),
        in_specs=[VMEM] * len(pieces) + [ORDER],
        out_specs=pl.BlockSpec((step, 8 * columns, depth), lambda g: (g, 0, 0)),
        out_shape=jax.ShapeDtypeStruct((rows, 8 * columns, depth), BF16),
        scratch_shapes=[pltpu.VMEM((8, rows, columns, depth), BF16)],
        compiler_params=ROOM,
        cost_estimate=lasting(5),
        name="assemble",
    )(*pieces, after)


def spread_kernel(g_ref, w_ref, member_ref, _, out_ref):
    width = FACTOR_WIDTH
    scale = scale_of(member_ref[...])
    blank = jnp.zeros((64, 128), BF16)

    def pair(at, carry):
        parts = []
        for one in range(2):
            given = g_ref[2 * at + one]
            parts.append(jnp.concatenate([given, blank], 1))
            parts.append(jnp.concatenate([blank, given], 1))
        both = (nt(w_ref[...], jnp.concatenate(parts, 0)) * scale).astype(BF16)
        for one in range(2):
            here = pl.ds(pl.multiple_of((2 * at + one) * width, width), width)
            out_ref[here, :] = jnp.concatenate(
                [
                    both[width * e : width * e + width, 128 * one : 128 * one + 128]
                    for e in range(16)
                ],
                1,
            )
        return carry

    lax.fori_loop(0, g_ref.shape[0] // 2, pair, 0)


def spread_of(given, w, member, after):
    rows, columns, _ = given.shape
    return pl.pallas_call(
        spread_kernel,
        in_specs=[VMEM] * 3 + [ORDER],
        out_specs=VMEM,
        out_shape=jax.ShapeDtypeStruct((rows * FACTOR_WIDTH, columns * FACTOR_WIDTH), BF16),
        compiler_params=ROOM,
        cost_estimate=lasting(8),
        name="spread",
    )(given, w, member, after)


def couple_kernel(a_ref, bd_ref, w_ref, member_ref, out_ref, o_s):
    width = FACTOR_WIDTH
    rows, columns = o_s.shape
    for at in range(columns // 256):
        here = slice(256 * at, 256 * at + 256)
        o_s[:, here] = nt(a_ref[...], bd_ref[here, :]).astype(BF16)
    scale = scale_of(member_ref[...])
    w = w_ref[...].astype(F32).T.astype(BF16)
    low = lax.broadcasted_iota(jnp.int32, (128, 128), 1) < 64

    def pair(at, carry):
        outer = o_s[pl.ds(pl.multiple_of(at * 2 * width, 2 * width), 2 * width), :]
        stacks = []
        for one in range(2):
            part = outer[width * one : width * one + width]
            stacks.append(
                jnp.concatenate([part[:, 128 * e : 128 * e + 128] for e in range(16)], 0)
            )
        both = nn(w, jnp.concatenate(stacks, 1))
        top = jnp.where(low, both[:128, :128], pltpu.roll(both[:128, 128:], 64, 1))
        bottom = jnp.where(low, pltpu.roll(both[128:, :128], 64, 1), both[128:, 128:])
        delta = ((top + bottom) * scale).T
        out_ref[pl.ds(at * 2, 2)] = delta.reshape(2, 64, 128).astype(BF16)
        return carry

    lax.fori_loop(0, rows // (2 * width), pair, 0, unroll=PAIR_UNROLL)


def couple(a_all, bd, w, member):
    rows, columns = a_all.shape[0], bd.shape[0]
    return pl.pallas_call(
        couple_kernel,
        in_specs=[VMEM] * 4,
        out_specs=VMEM,
        out_shape=jax.ShapeDtypeStruct(
            (rows // FACTOR_WIDTH, columns // FACTOR_WIDTH, 128), BF16
        ),
        scratch_shapes=[pltpu.VMEM((rows, columns), BF16)],
        compiler_params=ROOM,
        cost_estimate=lasting(6),
        name="couple",
    )(a_all, bd, w, member)


def grads_kernel(both_ref, s_ref, *refs):
    b_pieces, (a_ref, bd_ref, ga_ref, own_ref, other_ref, turned_s) = refs[:4], refs[4:]
    width = FACTOR_WIDTH
    blocks = own_ref.shape[0]
    columns = turned_s.shape[1] // width
    core = lax.axis_index("core")
    x_lo, y = res_index()
    near, far = (0, 1, 3, 4), (2, 5, 6, 7)
    for other in range(2):
        for part, piece in zip((near, far), b_pieces[2 * other : 2 * other + 2]):
            for at, block in enumerate(part):
                to = ((y + block) & 3) * 2 + (x_lo ^ (block // 4))
                to = pl.multiple_of((to * 2 + (core ^ other)) * 128, 128)
                lines = piece[128 * at : 128 * at + 128, :]
                put(turned_s, pl.ds(to, 128), lines.astype(F32))
    for at in range(width):
        here = slice(at * columns, at * columns + columns)
        bd_ref[here, :] = take(turned_s, pl.ds(at, columns, stride=width)).astype(BF16)
    a_ref[...] = both_ref[:, 128:].reshape(a_ref.shape)
    left = a_ref[...].astype(F32).T.astype(BF16)
    for at in range(columns * width // 256):
        here = slice(256 * at, 256 * at + 256)
        put(turned_s, here, nn(left, s_ref[:, here]).T)
    for other, out_ref in ((1, other_ref), (0, own_ref)):
        for block in range(blocks):
            for part in range(4):
                column = (2 * block + (core ^ other)) * 4 + part
                lines = take(turned_s, pl.ds(column, width, stride=columns))
                out_ref[block, width * part : width * part + width, :] = lines.astype(BF16)
    for at in range(4):
        here = slice(256 * at, 256 * at + 256)
        ga_ref[:, here] = nn(s_ref[here, :], bd_ref[...]).T.astype(BF16)


def factor_grads(both, spread, b_pieces):
    seqs = both.shape[2]
    rows, columns = spread.shape
    shape = jax.ShapeDtypeStruct((columns // 256, 128, seqs), BF16)
    return pl.pallas_call(
        grads_kernel,
        in_specs=[VMEM] * 6,
        out_specs=[VMEM] * 5,
        out_shape=[
            jax.ShapeDtypeStruct((rows, seqs), BF16),
            jax.ShapeDtypeStruct((columns, seqs), BF16),
            jax.ShapeDtypeStruct((seqs, rows), BF16),
            shape,
            shape,
        ],
        scratch_shapes=[pltpu.VMEM((2, columns, seqs // 2), F32)],
        compiler_params=ROOM,
        cost_estimate=lasting(9),
        name="factor_grads",
    )(both, spread, *b_pieces)


def fold_kernel(own_ref, other_ref, out_ref):
    out_ref[...] = (own_ref[...].astype(F32) + other_ref[...].astype(F32)).astype(BF16)


def fold(own, other):
    return pl.pallas_call(
        fold_kernel,
        in_specs=[VMEM] * 2,
        out_specs=VMEM,
        out_shape=jax.ShapeDtypeStruct(own.shape, BF16),
        compiler_params=ROOM,
        cost_estimate=lasting(1),
        name="fold",
    )(own, other)


def pack_kernel(ga_ref, gb_ref, out_ref):
    groups, members, _ = out_ref.shape
    wide = ga_ref.shape[1]
    total = gb_ref[0].astype(F32)
    for at in range(1, gb_ref.shape[0]):
        total = total + gb_ref[at].astype(F32)
    out_ref[:, :, :wide] = ga_ref[...].reshape(groups, members, wide)
    out_ref[:, :, wide:] = total.T.reshape(groups, members, total.shape[0]).astype(BF16)


def pack_grads(ga, gb, groups):
    seqs, wide = ga.shape
    return pl.pallas_call(
        pack_kernel,
        in_specs=[VMEM] * 2,
        out_specs=VMEM,
        out_shape=jax.ShapeDtypeStruct((groups, seqs // groups, wide + gb.shape[1]), BF16),
        compiler_params=ROOM,
        cost_estimate=lasting(3),
        name="pack_grads",
    )(ga, gb)


def home_kernel(gf_ref, w_ref, x_ref, member_ref, chain_ref, x_out_ref, ct_ref, x_s, ct_s, live_s):
    width = FACTOR_WIDTH
    groups, rows, depth = x_ref.shape
    parts = 4
    seqs = rows // 2 // parts
    residues = groups * parts
    wide = residues * width
    x_hi, z = seq_index()
    x_lo, y = res_index()
    first = ((y * 2 + x_lo) * 2 + lax.axis_index("core")) * residues
    live_s[...] = jnp.broadcast_to(column_of(member_ref[...]), live_s.shape)
    member = live_s[pl.ds(pl.multiple_of((x_hi * 4 + z) * seqs, seqs), seqs), :1]
    total = gf_ref[0, :, :wide].astype(F32)
    for at in range(1, groups):
        total = total + gf_ref[at, :, :wide].astype(F32)
    lane = lax.broadcasted_iota(jnp.int32, (1, 128), 1) // width
    lines = []
    for group in range(groups):
        live = jnp.zeros((1, 128), F32)
        for at in range(parts):
            here = chain_ref[first + group * parts + at].astype(F32)
            live = jnp.where(lane == at, here, live)
        live = live * member
        left = total[:, 128 * group : 128 * group + 128] * live
        right = gf_ref[group, :, wide:].astype(F32) * live
        lines.append(jnp.concatenate([left, right], 1))
    given = jnp.concatenate(lines, 0)
    lane = lax.broadcasted_iota(jnp.int32, (1, depth), 1) // width % parts
    back = jnp.concatenate([w_ref[:width, :]] * parts + [w_ref[width:, :]] * parts, 0)
    for at in range(parts):
        upstream = nn(jnp.where(lane == at, given, 0.0).astype(BF16), back)
        x = x_ref[:, seqs * at : seqs * at + seqs]
        x = x.reshape(groups * seqs, depth).astype(F32)
        center = x - jnp.mean(x, -1, keepdims=True)
        inverse = lax.rsqrt(jnp.mean(center * center, -1, keepdims=True) + 1e-05)
        scaled = center * inverse
        cotangent = inverse * (
            upstream
            - jnp.mean(upstream, -1, keepdims=True)
            - scaled * jnp.mean(upstream * scaled, -1, keepdims=True)
        )
        for group in range(groups):
            here = pl.ds(group * parts + at, seqs, stride=residues)
            put(x_s, here, x[group * seqs : group * seqs + seqs])
            put(ct_s, here, cotangent[group * seqs : group * seqs + seqs])
    x_out_ref[...] = take(x_s, slice(None)).reshape(seqs, residues, depth).astype(BF16)
    ct_ref[...] = take(ct_s, slice(None)).reshape(seqs, residues, depth).astype(BF16)


def finish_home(gf, w, both, member, chain):
    groups, rows, depth = both.shape
    seqs, residues = rows // 8, groups * 4
    shape = (seqs, residues, depth)
    return pl.pallas_call(
        home_kernel,
        in_specs=[VMEM] * 4 + [SMEM],
        out_specs=[VMEM] * 2,
        out_shape=[jax.ShapeDtypeStruct(shape, BF16)] * 2,
        scratch_shapes=[pltpu.VMEM((2, seqs * residues, depth // 2), F32)] * 2
        + [pltpu.VMEM((member.shape[1], 128), F32)],
        compiler_params=ROOM,
        cost_estimate=lasting(6),
        name="finish_home",
    )(gf, w, both, member, chain)


def hold_kernel(*refs):
    pass


def hold(arrays, after):
    count = len(arrays)
    return pl.pallas_call(
        hold_kernel,
        in_specs=[ORDER] * (count + 1),
        out_specs=[ORDER] * count,
        out_shape=[jax.ShapeDtypeStruct(one.shape, one.dtype) for one in arrays],
        input_output_aliases={at: at for at in range(count)},
        cost_estimate=lasting(0.1),
        name="hold",
    )(*arrays, after)


def turn_by(steps):
    return [(at, (at + steps) % 4) for at in range(4)]


SWAP = [(0, 1), (1, 0)]


def ring(x, along, across, after=None):
    partner = lax.ppermute(x, across, SWAP)
    below = lax.ppermute(x, along, turn_by(1))
    above = lax.ppermute(x, along, turn_by(3))
    far = lax.ppermute(x, along, turn_by(2))
    if after is not None:
        partner, far = hold([partner, far], after)
    partner_below = lax.ppermute(partner, along, turn_by(1))
    partner_above = lax.ppermute(partner, along, turn_by(3))
    partner_far = lax.ppermute(far, across, SWAP)
    return [x, above, far, below, partner, partner_above, partner_far, partner_below]


def ring_halves(x, along, across):
    half = x.shape[0] // 2
    partner = lax.ppermute(x, across, SWAP)
    below = lax.ppermute(x, along, turn_by(1))
    above = lax.ppermute(x, along, turn_by(3))
    far_low = lax.ppermute(below[:half], along, turn_by(1))
    far_high = lax.ppermute(above[half:], along, turn_by(3))
    partner_below = lax.ppermute(partner, along, turn_by(1))
    partner_above = lax.ppermute(partner, along, turn_by(3))
    partner_low = lax.ppermute(far_low, across, SWAP)
    partner_high = lax.ppermute(far_high, across, SWAP)
    return [
        x, above, far_low, far_high, below,
        partner, partner_above, partner_low, partner_high, partner_below,
    ]


def per_device(
    multiple_alignment_rep,
    pair_rep,
    aligned_member_valid,
    chain_position_valid,
    horizontal_entry_matrices,
    horizontal_exit_matrix,
    bias_proj,
    vertical_entry_matrices,
    vertical_exit_matrix,
    dyadic_projection_matrices,
    outer_out,
    pair_grad,
):
    seqs_here, res_here, depth = multiple_alignment_rep.shape
    residues = pair_rep.shape[1]
    pair_width = outer_out.shape[1]
    q_size, b_size, r_size = 8, 8, 16
    width = FACTOR_WIDTH
    q_at = lax.axis_index("x_hi") * 4 + lax.axis_index("z")
    member = aligned_member_valid.reshape(1, -1)
    chain_row = chain_position_valid.reshape(1, residues)

    dyadic_t = dyadic_projection_matrices.T
    cube = outer_out.reshape(width, width // 2, 2, pair_width)
    w_outer = cube.transpose(1, 0, 2, 3).reshape(16 * width, 2 * pair_width)
    grad_here = lax.dynamic_index_in_dim(
        pair_grad.reshape(res_here, r_size, q_size, 4, pair_width), q_at, 2, keepdims=False
    ).reshape(res_here, r_size * 4, pair_width)

    bias = pair_bias(pair_rep, bias_proj.T, chain_row)
    x_rows = lax.all_to_all(
        multiple_alignment_rep.reshape(b_size, seqs_here // b_size, res_here, depth),
        ("y", "x_lo"), 0, 0, tiled=True,
    )
    (x_rows,) = hold([x_rows], bias)
    x_other = lax.ppermute(x_rows, "core", SWAP)
    q, k, v, g = row_entry(x_rows, x_other, chain_row, horizontal_entry_matrices)
    bias_pieces = ring(bias, "y", "x_lo", after=q)
    near, far = (0, 1, 3, 4), (2, 5, 6, 7)
    after_row = ()
    for part in (near, far):
        after_row = row_attention(
            [(at // 4, at % 4) for at in part], q, k, v, g, x_rows, horizontal_exit_matrix,
            [bias_pieces[at] for at in part], after_row,
        )
        after_row = [after_row]
    (after_row,) = after_row

    spread = spread_of(grad_here, w_outer, member, after_row)
    columns = lax.all_to_all(
        after_row.reshape(q_size * b_size, 16, depth),
        ("x_hi", "z", "y", "x_lo"), 0, 0, tiled=True,
    )
    going, factor_b = col_attention(
        columns, member, chain_position_valid,
        vertical_entry_matrices, vertical_exit_matrix, dyadic_t, q_size, spread,
    )
    b_ring = ring(factor_b, "y", "x_lo")
    b_pieces = [jnp.concatenate([b_ring[at] for at in part], 0) for part in (near, far)]
    b_pieces += [lax.ppermute(piece, "core", SWAP) for piece in b_pieces]
    back = lax.all_to_all(going, ("x_hi", "z"), 0, 0, tiled=True)

    a_all, bd, ga, gb, gb_other = factor_grads(back, spread, b_pieces)
    gb_other = lax.ppermute(gb_other, "core", SWAP)
    delta = couple(a_all, bd, w_outer, member)
    deltas = ring_halves(delta, "z", "x_hi")
    gb = fold(gb, gb_other)
    gb = lax.all_to_all(gb, ("y", "x_lo"), 0, 0, tiled=True)
    factors = lax.all_to_all(pack_grads(ga, gb, q_size), ("x_hi", "z"), 0, 0, tiled=True)
    alignment_refreshed, cotangent = finish_home(
        factors, dyadic_t, back, member, chain_position_valid
    )
    couple_delta = assemble(deltas, cotangent)
    return (alignment_refreshed, couple_delta, cotangent)


def solution(mesh):
    torus = jax.sharding.Mesh(
        mesh.devices.reshape(2, 4, 4, 2, 2), ("x_hi", "z", "y", "x_lo", "core")
    )
    seq, res = ("x_hi", "z"), ("y", "x_lo", "core")
    placed = (
        P(seq, res, None),
        P(res, None, None),
        P(),
        P(),
        P(),
        P(),
        P(),
        P(),
        P(),
        P(),
        P(),
        P(res, None, None),
    )
    return jax.shard_map(
        per_device,
        mesh=torus,
        in_specs=placed,
        out_specs=(P(seq, res, None), P(res, None, None), P(seq, res, None)),
        check_vma=False,
    )
```

```python
import functools

import jax
import jax.numpy as jnp
from jax import lax
from jax.experimental import pallas as pl
from jax.experimental.pallas import tpu as pltpu
from jax.sharding import PartitionSpec as P

FACTOR_WIDTH = 32
H = 8
HEAD_SIZE = 32
LOG2E = 1.4426950408889634
MASKED = -1000000000.0 * LOG2E
BF16 = jnp.bfloat16
F32 = jnp.float32
NT = (((1,), (1,)), ((), ()))
COL_STEP = 128
ROW_UNROLL = 4
PAIR_UNROLL = 8
BIAS_STEP = 8
ASSEMBLE_STEP = 8

VMEM = pl.BlockSpec(memory_space=pltpu.VMEM)
SMEM = pl.BlockSpec(memory_space=pltpu.SMEM)
ORDER = pl.BlockSpec(memory_space=pl.ANY)
ROOM = pltpu.CompilerParams(vmem_limit_bytes=24 * 1024 * 1024)


def lasting(microseconds):
    return pl.CostEstimate(
        flops=0, bytes_accessed=int(microseconds * 3.69e6), transcendentals=0
    )


def nn(left, right):
    return jnp.dot(left, right, preferred_element_type=F32)


def nt(left, right):
    return lax.dot_general(left, right, NT, preferred_element_type=F32)


def standardize(values):
    center = values - jnp.mean(values, -1, keepdims=True)
    spread = jnp.mean(center * center, -1, keepdims=True)
    return center * lax.rsqrt(spread + 1e-05)


def put(ref, rows, values):
    for half in range(2):
        ref[half, rows, :] = values[:, 128 * half : 128 * half + 128]


def take(ref, rows):
    return jnp.concatenate([ref[0, rows, :], ref[1, rows, :]], 1)


def column_of(row):
    return jnp.broadcast_to(row.astype(F32), (8, row.shape[1])).T[:, :1]


def seq_index():
    return lax.axis_index("x_hi"), lax.axis_index("z")


def res_index():
    return lax.axis_index("x_lo"), lax.axis_index("y")


def scale_of(member):
    return 1.0 / jnp.sum(member.astype(F32), keepdims=True)


def bias_kernel(pair_ref, proj_ref, valid_ref, out_ref, turn_s):
    at = pl.program_id(0)
    rows, residues, depth = pair_ref.shape
    line = lax.broadcasted_iota(jnp.int32, (depth, depth), 0)
    lane = lax.broadcasted_iota(jnp.int32, (depth, depth), 1)
    centering = (jnp.where(line == lane, 1.0, 0.0) - 1.0 / depth).astype(BF16)
    live = valid_ref[...] > 0
    proj = proj_ref[...].astype(F32)
    blank = jnp.zeros_like(proj)
    mean = jnp.full_like(proj, 1.0 / depth)
    sides = jnp.concatenate(
        [jnp.concatenate([proj, blank], 1), jnp.concatenate([blank, mean], 1)], 0
    ).astype(BF16)
    center = nn(pair_ref[...].reshape(rows * residues, depth), centering)
    both = jnp.concatenate([center.astype(BF16), (center * center).astype(BF16)], 1)
    for one in range(rows):
        sums = nt(sides, both[one * residues : one * residues + residues])
        bias = sums[:H] * lax.rsqrt(sums[H:] + 1e-05) * LOG2E
        bias = jnp.where(live, bias, MASKED)
        here = pl.ds(pl.multiple_of((at * rows + one) * H, H), H)
        for part in range(residues // 128):
            turn_s[part, here, :] = bias[:, 128 * part : 128 * part + 128]

    @pl.when(at == pl.num_programs(0) - 1)
    def _():
        total = out_ref.shape[0] // H
        for head in range(H):
            for part in range(residues // 128):
                out_ref[total * head : total * head + total, 128 * part : 128 * part + 128] = (
                    turn_s[part, pl.ds(head, total, stride=H), :].astype(BF16)
                )


def pair_bias(pair, proj, valid):
    rows, residues, depth = pair.shape
    step = BIAS_STEP
    return pl.pallas_call(
        bias_kernel,
        grid=(rows // step,),
        in_specs=[
            pl.BlockSpec((step, residues, depth), lambda g: (g, 0, 0)),
            pl.BlockSpec((H, depth), lambda g: (0, 0)),
            pl.BlockSpec((1, residues), lambda g: (0, 0)),
        ],
        out_specs=pl.BlockSpec((rows * H, residues), lambda g: (0, 0)),
        out_shape=jax.ShapeDtypeStruct((rows * H, residues), BF16),
        scratch_shapes=[pltpu.VMEM((residues // 128, rows * H, 128), F32)],
        compiler_params=ROOM,
        cost_estimate=lasting(9),
        name="pair_bias",
    )(pair, proj, valid)


def scores_of(query, keys, side):
    lanes = slice(128 * side, 128 * side + 128)
    lane = lax.broadcasted_iota(jnp.int32, (1, 128), 1) // HEAD_SIZE
    part = query[:, lanes]
    spread = [jnp.where(lane == head, part, 0.0).astype(BF16) for head in range(4)]
    return nt(jnp.concatenate(spread, 0), keys[:, lanes])


def weigh(scores, values):
    rows = scores.shape[0] // 4
    lane = lax.broadcasted_iota(jnp.int32, (1, 128), 1) // HEAD_SIZE
    weights = jnp.exp2(scores - jnp.max(scores, -1, keepdims=True)).astype(BF16)
    both = nn(weights, values)
    summed, total = both[:rows, :128], both[:rows, 128:]
    for head in range(1, 4):
        here = slice(rows * head, rows * head + rows)
        summed = jnp.where(lane == head, both[here, :128], summed)
        total = jnp.where(lane == head, both[here, 128:], total)
    return summed / total


def entry_kernel(x_ref, other_ref, valid_ref, w_ref, q_ref, k_ref, v_ref, g_ref, live_s):
    blocks, seqs, rows, depth = x_ref.shape
    core = lax.axis_index("core")
    v_ref[:, :, :, 128:] = jnp.ones(v_ref.shape[:3] + (128,), BF16)
    live_s[...] = jnp.broadcast_to(column_of(valid_ref[...]), live_s.shape)
    for s in range(seqs):
        for other in range(2):
            source = other_ref if other else x_ref
            x = source[:, s].reshape(blocks * rows, depth)
            normed = standardize(x.astype(F32)).astype(BF16)
            pair = nn(normed, w_ref[:, depth : 3 * depth])
            side = 1 - core if other else core
            for at in range(blocks):
                here = slice(rows * at, rows * at + rows)
                to = pl.ds(pl.multiple_of((2 * at + side) * rows, rows), rows)
                k_ref[s, to, :] = (pair[here, :depth] * live_s[to, :1]).astype(BF16)
                for part in range(2):
                    lanes = slice(depth + 128 * part, depth + 128 * part + 128)
                    v_ref[s, part, to, :128] = pair[here, lanes].astype(BF16)
            if not other:
                query = nn(normed, w_ref[:, :depth]) * (HEAD_SIZE**-0.5 * LOG2E)
                q_ref[s] = query.astype(BF16)
                g_ref[s] = jax.nn.sigmoid(nn(normed, w_ref[:, 3 * depth :])).astype(BF16)


def row_entry(x, other, valid, w):
    blocks, seqs, rows, depth = x.shape
    here = jax.ShapeDtypeStruct((seqs, blocks * rows, depth), BF16)
    full = jax.ShapeDtypeStruct((seqs, 2 * blocks * rows, depth), BF16)
    sides = jax.ShapeDtypeStruct((seqs, 2, 2 * blocks * rows, 256), BF16)
    return pl.pallas_call(
        entry_kernel,
        in_specs=[VMEM] * 4,
        out_specs=[VMEM] * 4,
        out_shape=[here, full, sides, here],
        scratch_shapes=[pltpu.VMEM((2 * blocks * rows, 128), F32)],
        compiler_params=ROOM,
        cost_estimate=lasting(5),
        name="row_entry",
    )(x, other, valid, w)


def place(index, pieces, store):
    across, along = index
    for block, piece in enumerate(pieces):
        store((across ^ (block // 4)) * 4 + ((along + block) & 3), piece)


def place_halves(index, pieces, size, store):
    across, along = index
    pieces = list(pieces)
    for block in range(8):
        parts = 2 if block % 4 == 2 else 1
        for part in range(parts):
            at = (across ^ (block // 4)) * 4 + ((along + block) & 3)
            store(at, size // parts * part, size // parts, pieces.pop(0))


def row_kernel(steps, q_ref, k_ref, v_ref, g_ref, x_ref, wo_ref, *refs):
    count = len(steps)
    pieces, (out_ref, bias_s, after_s) = refs[:count], refs[-3:]
    blocks, seqs, rows, depth = x_ref.shape
    lines = count * rows
    for at, piece in enumerate(pieces):
        for head in range(H):
            to = lines * head + rows * at
            bias_s[to : to + rows, :] = piece[rows * head : rows * head + rows, :]
    for before in refs[count:-3]:
        out_ref[...] = before[...]
    x_lo, y = res_index()
    at_blocks = [((y + ahead) & 3) * 2 + (x_lo ^ across) for across, ahead in steps]
    spots = [pl.ds(pl.multiple_of(at * rows, rows), rows) for at in at_blocks]

    def sequence(s, carry):
        query = jnp.concatenate([q_ref[s, spot, :] for spot in spots], 0)
        gate = jnp.concatenate([g_ref[s, spot, :] for spot in spots], 0)
        x = jnp.concatenate([x_ref[at, s] for at in at_blocks], 0)
        sides = []
        for side in range(2):
            offset = bias_s[4 * lines * side : 4 * lines * side + 4 * lines, :].astype(F32)
            sides.append(scores_of(query, k_ref.at[s], side) + offset)
        output = jnp.concatenate([weigh(sides[side], v_ref[s, side]) for side in range(2)], 1)
        gated = (gate.astype(F32) * output).astype(BF16)
        after_s[s] = x.astype(F32) + nn(gated, wo_ref[...])
        return carry

    lax.fori_loop(0, seqs, sequence, 0, unroll=ROW_UNROLL)
    upper = lax.broadcasted_iota(jnp.int32, (rows // 8, 8, depth), 1) < 4
    for at, block in enumerate(at_blocks):
        even, odd = [], []
        for pair in range(seqs // 2):
            first, second = (
                after_s[one, rows * at : rows * at + rows, :].reshape(rows // 8, 8, depth)
                for one in (2 * pair, 2 * pair + 1)
            )
            even.append(jnp.where(upper, first, pltpu.roll(second, 4, 1)))
            odd.append(jnp.where(upper, pltpu.roll(first, 4, 1), second))
        even = jnp.concatenate(even, 1).astype(BF16)
        odd = jnp.concatenate(odd, 1).astype(BF16)
        for pair in range(rows // 8):
            out_ref[2 * pair, block] = even[pair]
            out_ref[2 * pair + 1, block] = odd[pair]


def row_attention(steps, q, k, v, g, x, wo, bias, before=()):
    blocks, seqs, rows, depth = x.shape
    return pl.pallas_call(
        functools.partial(row_kernel, steps),
        in_specs=[VMEM] * (6 + len(bias) + len(before)),
        out_specs=VMEM,
        out_shape=jax.ShapeDtypeStruct((rows // 4, blocks, 4 * seqs, depth), BF16),
        scratch_shapes=[
            pltpu.VMEM((len(bias) * bias[0].shape[0], bias[0].shape[1]), BF16),
            pltpu.VMEM((seqs, len(bias) * rows, depth), F32),
        ],
        compiler_params=ROOM,
        cost_estimate=lasting(8),
        name="row_attention",
    )(q, k, v, g, x, wo, *bias, *before)


def col_kernel(
    y_ref, valid_ref, chain_ref, w_ref, wo_ref, dyadic_ref, _,
    out_ref, b_ref, y_s, q_s, k_s, v_s, g_s, o_s,
):
    tokens, depth = y_s.shape[1], 2 * y_s.shape[2]
    parts = q_s.shape[0]
    seqs = tokens // parts
    live = valid_ref[...].astype(F32)
    live_column = column_of(live)
    offset = jnp.where(live > 0, 0.0, MASKED)
    x_hi, z = seq_index()
    x_lo, y_at = res_index()
    first = ((y_at * 2 + x_lo) * 2 + lax.axis_index("core")) * 32 + (x_hi * 4 + z) * parts
    put(y_s, slice(None), y_ref[...].reshape(tokens, depth).astype(F32))
    for at in range(parts):
        y = take(y_s, pl.ds(at, seqs, stride=parts))
        mixed = nn(standardize(y).astype(BF16), w_ref[...])
        q_s[at] = mixed[:, :depth] * (HEAD_SIZE**-0.5 * LOG2E)
        k_s[at] = (mixed[:, depth : 2 * depth] * live_column).astype(BF16)
        for part in range(2):
            lanes = slice(2 * depth + 128 * part, 2 * depth + 128 * part + 128)
            v_s[at, part, :, :128] = mixed[:, lanes].astype(BF16)
        g_s[at] = jax.nn.sigmoid(mixed[:, 3 * depth :])
    step = COL_STEP
    v_s[:, :, :, 128:] = jnp.ones(v_s.shape[:3] + (128,), BF16)

    def block(part, carry):
        here = pl.ds(pl.multiple_of(part * step, step), step)
        scores = [
            [scores_of(q_s[at, here, :], k_s[at], side) + offset for side in range(2)]
            for at in range(parts)
        ]
        for at in range(parts):
            output = jnp.concatenate(
                [weigh(scores[at][side], v_s[at, side]) for side in range(2)], 1
            )
            o_s[at, here, :] = (g_s[at, here, :] * output).astype(BF16)
        return carry

    lax.fori_loop(0, seqs // step, block, 0)
    for at in range(parts):
        y = take(y_s, pl.ds(at, seqs, stride=parts))
        done = (y + nn(o_s[at], wo_ref[...])).astype(BF16)
        groups = out_ref.shape[0]
        here = slice(seqs // groups * at, seqs // groups * at + seqs // groups)
        out_ref[:, here, :] = done.reshape(groups, seqs // groups, depth)
        normed = standardize(done.astype(F32)).astype(BF16)
        factors = nt(dyadic_ref[...], normed) * (live * chain_ref[first + at].astype(F32))
        for group in range(groups):
            to = slice(128 + 32 * at, 160 + 32 * at)
            out_ref[group, to, :] = factors[:32].astype(BF16)
        b_ref[pl.ds(32 * at, 32), :] = factors[32:].astype(BF16)


def col_attention(y, valid, chain, w, wo, dyadic_t, groups, after):
    sources, eight, depth = y.shape
    tokens = sources * eight
    seqs = tokens // 4
    return pl.pallas_call(
        col_kernel,
        in_specs=[VMEM] * 2 + [SMEM] + [VMEM] * 3 + [ORDER],
        out_specs=[VMEM] * 2,
        out_shape=[
            jax.ShapeDtypeStruct((groups, 2 * 4 * FACTOR_WIDTH, seqs), BF16),
            jax.ShapeDtypeStruct((4 * FACTOR_WIDTH, seqs), BF16),
        ],
        scratch_shapes=[
            pltpu.VMEM((2, tokens, depth // 2), F32),
            pltpu.VMEM((4, seqs, depth), F32),
            pltpu.VMEM((4, seqs, depth), BF16),
            pltpu.VMEM((4, 2, seqs, 256), BF16),
            pltpu.VMEM((4, seqs, depth), F32),
            pltpu.VMEM((4, seqs, depth), BF16),
        ],
        compiler_params=ROOM,
        cost_estimate=lasting(8),
        name="col_attention",
    )(y, valid, chain, w, wo, dyadic_t, after)


def assemble_kernel(*refs):
    pieces, (out_ref, d_s) = refs[:10], refs[11:]
    step = out_ref.shape[0]
    at = pl.program_id(0)

    def store(block, start, size, piece):
        d_s[block, start : start + size] = piece[...]

    @pl.when(at == 0)
    def _():
        place_halves(seq_index(), pieces, d_s.shape[1], store)

    upper = lax.broadcasted_iota(jnp.int32, (8, 8, 128), 1) < 4

    def line(one, carry):
        even, odd = [], []
        for pair in range(4):
            first = d_s[2 * pair, at * step + one].astype(F32).reshape(8, 8, 128)
            second = d_s[2 * pair + 1, at * step + one].astype(F32).reshape(8, 8, 128)
            even.append(jnp.where(upper, first, pltpu.roll(second, 4, 1)))
            odd.append(jnp.where(upper, pltpu.roll(first, 4, 1), second))
        both = jnp.stack([jnp.stack(even, 1), jnp.stack(odd, 1)], 1)
        out_ref[one] = both.reshape(512, 128).astype(BF16)
        return carry

    lax.fori_loop(0, step, line, 0, unroll=2)


def assemble(pieces, after):
    rows, columns, depth = pieces[0].shape
    step = ASSEMBLE_STEP
    return pl.pallas_call(
        assemble_kernel,
        grid=(rows // step,),
        in_specs=[VMEM] * len(pieces) + [ORDER],
        out_specs=pl.BlockSpec((step, 8 * columns, depth), lambda g: (g, 0, 0)),
        out_shape=jax.ShapeDtypeStruct((rows, 8 * columns, depth), BF16),
        scratch_shapes=[pltpu.VMEM((8, rows, columns, depth), BF16)],
        compiler_params=ROOM,
        cost_estimate=lasting(5),
        name="assemble",
    )(*pieces, after)


def spread_kernel(g_ref, w_ref, member_ref, _, out_ref):
    width = FACTOR_WIDTH
    scale = scale_of(member_ref[...])
    blank = jnp.zeros((64, 128), BF16)

    def pair(at, carry):
        parts = []
        for one in range(2):
            given = g_ref[2 * at + one]
            parts.append(jnp.concatenate([given, blank], 1))
            parts.append(jnp.concatenate([blank, given], 1))
        both = (nt(w_ref[...], jnp.concatenate(parts, 0)) * scale).astype(BF16)
        for one in range(2):
            here = pl.ds(pl.multiple_of((2 * at + one) * width, width), width)
            out_ref[here, :] = jnp.concatenate(
                [
                    both[width * e : width * e + width, 128 * one : 128 * one + 128]
                    for e in range(16)
                ],
                1,
            )
        return carry

    lax.fori_loop(0, g_ref.shape[0] // 2, pair, 0)


def spread_of(given, w, member, after):
    rows, columns, _ = given.shape
    return pl.pallas_call(
        spread_kernel,
        in_specs=[VMEM] * 3 + [ORDER],
        out_specs=VMEM,
        out_shape=jax.ShapeDtypeStruct((rows * FACTOR_WIDTH, columns * FACTOR_WIDTH), BF16),
        compiler_params=ROOM,
        cost_estimate=lasting(8),
        name="spread",
    )(given, w, member, after)


def couple_kernel(a_ref, bd_ref, w_ref, member_ref, out_ref, o_s):
    width = FACTOR_WIDTH
    rows, columns = o_s.shape
    for at in range(columns // 256):
        here = slice(256 * at, 256 * at + 256)
        o_s[:, here] = nt(a_ref[...], bd_ref[here, :]).astype(BF16)
    scale = scale_of(member_ref[...])
    w = w_ref[...].astype(F32).T.astype(BF16)
    low = lax.broadcasted_iota(jnp.int32, (128, 128), 1) < 64

    def pair(at, carry):
        outer = o_s[pl.ds(pl.multiple_of(at * 2 * width, 2 * width), 2 * width), :]
        stacks = []
        for one in range(2):
            part = outer[width * one : width * one + width]
            stacks.append(
                jnp.concatenate([part[:, 128 * e : 128 * e + 128] for e in range(16)], 0)
            )
        both = nn(w, jnp.concatenate(stacks, 1))
        top = jnp.where(low, both[:128, :128], pltpu.roll(both[:128, 128:], 64, 1))
        bottom = jnp.where(low, pltpu.roll(both[128:, :128], 64, 1), both[128:, 128:])
        delta = ((top + bottom) * scale).T
        out_ref[pl.ds(at * 2, 2)] = delta.reshape(2, 64, 128).astype(BF16)
        return carry

    lax.fori_loop(0, rows // (2 * width), pair, 0, unroll=PAIR_UNROLL)


def couple(a_all, bd, w, member):
    rows, columns = a_all.shape[0], bd.shape[0]
    return pl.pallas_call(
        couple_kernel,
        in_specs=[VMEM] * 4,
        out_specs=VMEM,
        out_shape=jax.ShapeDtypeStruct(
            (rows // FACTOR_WIDTH, columns // FACTOR_WIDTH, 128), BF16
        ),
        scratch_shapes=[pltpu.VMEM((rows, columns), BF16)],
        compiler_params=ROOM,
        cost_estimate=lasting(6),
        name="couple",
    )(a_all, bd, w, member)


def grads_kernel(both_ref, s_ref, *refs):
    b_pieces, (a_ref, bd_ref, ga_ref, own_ref, other_ref, turned_s) = refs[:4], refs[4:]
    width = FACTOR_WIDTH
    blocks = own_ref.shape[0]
    columns = turned_s.shape[1] // width
    core = lax.axis_index("core")
    x_lo, y = res_index()
    near, far = (0, 1, 3, 4), (2, 5, 6, 7)
    for other in range(2):
        for part, piece in zip((near, far), b_pieces[2 * other : 2 * other + 2]):
            for at, block in enumerate(part):
                to = ((y + block) & 3) * 2 + (x_lo ^ (block // 4))
                to = pl.multiple_of((to * 2 + (core ^ other)) * 128, 128)
                lines = piece[128 * at : 128 * at + 128, :]
                put(turned_s, pl.ds(to, 128), lines.astype(F32))
    for at in range(width):
        here = slice(at * columns, at * columns + columns)
        bd_ref[here, :] = take(turned_s, pl.ds(at, columns, stride=width)).astype(BF16)
    a_ref[...] = both_ref[:, 128:].reshape(a_ref.shape)
    left = a_ref[...].astype(F32).T.astype(BF16)
    for at in range(columns * width // 256):
        here = slice(256 * at, 256 * at + 256)
        put(turned_s, here, nn(left, s_ref[:, here]).T)
    for other, out_ref in ((1, other_ref), (0, own_ref)):
        for block in range(blocks):
            for part in range(4):
                column = (2 * block + (core ^ other)) * 4 + part
                lines = take(turned_s, pl.ds(column, width, stride=columns))
                out_ref[block, width * part : width * part + width, :] = lines.astype(BF16)
    for at in range(4):
        here = slice(256 * at, 256 * at + 256)
        ga_ref[:, here] = nn(s_ref[here, :], bd_ref[...]).T.astype(BF16)


def factor_grads(both, spread, b_pieces):
    seqs = both.shape[2]
    rows, columns = spread.shape
    shape = jax.ShapeDtypeStruct((columns // 256, 128, seqs), BF16)
    return pl.pallas_call(
        grads_kernel,
        in_specs=[VMEM] * 6,
        out_specs=[VMEM] * 5,
        out_shape=[
            jax.ShapeDtypeStruct((rows, seqs), BF16),
            jax.ShapeDtypeStruct((columns, seqs), BF16),
            jax.ShapeDtypeStruct((seqs, rows), BF16),
            shape,
            shape,
        ],
        scratch_shapes=[pltpu.VMEM((2, columns, seqs // 2), F32)],
        compiler_params=ROOM,
        cost_estimate=lasting(9),
        name="factor_grads",
    )(both, spread, *b_pieces)


def fold_kernel(own_ref, other_ref, out_ref):
    out_ref[...] = (own_ref[...].astype(F32) + other_ref[...].astype(F32)).astype(BF16)


def fold(own, other):
    return pl.pallas_call(
        fold_kernel,
        in_specs=[VMEM] * 2,
        out_specs=VMEM,
        out_shape=jax.ShapeDtypeStruct(own.shape, BF16),
        compiler_params=ROOM,
        cost_estimate=lasting(1),
        name="fold",
    )(own, other)


def pack_kernel(ga_ref, gb_ref, out_ref):
    groups, members, _ = out_ref.shape
    wide = ga_ref.shape[1]
    total = gb_ref[0].astype(F32)
    for at in range(1, gb_ref.shape[0]):
        total = total + gb_ref[at].astype(F32)
    out_ref[:, :, :wide] = ga_ref[...].reshape(groups, members, wide)
    out_ref[:, :, wide:] = total.T.reshape(groups, members, total.shape[0]).astype(BF16)


def pack_grads(ga, gb, groups):
    seqs, wide = ga.shape
    return pl.pallas_call(
        pack_kernel,
        in_specs=[VMEM] * 2,
        out_specs=VMEM,
        out_shape=jax.ShapeDtypeStruct((groups, seqs // groups, wide + gb.shape[1]), BF16),
        compiler_params=ROOM,
        cost_estimate=lasting(3),
        name="pack_grads",
    )(ga, gb)


def home_kernel(gf_ref, w_ref, x_ref, member_ref, chain_ref, x_out_ref, ct_ref, x_s, ct_s, live_s):
    width = FACTOR_WIDTH
    groups, rows, depth = x_ref.shape
    parts = 4
    seqs = rows // 2 // parts
    residues = groups * parts
    wide = residues * width
    x_hi, z = seq_index()
    x_lo, y = res_index()
    first = ((y * 2 + x_lo) * 2 + lax.axis_index("core")) * residues
    live_s[...] = jnp.broadcast_to(column_of(member_ref[...]), live_s.shape)
    member = live_s[pl.ds(pl.multiple_of((x_hi * 4 + z) * seqs, seqs), seqs), :1]
    total = gf_ref[0, :, :wide].astype(F32)
    for at in range(1, groups):
        total = total + gf_ref[at, :, :wide].astype(F32)
    lane = lax.broadcasted_iota(jnp.int32, (1, 128), 1) // width
    lines = []
    for group in range(groups):
        live = jnp.zeros((1, 128), F32)
        for at in range(parts):
            here = chain_ref[first + group * parts + at].astype(F32)
            live = jnp.where(lane == at, here, live)
        live = live * member
        left = total[:, 128 * group : 128 * group + 128] * live
        right = gf_ref[group, :, wide:].astype(F32) * live
        lines.append(jnp.concatenate([left, right], 1))
    given = jnp.concatenate(lines, 0)
    lane = lax.broadcasted_iota(jnp.int32, (1, depth), 1) // width % parts
    back = jnp.concatenate([w_ref[:width, :]] * parts + [w_ref[width:, :]] * parts, 0)
    for at in range(parts):
        upstream = nn(jnp.where(lane == at, given, 0.0).astype(BF16), back)
        x = x_ref[:, seqs * at : seqs * at + seqs]
        x = x.reshape(groups * seqs, depth).astype(F32)
        center = x - jnp.mean(x, -1, keepdims=True)
        inverse = lax.rsqrt(jnp.mean(center * center, -1, keepdims=True) + 1e-05)
        scaled = center * inverse
        cotangent = inverse * (
            upstream
            - jnp.mean(upstream, -1, keepdims=True)
            - scaled * jnp.mean(upstream * scaled, -1, keepdims=True)
        )
        for group in range(groups):
            here = pl.ds(group * parts + at, seqs, stride=residues)
            put(x_s, here, x[group * seqs : group * seqs + seqs])
            put(ct_s, here, cotangent[group * seqs : group * seqs + seqs])
    x_out_ref[...] = take(x_s, slice(None)).reshape(seqs, residues, depth).astype(BF16)
    ct_ref[...] = take(ct_s, slice(None)).reshape(seqs, residues, depth).astype(BF16)


def finish_home(gf, w, both, member, chain):
    groups, rows, depth = both.shape
    seqs, residues = rows // 8, groups * 4
    shape = (seqs, residues, depth)
    return pl.pallas_call(
        home_kernel,
        in_specs=[VMEM] * 4 + [SMEM],
        out_specs=[VMEM] * 2,
        out_shape=[jax.ShapeDtypeStruct(shape, BF16)] * 2,
        scratch_shapes=[pltpu.VMEM((2, seqs * residues, depth // 2), F32)] * 2
        + [pltpu.VMEM((member.shape[1], 128), F32)],
        compiler_params=ROOM,
        cost_estimate=lasting(6),
        name="finish_home",
    )(gf, w, both, member, chain)


def hold_kernel(*refs):
    pass


def hold(arrays, after):
    count = len(arrays)
    return pl.pallas_call(
        hold_kernel,
        in_specs=[ORDER] * (count + 1),
        out_specs=[ORDER] * count,
        out_shape=[jax.ShapeDtypeStruct(one.shape, one.dtype) for one in arrays],
        input_output_aliases={at: at for at in range(count)},
        cost_estimate=lasting(0.1),
        name="hold",
    )(*arrays, after)


def turn_by(steps):
    return [(at, (at + steps) % 4) for at in range(4)]


SWAP = [(0, 1), (1, 0)]


def ring(x, along, across, after=None):
    partner = lax.ppermute(x, across, SWAP)
    below = lax.ppermute(x, along, turn_by(1))
    above = lax.ppermute(x, along, turn_by(3))
    far = lax.ppermute(x, along, turn_by(2))
    if after is not None:
        partner, far = hold([partner, far], after)
    partner_below = lax.ppermute(partner, along, turn_by(1))
    partner_above = lax.ppermute(partner, along, turn_by(3))
    partner_far = lax.ppermute(far, across, SWAP)
    return [x, above, far, below, partner, partner_above, partner_far, partner_below]


def ring_halves(x, along, across):
    half = x.shape[0] // 2
    partner = lax.ppermute(x, across, SWAP)
    below = lax.ppermute(x, along, turn_by(1))
    above = lax.ppermute(x, along, turn_by(3))
    far_low = lax.ppermute(below[:half], along, turn_by(1))
    far_high = lax.ppermute(above[half:], along, turn_by(3))
    partner_below = lax.ppermute(partner, along, turn_by(1))
    partner_above = lax.ppermute(partner, along, turn_by(3))
    partner_low = lax.ppermute(far_low, across, SWAP)
    partner_high = lax.ppermute(far_high, across, SWAP)
    return [
        x, above, far_low, far_high, below,
        partner, partner_above, partner_low, partner_high, partner_below,
    ]


def per_device(
    multiple_alignment_rep,
    pair_rep,
    aligned_member_valid,
    chain_position_valid,
    horizontal_entry_matrices,
    horizontal_exit_matrix,
    bias_proj,
    vertical_entry_matrices,
    vertical_exit_matrix,
    dyadic_projection_matrices,
    outer_out,
    pair_grad,
):
    seqs_here, res_here, depth = multiple_alignment_rep.shape
    residues = pair_rep.shape[1]
    pair_width = outer_out.shape[1]
    q_size, b_size, r_size = 8, 8, 16
    width = FACTOR_WIDTH
    q_at = lax.axis_index("x_hi") * 4 + lax.axis_index("z")
    member = aligned_member_valid.reshape(1, -1)
    chain_row = chain_position_valid.reshape(1, residues)

    dyadic_t = dyadic_projection_matrices.T
    cube = outer_out.reshape(width, width // 2, 2, pair_width)
    w_outer = cube.transpose(1, 0, 2, 3).reshape(16 * width, 2 * pair_width)
    grad_here = lax.dynamic_index_in_dim(
        pair_grad.reshape(res_here, r_size, q_size, 4, pair_width), q_at, 2, keepdims=False
    ).reshape(res_here, r_size * 4, pair_width)

    bias = pair_bias(pair_rep, bias_proj.T, chain_row)
    x_rows = lax.all_to_all(
        multiple_alignment_rep.reshape(b_size, seqs_here // b_size, res_here, depth),
        ("y", "x_lo"), 0, 0, tiled=True,
    )
    (x_rows,) = hold([x_rows], bias)
    x_other = lax.ppermute(x_rows, "core", SWAP)
    q, k, v, g = row_entry(x_rows, x_other, chain_row, horizontal_entry_matrices)
    bias_pieces = ring(bias, "y", "x_lo", after=q)
    near, far = (0, 1, 3, 4), (2, 5, 6, 7)
    after_row = ()
    for part in (near, far):
        after_row = row_attention(
            [(at // 4, at % 4) for at in part], q, k, v, g, x_rows, horizontal_exit_matrix,
            [bias_pieces[at] for at in part], after_row,
        )
        after_row = [after_row]
    (after_row,) = after_row

    spread = spread_of(grad_here, w_outer, member, after_row)
    columns = lax.all_to_all(
        after_row.reshape(q_size * b_size, 16, depth),
        ("x_hi", "z", "y", "x_lo"), 0, 0, tiled=True,
    )
    going, factor_b = col_attention(
        columns, member, chain_position_valid,
        vertical_entry_matrices, vertical_exit_matrix, dyadic_t, q_size, spread,
    )
    b_ring = ring(factor_b, "y", "x_lo")
    b_pieces = [jnp.concatenate([b_ring[at] for at in part], 0) for part in (near, far)]
    b_pieces += [lax.ppermute(piece, "core", SWAP) for piece in b_pieces]
    back = lax.all_to_all(going, ("x_hi", "z"), 0, 0, tiled=True)

    a_all, bd, ga, gb, gb_other = factor_grads(back, spread, b_pieces)
    gb_other = lax.ppermute(gb_other, "core", SWAP)
    delta = couple(a_all, bd, w_outer, member)
    deltas = ring_halves(delta, "z", "x_hi")
    gb = fold(gb, gb_other)
    gb = lax.all_to_all(gb, ("y", "x_lo"), 0, 0, tiled=True)
    factors = lax.all_to_all(pack_grads(ga, gb, q_size), ("x_hi", "z"), 0, 0, tiled=True)
    alignment_refreshed, cotangent = finish_home(
        factors, dyadic_t, back, member, chain_position_valid
    )
    couple_delta = assemble(deltas, cotangent)
    return (alignment_refreshed, couple_delta, cotangent)


def solution(mesh):
    torus = jax.sharding.Mesh(
        mesh.devices.reshape(2, 4, 4, 2, 2), ("x_hi", "z", "y", "x_lo", "core")
    )
    seq, res = ("x_hi", "z"), ("y", "x_lo", "core")
    placed = (
        P(seq, res, None),
        P(res, None, None),
        P(),
        P(),
        P(),
        P(),
        P(),
        P(),
        P(),
        P(),
        P(),
        P(res, None, None),
    )
    return jax.shard_map(
        per_device,
        mesh=torus,
        in_specs=placed,
        out_specs=(P(seq, res, None), P(res, None, None), P(seq, res, None)),
        check_vma=False,
    )
```

```python
import functools

import jax
import jax.numpy as jnp
from jax import lax
from jax.experimental import pallas as pl
from jax.experimental.pallas import tpu as pltpu
from jax.sharding import PartitionSpec as P

FACTOR_WIDTH = 32
H = 8
HEAD_SIZE = 32
LOG2E = 1.4426950408889634
MASKED = -1000000000.0 * LOG2E
BF16 = jnp.bfloat16
F32 = jnp.float32
NT = (((1,), (1,)), ((), ()))
COL_STEP = 128
ROW_UNROLL = 4
PAIR_UNROLL = 8
BIAS_STEP = 8
ASSEMBLE_STEP = 8

VMEM = pl.BlockSpec(memory_space=pltpu.VMEM)
SMEM = pl.BlockSpec(memory_space=pltpu.SMEM)
ORDER = pl.BlockSpec(memory_space=pl.ANY)
TOKEN = jax.ShapeDtypeStruct((8, 128), jnp.float32)
ROOM = pltpu.CompilerParams(vmem_limit_bytes=24 * 1024 * 1024)


def lasting(microseconds):
    return pl.CostEstimate(
        flops=0, bytes_accessed=int(microseconds * 3.69e6), transcendentals=0
    )


def nn(left, right):
    return jnp.dot(left, right, preferred_element_type=F32)


def nt(left, right):
    return lax.dot_general(left, right, NT, preferred_element_type=F32)


def standardize(values):
    center = values - jnp.mean(values, -1, keepdims=True)
    spread = jnp.mean(center * center, -1, keepdims=True)
    return center * lax.rsqrt(spread + 1e-05)


def put(ref, rows, values):
    for half in range(2):
        ref[half, rows, :] = values[:, 128 * half : 128 * half + 128]


def take(ref, rows):
    return jnp.concatenate([ref[0, rows, :], ref[1, rows, :]], 1)


def column_of(row):
    return jnp.broadcast_to(row.astype(F32), (8, row.shape[1])).T[:, :1]


def seq_index():
    return lax.axis_index("x_hi"), lax.axis_index("z")


def res_index():
    return lax.axis_index("x_lo"), lax.axis_index("y")


def scale_of(member):
    return 1.0 / jnp.sum(member.astype(F32), keepdims=True)


def bias_kernel(pair_ref, proj_ref, valid_ref, out_ref, token_ref, turn_s):
    token_ref[...] = jnp.zeros_like(token_ref)
    at = pl.program_id(0)
    rows, residues, depth = pair_ref.shape
    line = lax.broadcasted_iota(jnp.int32, (depth, depth), 0)
    lane = lax.broadcasted_iota(jnp.int32, (depth, depth), 1)
    centering = (jnp.where(line == lane, 1.0, 0.0) - 1.0 / depth).astype(BF16)
    live = valid_ref[...] > 0
    proj = proj_ref[...].astype(F32)
    blank = jnp.zeros_like(proj)
    mean = jnp.full_like(proj, 1.0 / depth)
    sides = jnp.concatenate(
        [jnp.concatenate([proj, blank], 1), jnp.concatenate([blank, mean], 1)], 0
    ).astype(BF16)
    center = nn(pair_ref[...].reshape(rows * residues, depth), centering)
    both = jnp.concatenate([center.astype(BF16), (center * center).astype(BF16)], 1)
    for one in range(rows):
        sums = nt(sides, both[one * residues : one * residues + residues])
        bias = sums[:H] * lax.rsqrt(sums[H:] + 1e-05) * LOG2E
        bias = jnp.where(live, bias, MASKED)
        here = pl.ds(pl.multiple_of((at * rows + one) * H, H), H)
        for part in range(residues // 128):
            turn_s[part, here, :] = bias[:, 128 * part : 128 * part + 128]

    @pl.when(at == pl.num_programs(0) - 1)
    def _():
        total = out_ref.shape[0] // H
        for head in range(H):
            for part in range(residues // 128):
                out_ref[total * head : total * head + total, 128 * part : 128 * part + 128] = (
                    turn_s[part, pl.ds(head, total, stride=H), :].astype(BF16)
                )


def pair_bias(pair, proj, valid):
    rows, residues, depth = pair.shape
    step = BIAS_STEP
    return pl.pallas_call(
        bias_kernel,
        grid=(rows // step,),
        in_specs=[
            pl.BlockSpec((step, residues, depth), lambda g: (g, 0, 0)),
            pl.BlockSpec((H, depth), lambda g: (0, 0)),
            pl.BlockSpec((1, residues), lambda g: (0, 0)),
        ],
        out_specs=[
            pl.BlockSpec((rows * H, residues), lambda g: (0, 0)),
            pl.BlockSpec(TOKEN.shape, lambda g: (0, 0)),
        ],
        out_shape=[jax.ShapeDtypeStruct((rows * H, residues), BF16), TOKEN],
        scratch_shapes=[pltpu.VMEM((residues // 128, rows * H, 128), F32)],
        compiler_params=pltpu.CompilerParams(vmem_limit_bytes=56 * 1024 * 1024),
        cost_estimate=lasting(9),
        name="pair_bias",
    )(pair, proj, valid)


def scores_of(query, keys, side):
    lanes = slice(128 * side, 128 * side + 128)
    lane = lax.broadcasted_iota(jnp.int32, (1, 128), 1) // HEAD_SIZE
    part = query[:, lanes]
    spread = [jnp.where(lane == head, part, 0.0).astype(BF16) for head in range(4)]
    return nt(jnp.concatenate(spread, 0), keys[:, lanes])


def weigh(scores, values):
    rows = scores.shape[0] // 4
    lane = lax.broadcasted_iota(jnp.int32, (1, 128), 1) // HEAD_SIZE
    weights = jnp.exp2(scores - jnp.max(scores, -1, keepdims=True)).astype(BF16)
    both = nn(weights, values)
    summed, total = both[:rows, :128], both[:rows, 128:]
    for head in range(1, 4):
        here = slice(rows * head, rows * head + rows)
        summed = jnp.where(lane == head, both[here, :128], summed)
        total = jnp.where(lane == head, both[here, 128:], total)
    return summed / total


def entry_kernel(x_ref, other_ref, valid_ref, w_ref, q_ref, k_ref, v_ref, g_ref, token_ref, live_s):
    token_ref[...] = jnp.zeros_like(token_ref)
    blocks, seqs, rows, depth = x_ref.shape
    core = lax.axis_index("core")
    v_ref[:, :, :, 128:] = jnp.ones(v_ref.shape[:3] + (128,), BF16)
    live_s[...] = jnp.broadcast_to(column_of(valid_ref[...]), live_s.shape)
    for s in range(seqs):
        for other in range(2):
            source = other_ref if other else x_ref
            x = source[:, s].reshape(blocks * rows, depth)
            normed = standardize(x.astype(F32)).astype(BF16)
            pair = nn(normed, w_ref[:, depth : 3 * depth])
            side = 1 - core if other else core
            for at in range(blocks):
                here = slice(rows * at, rows * at + rows)
                to = pl.ds(pl.multiple_of((2 * at + side) * rows, rows), rows)
                k_ref[s, to, :] = (pair[here, :depth] * live_s[to, :1]).astype(BF16)
                for part in range(2):
                    lanes = slice(depth + 128 * part, depth + 128 * part + 128)
                    v_ref[s, part, to, :128] = pair[here, lanes].astype(BF16)
            if not other:
                query = nn(normed, w_ref[:, :depth]) * (HEAD_SIZE**-0.5 * LOG2E)
                q_ref[s] = query.astype(BF16)
                g_ref[s] = jax.nn.sigmoid(nn(normed, w_ref[:, 3 * depth :])).astype(BF16)


def row_entry(x, other, valid, w):
    blocks, seqs, rows, depth = x.shape
    here = jax.ShapeDtypeStruct((seqs, blocks * rows, depth), BF16)
    full = jax.ShapeDtypeStruct((seqs, 2 * blocks * rows, depth), BF16)
    sides = jax.ShapeDtypeStruct((seqs, 2, 2 * blocks * rows, 256), BF16)
    return pl.pallas_call(
        entry_kernel,
        in_specs=[VMEM] * 4,
        out_specs=[VMEM] * 5,
        out_shape=[here, full, sides, here, TOKEN],
        scratch_shapes=[pltpu.VMEM((2 * blocks * rows, 128), F32)],
        compiler_params=ROOM,
        cost_estimate=lasting(5),
        name="row_entry",
    )(x, other, valid, w)


def place(index, pieces, store):
    across, along = index
    for block, piece in enumerate(pieces):
        store((across ^ (block // 4)) * 4 + ((along + block) & 3), piece)


def place_halves(index, pieces, size, store):
    across, along = index
    pieces = list(pieces)
    for block in range(8):
        parts = 2 if block % 4 == 2 else 1
        for part in range(parts):
            at = (across ^ (block // 4)) * 4 + ((along + block) & 3)
            store(at, size // parts * part, size // parts, pieces.pop(0))


def row_kernel(steps, q_ref, k_ref, v_ref, g_ref, x_ref, wo_ref, *refs):
    count = len(steps)
    pieces, (out_ref, bias_s, after_s) = refs[:count], refs[-3:]
    blocks, seqs, rows, depth = x_ref.shape
    lines = count * rows
    for at, piece in enumerate(pieces):
        for head in range(H):
            to = lines * head + rows * at
            bias_s[to : to + rows, :] = piece[rows * head : rows * head + rows, :]
    for before in refs[count:-3]:
        out_ref[...] = before[...]
    x_lo, y = res_index()
    at_blocks = [((y + ahead) & 3) * 2 + (x_lo ^ across) for across, ahead in steps]
    spots = [pl.ds(pl.multiple_of(at * rows, rows), rows) for at in at_blocks]

    def sequence(s, carry):
        query = jnp.concatenate([q_ref[s, spot, :] for spot in spots], 0)
        gate = jnp.concatenate([g_ref[s, spot, :] for spot in spots], 0)
        x = jnp.concatenate([x_ref[at, s] for at in at_blocks], 0)
        sides = []
        for side in range(2):
            offset = bias_s[4 * lines * side : 4 * lines * side + 4 * lines, :].astype(F32)
            sides.append(scores_of(query, k_ref.at[s], side) + offset)
        output = jnp.concatenate([weigh(sides[side], v_ref[s, side]) for side in range(2)], 1)
        gated = (gate.astype(F32) * output).astype(BF16)
        after_s[s] = x.astype(F32) + nn(gated, wo_ref[...])
        return carry

    lax.fori_loop(0, seqs, sequence, 0, unroll=ROW_UNROLL)
    upper = lax.broadcasted_iota(jnp.int32, (rows // 8, 8, depth), 1) < 4
    for at, block in enumerate(at_blocks):
        even, odd = [], []
        for pair in range(seqs // 2):
            first, second = (
                after_s[one, rows * at : rows * at + rows, :].reshape(rows // 8, 8, depth)
                for one in (2 * pair, 2 * pair + 1)
            )
            even.append(jnp.where(upper, first, pltpu.roll(second, 4, 1)))
            odd.append(jnp.where(upper, pltpu.roll(first, 4, 1), second))
        even = jnp.concatenate(even, 1).astype(BF16)
        odd = jnp.concatenate(odd, 1).astype(BF16)
        for pair in range(rows // 8):
            out_ref[2 * pair, block] = even[pair]
            out_ref[2 * pair + 1, block] = odd[pair]


def row_attention(steps, q, k, v, g, x, wo, bias, before=()):
    blocks, seqs, rows, depth = x.shape
    return pl.pallas_call(
        functools.partial(row_kernel, steps),
        in_specs=[VMEM] * (6 + len(bias) + len(before)),
        out_specs=VMEM,
        out_shape=jax.ShapeDtypeStruct((rows // 4, blocks, 4 * seqs, depth), BF16),
        scratch_shapes=[
            pltpu.VMEM((len(bias) * bias[0].shape[0], bias[0].shape[1]), BF16),
            pltpu.VMEM((seqs, len(bias) * rows, depth), F32),
        ],
        compiler_params=ROOM,
        cost_estimate=lasting(8),
        name="row_attention",
    )(q, k, v, g, x, wo, *bias, *before)


def col_kernel(
    y_ref, valid_ref, chain_ref, w_ref, wo_ref, dyadic_ref, _,
    out_ref, b_ref, y_s, q_s, k_s, v_s, g_s, o_s,
):
    tokens, depth = y_s.shape[1], 2 * y_s.shape[2]
    parts = q_s.shape[0]
    seqs = tokens // parts
    live = valid_ref[...].astype(F32)
    live_column = column_of(live)
    offset = jnp.where(live > 0, 0.0, MASKED)
    x_hi, z = seq_index()
    x_lo, y_at = res_index()
    first = ((y_at * 2 + x_lo) * 2 + lax.axis_index("core")) * 32 + (x_hi * 4 + z) * parts
    put(y_s, slice(None), y_ref[...].reshape(tokens, depth).astype(F32))
    for at in range(parts):
        y = take(y_s, pl.ds(at, seqs, stride=parts))
        mixed = nn(standardize(y).astype(BF16), w_ref[...])
        q_s[at] = mixed[:, :depth] * (HEAD_SIZE**-0.5 * LOG2E)
        k_s[at] = (mixed[:, depth : 2 * depth] * live_column).astype(BF16)
        for part in range(2):
            lanes = slice(2 * depth + 128 * part, 2 * depth + 128 * part + 128)
            v_s[at, part, :, :128] = mixed[:, lanes].astype(BF16)
        g_s[at] = jax.nn.sigmoid(mixed[:, 3 * depth :])
    step = COL_STEP
    v_s[:, :, :, 128:] = jnp.ones(v_s.shape[:3] + (128,), BF16)

    def block(part, carry):
        here = pl.ds(pl.multiple_of(part * step, step), step)
        scores = [
            [scores_of(q_s[at, here, :], k_s[at], side) + offset for side in range(2)]
            for at in range(parts)
        ]
        for at in range(parts):
            output = jnp.concatenate(
                [weigh(scores[at][side], v_s[at, side]) for side in range(2)], 1
            )
            o_s[at, here, :] = (g_s[at, here, :] * output).astype(BF16)
        return carry

    lax.fori_loop(0, seqs // step, block, 0)
    for at in range(parts):
        y = take(y_s, pl.ds(at, seqs, stride=parts))
        done = (y + nn(o_s[at], wo_ref[...])).astype(BF16)
        groups = out_ref.shape[0]
        here = slice(seqs // groups * at, seqs // groups * at + seqs // groups)
        out_ref[:, here, :] = done.reshape(groups, seqs // groups, depth)
        normed = standardize(done.astype(F32)).astype(BF16)
        factors = nt(dyadic_ref[...], normed) * (live * chain_ref[first + at].astype(F32))
        for group in range(groups):
            to = slice(128 + 32 * at, 160 + 32 * at)
            out_ref[group, to, :] = factors[:32].astype(BF16)
        b_ref[pl.ds(32 * at, 32), :] = factors[32:].astype(BF16)


def col_attention(y, valid, chain, w, wo, dyadic_t, groups, after):
    sources, eight, depth = y.shape
    tokens = sources * eight
    seqs = tokens // 4
    return pl.pallas_call(
        col_kernel,
        in_specs=[VMEM] * 2 + [SMEM] + [VMEM] * 3 + [ORDER],
        out_specs=[VMEM] * 2,
        out_shape=[
            jax.ShapeDtypeStruct((groups, 2 * 4 * FACTOR_WIDTH, seqs), BF16),
            jax.ShapeDtypeStruct((4 * FACTOR_WIDTH, seqs), BF16),
        ],
        scratch_shapes=[
            pltpu.VMEM((2, tokens, depth // 2), F32),
            pltpu.VMEM((4, seqs, depth), F32),
            pltpu.VMEM((4, seqs, depth), BF16),
            pltpu.VMEM((4, 2, seqs, 256), BF16),
            pltpu.VMEM((4, seqs, depth), F32),
            pltpu.VMEM((4, seqs, depth), BF16),
        ],
        compiler_params=ROOM,
        cost_estimate=lasting(8),
        name="col_attention",
    )(y, valid, chain, w, wo, dyadic_t, after)


def assemble_kernel(*refs):
    pieces, (out_ref, d_s) = refs[:10], refs[11:]
    step = out_ref.shape[0]
    at = pl.program_id(0)

    def store(block, start, size, piece):
        d_s[block, start : start + size] = piece[...]

    @pl.when(at == 0)
    def _():
        place_halves(seq_index(), pieces, d_s.shape[1], store)

    upper = lax.broadcasted_iota(jnp.int32, (8, 8, 128), 1) < 4

    def line(one, carry):
        even, odd = [], []
        for pair in range(4):
            first = d_s[2 * pair, at * step + one].astype(F32).reshape(8, 8, 128)
            second = d_s[2 * pair + 1, at * step + one].astype(F32).reshape(8, 8, 128)
            even.append(jnp.where(upper, first, pltpu.roll(second, 4, 1)))
            odd.append(jnp.where(upper, pltpu.roll(first, 4, 1), second))
        both = jnp.stack([jnp.stack(even, 1), jnp.stack(odd, 1)], 1)
        out_ref[one] = both.reshape(512, 128).astype(BF16)
        return carry

    lax.fori_loop(0, step, line, 0, unroll=2)


def assemble(pieces, after):
    rows, columns, depth = pieces[0].shape
    step = ASSEMBLE_STEP
    return pl.pallas_call(
        assemble_kernel,
        grid=(rows // step,),
        in_specs=[VMEM] * len(pieces) + [ORDER],
        out_specs=pl.BlockSpec((step, 8 * columns, depth), lambda g: (g, 0, 0)),
        out_shape=jax.ShapeDtypeStruct((rows, 8 * columns, depth), BF16),
        scratch_shapes=[pltpu.VMEM((8, rows, columns, depth), BF16)],
        compiler_params=ROOM,
        cost_estimate=lasting(5),
        name="assemble",
    )(*pieces, after)


def spread_kernel(g_ref, w_ref, member_ref, _, out_ref, token_ref):
    token_ref[...] = jnp.zeros_like(token_ref)
    width = FACTOR_WIDTH
    scale = scale_of(member_ref[...])
    blank = jnp.zeros((64, 128), BF16)

    def pair(at, carry):
        parts = []
        for one in range(2):
            given = g_ref[2 * at + one]
            parts.append(jnp.concatenate([given, blank], 1))
            parts.append(jnp.concatenate([blank, given], 1))
        both = (nt(w_ref[...], jnp.concatenate(parts, 0)) * scale).astype(BF16)
        for one in range(2):
            here = pl.ds(pl.multiple_of((2 * at + one) * width, width), width)
            out_ref[here, :] = jnp.concatenate(
                [
                    both[width * e : width * e + width, 128 * one : 128 * one + 128]
                    for e in range(16)
                ],
                1,
            )
        return carry

    lax.fori_loop(0, g_ref.shape[0] // 2, pair, 0)


def spread_of(given, w, member, after):
    rows, columns, _ = given.shape
    return pl.pallas_call(
        spread_kernel,
        in_specs=[VMEM] * 3 + [ORDER],
        out_specs=[VMEM] * 2,
        out_shape=[
            jax.ShapeDtypeStruct((rows * FACTOR_WIDTH, columns * FACTOR_WIDTH), BF16),
            TOKEN,
        ],
        compiler_params=ROOM,
        cost_estimate=lasting(8),
        name="spread",
    )(given, w, member, after)


def couple_kernel(a_ref, bd_ref, w_ref, member_ref, out_ref, o_s):
    width = FACTOR_WIDTH
    rows, columns = o_s.shape
    for at in range(columns // 256):
        here = slice(256 * at, 256 * at + 256)
        o_s[:, here] = nt(a_ref[...], bd_ref[here, :]).astype(BF16)
    scale = scale_of(member_ref[...])
    w = w_ref[...].astype(F32).T.astype(BF16)
    low = lax.broadcasted_iota(jnp.int32, (128, 128), 1) < 64

    def pair(at, carry):
        outer = o_s[pl.ds(pl.multiple_of(at * 2 * width, 2 * width), 2 * width), :]
        stacks = []
        for one in range(2):
            part = outer[width * one : width * one + width]
            stacks.append(
                jnp.concatenate([part[:, 128 * e : 128 * e + 128] for e in range(16)], 0)
            )
        both = nn(w, jnp.concatenate(stacks, 1))
        top = jnp.where(low, both[:128, :128], pltpu.roll(both[:128, 128:], 64, 1))
        bottom = jnp.where(low, pltpu.roll(both[128:, :128], 64, 1), both[128:, 128:])
        delta = ((top + bottom) * scale).T
        out_ref[pl.ds(at * 2, 2)] = delta.reshape(2, 64, 128).astype(BF16)
        return carry

    lax.fori_loop(0, rows // (2 * width), pair, 0, unroll=PAIR_UNROLL)


def couple(a_all, bd, w, member):
    rows, columns = a_all.shape[0], bd.shape[0]
    return pl.pallas_call(
        couple_kernel,
        in_specs=[VMEM] * 4,
        out_specs=VMEM,
        out_shape=jax.ShapeDtypeStruct(
            (rows // FACTOR_WIDTH, columns // FACTOR_WIDTH, 128), BF16
        ),
        scratch_shapes=[pltpu.VMEM((rows, columns), BF16)],
        compiler_params=ROOM,
        cost_estimate=lasting(6),
        name="couple",
    )(a_all, bd, w, member)


def grads_kernel(both_ref, spread_ref, *refs):
    b_pieces, (a_ref, bd_ref, ga_ref, own_ref, other_ref, turned_s, s_ref, done) = refs[:4], refs[4:]
    fetch = pltpu.make_async_copy(spread_ref, s_ref, done)
    fetch.start()
    width = FACTOR_WIDTH
    blocks = own_ref.shape[0]
    columns = turned_s.shape[1] // width
    core = lax.axis_index("core")
    x_lo, y = res_index()
    near, far = (0, 1, 3, 4), (2, 5, 6, 7)
    for other in range(2):
        for part, piece in zip((near, far), b_pieces[2 * other : 2 * other + 2]):
            for at, block in enumerate(part):
                to = ((y + block) & 3) * 2 + (x_lo ^ (block // 4))
                to = pl.multiple_of((to * 2 + (core ^ other)) * 128, 128)
                lines = piece[128 * at : 128 * at + 128, :]
                put(turned_s, pl.ds(to, 128), lines.astype(F32))
    for at in range(width):
        here = slice(at * columns, at * columns + columns)
        bd_ref[here, :] = take(turned_s, pl.ds(at, columns, stride=width)).astype(BF16)
    a_ref[...] = both_ref[:, 128:].reshape(a_ref.shape)
    left = a_ref[...].astype(F32).T.astype(BF16)
    fetch.wait()
    for at in range(columns * width // 256):
        here = slice(256 * at, 256 * at + 256)
        put(turned_s, here, nn(left, s_ref[:, here]).T)
    for other, out_ref in ((1, other_ref), (0, own_ref)):
        for block in range(blocks):
            for part in range(4):
                column = (2 * block + (core ^ other)) * 4 + part
                lines = take(turned_s, pl.ds(column, width, stride=columns))
                out_ref[block, width * part : width * part + width, :] = lines.astype(BF16)
    for at in range(4):
        here = slice(256 * at, 256 * at + 256)
        ga_ref[:, here] = nn(s_ref[here, :], bd_ref[...]).T.astype(BF16)


def factor_grads(both, spread, b_pieces):
    seqs = both.shape[2]
    rows, columns = spread.shape
    shape = jax.ShapeDtypeStruct((columns // 256, 128, seqs), BF16)
    return pl.pallas_call(
        grads_kernel,
        in_specs=[VMEM, pl.BlockSpec(memory_space=pl.ANY)] + [VMEM] * 4,
        out_specs=[VMEM] * 5,
        out_shape=[
            jax.ShapeDtypeStruct((rows, seqs), BF16),
            jax.ShapeDtypeStruct((columns, seqs), BF16),
            jax.ShapeDtypeStruct((seqs, rows), BF16),
            shape,
            shape,
        ],
        scratch_shapes=[
            pltpu.VMEM((2, columns, seqs // 2), F32),
            pltpu.VMEM((rows, columns), BF16),
            pltpu.SemaphoreType.DMA(()),
        ],
        compiler_params=ROOM,
        cost_estimate=lasting(9),
        name="factor_grads",
    )(both, spread, *b_pieces)


def fold_kernel(own_ref, other_ref, out_ref):
    out_ref[...] = (own_ref[...].astype(F32) + other_ref[...].astype(F32)).astype(BF16)


def fold(own, other):
    return pl.pallas_call(
        fold_kernel,
        in_specs=[VMEM] * 2,
        out_specs=VMEM,
        out_shape=jax.ShapeDtypeStruct(own.shape, BF16),
        compiler_params=ROOM,
        cost_estimate=lasting(1),
        name="fold",
    )(own, other)


def pack_kernel(ga_ref, gb_ref, out_ref):
    groups, members, _ = out_ref.shape
    wide = ga_ref.shape[1]
    total = gb_ref[0].astype(F32)
    for at in range(1, gb_ref.shape[0]):
        total = total + gb_ref[at].astype(F32)
    out_ref[:, :, :wide] = ga_ref[...].reshape(groups, members, wide)
    out_ref[:, :, wide:] = total.T.reshape(groups, members, total.shape[0]).astype(BF16)


def pack_grads(ga, gb, groups):
    seqs, wide = ga.shape
    return pl.pallas_call(
        pack_kernel,
        in_specs=[VMEM] * 2,
        out_specs=VMEM,
        out_shape=jax.ShapeDtypeStruct((groups, seqs // groups, wide + gb.shape[1]), BF16),
        compiler_params=ROOM,
        cost_estimate=lasting(3),
        name="pack_grads",
    )(ga, gb)


def home_kernel(gf_ref, w_ref, x_ref, member_ref, chain_ref, x_out_ref, ct_ref, token_ref, x_s, ct_s, live_s):
    token_ref[...] = jnp.zeros_like(token_ref)
    width = FACTOR_WIDTH
    groups, rows, depth = x_ref.shape
    parts = 4
    seqs = rows // 2 // parts
    residues = groups * parts
    wide = residues * width
    x_hi, z = seq_index()
    x_lo, y = res_index()
    first = ((y * 2 + x_lo) * 2 + lax.axis_index("core")) * residues
    live_s[...] = jnp.broadcast_to(column_of(member_ref[...]), live_s.shape)
    member = live_s[pl.ds(pl.multiple_of((x_hi * 4 + z) * seqs, seqs), seqs), :1]
    total = gf_ref[0, :, :wide].astype(F32)
    for at in range(1, groups):
        total = total + gf_ref[at, :, :wide].astype(F32)
    lane = lax.broadcasted_iota(jnp.int32, (1, 128), 1) // width
    lines = []
    for group in range(groups):
        live = jnp.zeros((1, 128), F32)
        for at in range(parts):
            here = chain_ref[first + group * parts + at].astype(F32)
            live = jnp.where(lane == at, here, live)
        live = live * member
        left = total[:, 128 * group : 128 * group + 128] * live
        right = gf_ref[group, :, wide:].astype(F32) * live
        lines.append(jnp.concatenate([left, right], 1))
    given = jnp.concatenate(lines, 0)
    lane = lax.broadcasted_iota(jnp.int32, (1, depth), 1) // width % parts
    back = jnp.concatenate([w_ref[:width, :]] * parts + [w_ref[width:, :]] * parts, 0)
    for at in range(parts):
        upstream = nn(jnp.where(lane == at, given, 0.0).astype(BF16), back)
        x = x_ref[:, seqs * at : seqs * at + seqs]
        x = x.reshape(groups * seqs, depth).astype(F32)
        center = x - jnp.mean(x, -1, keepdims=True)
        inverse = lax.rsqrt(jnp.mean(center * center, -1, keepdims=True) + 1e-05)
        scaled = center * inverse
        cotangent = inverse * (
            upstream
            - jnp.mean(upstream, -1, keepdims=True)
            - scaled * jnp.mean(upstream * scaled, -1, keepdims=True)
        )
        for group in range(groups):
            here = pl.ds(group * parts + at, seqs, stride=residues)
            put(x_s, here, x[group * seqs : group * seqs + seqs])
            put(ct_s, here, cotangent[group * seqs : group * seqs + seqs])
    x_out_ref[...] = take(x_s, slice(None)).reshape(seqs, residues, depth).astype(BF16)
    ct_ref[...] = take(ct_s, slice(None)).reshape(seqs, residues, depth).astype(BF16)


def finish_home(gf, w, both, member, chain):
    groups, rows, depth = both.shape
    seqs, residues = rows // 8, groups * 4
    shape = (seqs, residues, depth)
    return pl.pallas_call(
        home_kernel,
        in_specs=[VMEM] * 4 + [SMEM],
        out_specs=[VMEM] * 3,
        out_shape=[jax.ShapeDtypeStruct(shape, BF16)] * 2 + [TOKEN],
        scratch_shapes=[pltpu.VMEM((2, seqs * residues, depth // 2), F32)] * 2
        + [pltpu.VMEM((member.shape[1], 128), F32)],
        compiler_params=ROOM,
        cost_estimate=lasting(6),
        name="finish_home",
    )(gf, w, both, member, chain)


def hold_kernel(*refs):
    pass


def hold(arrays, after):
    count = len(arrays)
    return pl.pallas_call(
        hold_kernel,
        in_specs=[ORDER] * (count + 1),
        out_specs=[ORDER] * count,
        out_shape=[jax.ShapeDtypeStruct(one.shape, one.dtype) for one in arrays],
        input_output_aliases={at: at for at in range(count)},
        cost_estimate=lasting(0.1),
        name="hold",
    )(*arrays, after)


def turn_by(steps):
    return [(at, (at + steps) % 4) for at in range(4)]


SWAP = [(0, 1), (1, 0)]


def ring(x, along, across, after=None):
    partner = lax.ppermute(x, across, SWAP)
    below = lax.ppermute(x, along, turn_by(1))
    above = lax.ppermute(x, along, turn_by(3))
    far = lax.ppermute(x, along, turn_by(2))
    if after is not None:
        partner, far = hold([partner, far], after)
    partner_below = lax.ppermute(partner, along, turn_by(1))
    partner_above = lax.ppermute(partner, along, turn_by(3))
    partner_far = lax.ppermute(far, across, SWAP)
    return [x, above, far, below, partner, partner_above, partner_far, partner_below]


def ring_halves(x, along, across):
    half = x.shape[0] // 2
    partner = lax.ppermute(x, across, SWAP)
    below = lax.ppermute(x, along, turn_by(1))
    above = lax.ppermute(x, along, turn_by(3))
    far_low = lax.ppermute(below[:half], along, turn_by(1))
    far_high = lax.ppermute(above[half:], along, turn_by(3))
    partner_below = lax.ppermute(partner, along, turn_by(1))
    partner_above = lax.ppermute(partner, along, turn_by(3))
    partner_low = lax.ppermute(far_low, across, SWAP)
    partner_high = lax.ppermute(far_high, across, SWAP)
    return [
        x, above, far_low, far_high, below,
        partner, partner_above, partner_low, partner_high, partner_below,
    ]


def per_device(
    multiple_alignment_rep,
    pair_rep,
    aligned_member_valid,
    chain_position_valid,
    horizontal_entry_matrices,
    horizontal_exit_matrix,
    bias_proj,
    vertical_entry_matrices,
    vertical_exit_matrix,
    dyadic_projection_matrices,
    outer_out,
    pair_grad,
):
    seqs_here, res_here, depth = multiple_alignment_rep.shape
    residues = pair_rep.shape[1]
    pair_width = outer_out.shape[1]
    q_size, b_size, r_size = 8, 8, 16
    width = FACTOR_WIDTH
    q_at = lax.axis_index("x_hi") * 4 + lax.axis_index("z")
    member = aligned_member_valid.reshape(1, -1)
    chain_row = chain_position_valid.reshape(1, residues)

    dyadic_t = dyadic_projection_matrices.T
    cube = outer_out.reshape(width, width // 2, 2, pair_width)
    w_outer = cube.transpose(1, 0, 2, 3).reshape(16 * width, 2 * pair_width)
    grad_here = lax.dynamic_index_in_dim(
        pair_grad.reshape(res_here, r_size, q_size, 4, pair_width), q_at, 2, keepdims=False
    ).reshape(res_here, r_size * 4, pair_width)

    bias, bias_token = pair_bias(pair_rep, bias_proj.T, chain_row)
    x_rows = lax.all_to_all(
        multiple_alignment_rep.reshape(b_size, seqs_here // b_size, res_here, depth),
        ("y", "x_lo"), 0, 0, tiled=True,
    )
    (x_rows,) = hold([x_rows], bias_token)
    x_other = lax.ppermute(x_rows, "core", SWAP)
    q, k, v, g, entry_token = row_entry(x_rows, x_other, chain_row, horizontal_entry_matrices)
    bias_pieces = ring(bias, "y", "x_lo", after=entry_token)
    near, far = (0, 1, 3, 4), (2, 5, 6, 7)
    after_row = ()
    for part in (near, far):
        after_row = row_attention(
            [(at // 4, at % 4) for at in part], q, k, v, g, x_rows, horizontal_exit_matrix,
            [bias_pieces[at] for at in part], after_row,
        )
        after_row = [after_row]
    (after_row,) = after_row

    spread, spread_token = spread_of(grad_here, w_outer, member, after_row)
    columns = lax.all_to_all(
        after_row.reshape(q_size * b_size, 16, depth),
        ("x_hi", "z", "y", "x_lo"), 0, 0, tiled=True,
    )
    going, factor_b = col_attention(
        columns, member, chain_position_valid,
        vertical_entry_matrices, vertical_exit_matrix, dyadic_t, q_size, spread_token,
    )
    b_ring = ring(factor_b, "y", "x_lo")
    b_pieces = [jnp.concatenate([b_ring[at] for at in part], 0) for part in (near, far)]
    b_pieces += [lax.ppermute(piece, "core", SWAP) for piece in b_pieces]
    back = lax.all_to_all(going, ("x_hi", "z"), 0, 0, tiled=True)

    a_all, bd, ga, gb, gb_other = factor_grads(back, spread, b_pieces)
    gb_other = lax.ppermute(gb_other, "core", SWAP)
    delta = couple(a_all, bd, w_outer, member)
    deltas = ring_halves(delta, "z", "x_hi")
    gb = fold(gb, gb_other)
    gb = lax.all_to_all(gb, ("y", "x_lo"), 0, 0, tiled=True)
    factors = lax.all_to_all(pack_grads(ga, gb, q_size), ("x_hi", "z"), 0, 0, tiled=True)
    alignment_refreshed, cotangent, home_token = finish_home(
        factors, dyadic_t, back, member, chain_position_valid
    )
    couple_delta = assemble(deltas, home_token)
    return (alignment_refreshed, couple_delta, cotangent)


def solution(mesh):
    torus = jax.sharding.Mesh(
        mesh.devices.reshape(2, 4, 4, 2, 2), ("x_hi", "z", "y", "x_lo", "core")
    )
    seq, res = ("x_hi", "z"), ("y", "x_lo", "core")
    placed = (
        P(seq, res, None),
        P(res, None, None),
        P(),
        P(),
        P(),
        P(),
        P(),
        P(),
        P(),
        P(),
        P(),
        P(res, None, None),
    )
    return jax.shard_map(
        per_device,
        mesh=torus,
        in_specs=placed,
        out_specs=(P(seq, res, None), P(res, None, None), P(seq, res, None)),
        check_vma=False,
    )
```

```python
import functools

import jax
import jax.numpy as jnp
from jax import lax
from jax.experimental import pallas as pl
from jax.experimental.pallas import tpu as pltpu
from jax.sharding import PartitionSpec as P

FACTOR_WIDTH = 32
H = 8
HEAD_SIZE = 32
LOG2E = 1.4426950408889634
MASKED = -1000000000.0 * LOG2E
BF16 = jnp.bfloat16
F32 = jnp.float32
NT = (((1,), (1,)), ((), ()))
COL_STEP = 128
ROW_UNROLL = 4
PAIR_UNROLL = 8
BIAS_STEP = 8
ASSEMBLE_STEP = 8

VMEM = pl.BlockSpec(memory_space=pltpu.VMEM)
SMEM = pl.BlockSpec(memory_space=pltpu.SMEM)
ORDER = pl.BlockSpec(memory_space=pl.ANY)
TOKEN = jax.ShapeDtypeStruct((8, 128), jnp.float32)
ROOM = pltpu.CompilerParams(vmem_limit_bytes=24 * 1024 * 1024)


def lasting(microseconds):
    return pl.CostEstimate(
        flops=0, bytes_accessed=int(microseconds * 3.69e6), transcendentals=0
    )


def nn(left, right):
    return jnp.dot(left, right, preferred_element_type=F32)


def nt(left, right):
    return lax.dot_general(left, right, NT, preferred_element_type=F32)


def standardize(values):
    center = values - jnp.mean(values, -1, keepdims=True)
    spread = jnp.mean(center * center, -1, keepdims=True)
    return center * lax.rsqrt(spread + 1e-05)


def put(ref, rows, values):
    for half in range(2):
        ref[half, rows, :] = values[:, 128 * half : 128 * half + 128]


def take(ref, rows):
    return jnp.concatenate([ref[0, rows, :], ref[1, rows, :]], 1)


def column_of(row):
    return jnp.broadcast_to(row.astype(F32), (8, row.shape[1])).T[:, :1]


def seq_index():
    return lax.axis_index("x_hi"), lax.axis_index("z")


def res_index():
    return lax.axis_index("x_lo"), lax.axis_index("y")


def scale_of(member):
    return 1.0 / jnp.sum(member.astype(F32), keepdims=True)


def bias_kernel(pair_ref, proj_ref, valid_ref, out_ref, token_ref, turn_s):
    token_ref[...] = jnp.zeros_like(token_ref)
    at = pl.program_id(0)
    rows, residues, depth = pair_ref.shape
    line = lax.broadcasted_iota(jnp.int32, (depth, depth), 0)
    lane = lax.broadcasted_iota(jnp.int32, (depth, depth), 1)
    centering = (jnp.where(line == lane, 1.0, 0.0) - 1.0 / depth).astype(BF16)
    live = valid_ref[...] > 0
    proj = proj_ref[...].astype(F32)
    blank = jnp.zeros_like(proj)
    mean = jnp.full_like(proj, 1.0 / depth)
    sides = jnp.concatenate(
        [jnp.concatenate([proj, blank], 1), jnp.concatenate([blank, mean], 1)], 0
    ).astype(BF16)
    center = nn(pair_ref[...].reshape(rows * residues, depth), centering)
    both = jnp.concatenate([center.astype(BF16), (center * center).astype(BF16)], 1)
    for one in range(rows):
        sums = nt(sides, both[one * residues : one * residues + residues])
        bias = sums[:H] * lax.rsqrt(sums[H:] + 1e-05) * LOG2E
        bias = jnp.where(live, bias, MASKED)
        here = pl.ds(pl.multiple_of((at * rows + one) * H, H), H)
        for part in range(residues // 128):
            turn_s[part, here, :] = bias[:, 128 * part : 128 * part + 128]

    @pl.when(at == pl.num_programs(0) - 1)
    def _():
        total = out_ref.shape[0] // H
        for head in range(H):
            for part in range(residues // 128):
                out_ref[total * head : total * head + total, 128 * part : 128 * part + 128] = (
                    turn_s[part, pl.ds(head, total, stride=H), :].astype(BF16)
                )


def pair_bias(pair, proj, valid):
    rows, residues, depth = pair.shape
    step = BIAS_STEP
    return pl.pallas_call(
        bias_kernel,
        grid=(rows // step,),
        in_specs=[
            pl.BlockSpec((step, residues, depth), lambda g: (g, 0, 0)),
            pl.BlockSpec((H, depth), lambda g: (0, 0)),
            pl.BlockSpec((1, residues), lambda g: (0, 0)),
        ],
        out_specs=[
            pl.BlockSpec((rows * H, residues), lambda g: (0, 0)),
            pl.BlockSpec(TOKEN.shape, lambda g: (0, 0)),
        ],
        out_shape=[jax.ShapeDtypeStruct((rows * H, residues), BF16), TOKEN],
        scratch_shapes=[pltpu.VMEM((residues // 128, rows * H, 128), F32)],
        compiler_params=pltpu.CompilerParams(vmem_limit_bytes=56 * 1024 * 1024),
        cost_estimate=lasting(9),
        name="pair_bias",
    )(pair, proj, valid)


def scores_of(query, keys, side):
    lanes = slice(128 * side, 128 * side + 128)
    lane = lax.broadcasted_iota(jnp.int32, (1, 128), 1) // HEAD_SIZE
    part = query[:, lanes]
    spread = [jnp.where(lane == head, part, 0.0).astype(BF16) for head in range(4)]
    return nt(jnp.concatenate(spread, 0), keys[:, lanes])


def weigh(scores, values):
    rows = scores.shape[0] // 4
    lane = lax.broadcasted_iota(jnp.int32, (1, 128), 1) // HEAD_SIZE
    weights = jnp.exp2(scores - jnp.max(scores, -1, keepdims=True)).astype(BF16)
    both = nn(weights, values)
    summed, total = both[:rows, :128], both[:rows, 128:]
    for head in range(1, 4):
        here = slice(rows * head, rows * head + rows)
        summed = jnp.where(lane == head, both[here, :128], summed)
        total = jnp.where(lane == head, both[here, 128:], total)
    return summed / total


def entry_kernel(x_ref, other_ref, valid_ref, w_ref, q_ref, k_ref, v_ref, g_ref, token_ref, live_s):
    token_ref[...] = jnp.zeros_like(token_ref)
    blocks, seqs, rows, depth = x_ref.shape
    core = lax.axis_index("core")
    v_ref[:, :, :, 128:] = jnp.ones(v_ref.shape[:3] + (128,), BF16)
    live_s[...] = jnp.broadcast_to(column_of(valid_ref[...]), live_s.shape)
    for s in range(seqs):
        for other in range(2):
            source = other_ref if other else x_ref
            x = source[:, s].reshape(blocks * rows, depth)
            normed = standardize(x.astype(F32)).astype(BF16)
            pair = nn(normed, w_ref[:, depth : 3 * depth])
            side = 1 - core if other else core
            for at in range(blocks):
                here = slice(rows * at, rows * at + rows)
                to = pl.ds(pl.multiple_of((2 * at + side) * rows, rows), rows)
                k_ref[s, to, :] = (pair[here, :depth] * live_s[to, :1]).astype(BF16)
                for part in range(2):
                    lanes = slice(depth + 128 * part, depth + 128 * part + 128)
                    v_ref[s, part, to, :128] = pair[here, lanes].astype(BF16)
            if not other:
                query = nn(normed, w_ref[:, :depth]) * (HEAD_SIZE**-0.5 * LOG2E)
                q_ref[s] = query.astype(BF16)
                g_ref[s] = jax.nn.sigmoid(nn(normed, w_ref[:, 3 * depth :])).astype(BF16)


def row_entry(x, other, valid, w):
    blocks, seqs, rows, depth = x.shape
    here = jax.ShapeDtypeStruct((seqs, blocks * rows, depth), BF16)
    full = jax.ShapeDtypeStruct((seqs, 2 * blocks * rows, depth), BF16)
    sides = jax.ShapeDtypeStruct((seqs, 2, 2 * blocks * rows, 256), BF16)
    return pl.pallas_call(
        entry_kernel,
        in_specs=[VMEM] * 4,
        out_specs=[VMEM] * 5,
        out_shape=[here, full, sides, here, TOKEN],
        scratch_shapes=[pltpu.VMEM((2 * blocks * rows, 128), F32)],
        compiler_params=ROOM,
        cost_estimate=lasting(5),
        name="row_entry",
    )(x, other, valid, w)


def place(index, pieces, store):
    across, along = index
    for block, piece in enumerate(pieces):
        store((across ^ (block // 4)) * 4 + ((along + block) & 3), piece)


def place_halves(index, pieces, size, store):
    across, along = index
    pieces = list(pieces)
    for block in range(8):
        parts = 2 if block % 4 == 2 else 1
        for part in range(parts):
            at = (across ^ (block // 4)) * 4 + ((along + block) & 3)
            store(at, size // parts * part, size // parts, pieces.pop(0))


def row_kernel(steps, q_ref, k_ref, v_ref, g_ref, x_ref, wo_ref, *refs):
    count = len(steps)
    pieces, (out_ref, bias_s, after_s) = refs[:count], refs[-3:]
    blocks, seqs, rows, depth = x_ref.shape
    lines = count * rows
    for at, piece in enumerate(pieces):
        for head in range(H):
            to = lines * head + rows * at
            bias_s[to : to + rows, :] = piece[rows * head : rows * head + rows, :]
    for before in refs[count:-3]:
        out_ref[...] = before[...]
    x_lo, y = res_index()
    at_blocks = [((y + ahead) & 3) * 2 + (x_lo ^ across) for across, ahead in steps]
    spots = [pl.ds(pl.multiple_of(at * rows, rows), rows) for at in at_blocks]

    def sequence(s, carry):
        query = jnp.concatenate([q_ref[s, spot, :] for spot in spots], 0)
        gate = jnp.concatenate([g_ref[s, spot, :] for spot in spots], 0)
        x = jnp.concatenate([x_ref[at, s] for at in at_blocks], 0)
        sides = []
        for side in range(2):
            offset = bias_s[4 * lines * side : 4 * lines * side + 4 * lines, :].astype(F32)
            sides.append(scores_of(query, k_ref.at[s], side) + offset)
        output = jnp.concatenate([weigh(sides[side], v_ref[s, side]) for side in range(2)], 1)
        gated = (gate.astype(F32) * output).astype(BF16)
        after_s[s] = x.astype(F32) + nn(gated, wo_ref[...])
        return carry

    lax.fori_loop(0, seqs, sequence, 0, unroll=ROW_UNROLL)
    upper = lax.broadcasted_iota(jnp.int32, (rows // 8, 8, depth), 1) < 4
    for at, block in enumerate(at_blocks):
        even, odd = [], []
        for pair in range(seqs // 2):
            first, second = (
                after_s[one, rows * at : rows * at + rows, :].reshape(rows // 8, 8, depth)
                for one in (2 * pair, 2 * pair + 1)
            )
            even.append(jnp.where(upper, first, pltpu.roll(second, 4, 1)))
            odd.append(jnp.where(upper, pltpu.roll(first, 4, 1), second))
        even = jnp.concatenate(even, 1).astype(BF16)
        odd = jnp.concatenate(odd, 1).astype(BF16)
        for pair in range(rows // 8):
            out_ref[2 * pair, block] = even[pair]
            out_ref[2 * pair + 1, block] = odd[pair]


def row_attention(steps, q, k, v, g, x, wo, bias, before=()):
    blocks, seqs, rows, depth = x.shape
    return pl.pallas_call(
        functools.partial(row_kernel, steps),
        in_specs=[VMEM] * (6 + len(bias) + len(before)),
        out_specs=VMEM,
        out_shape=jax.ShapeDtypeStruct((rows // 4, blocks, 4 * seqs, depth), BF16),
        scratch_shapes=[
            pltpu.VMEM((len(bias) * bias[0].shape[0], bias[0].shape[1]), BF16),
            pltpu.VMEM((seqs, len(bias) * rows, depth), F32),
        ],
        compiler_params=ROOM,
        cost_estimate=lasting(8),
        name="row_attention",
    )(q, k, v, g, x, wo, *bias, *before)


def col_kernel(
    y_ref, valid_ref, chain_ref, w_ref, wo_ref, dyadic_ref, _,
    out_ref, b_ref, y_s, q_s, k_s, v_s, g_s, o_s,
):
    tokens, depth = y_s.shape[1], 2 * y_s.shape[2]
    parts = q_s.shape[0]
    seqs = tokens // parts
    live = valid_ref[...].astype(F32)
    live_column = column_of(live)
    offset = jnp.where(live > 0, 0.0, MASKED)
    x_hi, z = seq_index()
    x_lo, y_at = res_index()
    first = ((y_at * 2 + x_lo) * 2 + lax.axis_index("core")) * 32 + (x_hi * 4 + z) * parts
    put(y_s, slice(None), y_ref[...].reshape(tokens, depth).astype(F32))
    for at in range(parts):
        y = take(y_s, pl.ds(at, seqs, stride=parts))
        mixed = nn(standardize(y).astype(BF16), w_ref[...])
        q_s[at] = mixed[:, :depth] * (HEAD_SIZE**-0.5 * LOG2E)
        k_s[at] = (mixed[:, depth : 2 * depth] * live_column).astype(BF16)
        for part in range(2):
            lanes = slice(2 * depth + 128 * part, 2 * depth + 128 * part + 128)
            v_s[at, part, :, :128] = mixed[:, lanes].astype(BF16)
        g_s[at] = jax.nn.sigmoid(mixed[:, 3 * depth :])
    step = COL_STEP
    v_s[:, :, :, 128:] = jnp.ones(v_s.shape[:3] + (128,), BF16)

    def block(part, carry):
        here = pl.ds(pl.multiple_of(part * step, step), step)
        scores = [
            [scores_of(q_s[at, here, :], k_s[at], side) + offset for side in range(2)]
            for at in range(parts)
        ]
        for at in range(parts):
            output = jnp.concatenate(
                [weigh(scores[at][side], v_s[at, side]) for side in range(2)], 1
            )
            o_s[at, here, :] = (g_s[at, here, :] * output).astype(BF16)
        return carry

    lax.fori_loop(0, seqs // step, block, 0)
    for at in range(parts):
        y = take(y_s, pl.ds(at, seqs, stride=parts))
        done = (y + nn(o_s[at], wo_ref[...])).astype(BF16)
        groups = out_ref.shape[0]
        here = slice(seqs // groups * at, seqs // groups * at + seqs // groups)
        out_ref[:, here, :] = done.reshape(groups, seqs // groups, depth)
        normed = standardize(done.astype(F32)).astype(BF16)
        factors = nt(dyadic_ref[...], normed) * (live * chain_ref[first + at].astype(F32))
        for group in range(groups):
            to = slice(128 + 32 * at, 160 + 32 * at)
            out_ref[group, to, :] = factors[:32].astype(BF16)
        b_ref[pl.ds(32 * at, 32), :] = factors[32:].astype(BF16)


def col_attention(y, valid, chain, w, wo, dyadic_t, groups, after):
    sources, eight, depth = y.shape
    tokens = sources * eight
    seqs = tokens // 4
    return pl.pallas_call(
        col_kernel,
        in_specs=[VMEM] * 2 + [SMEM] + [VMEM] * 3 + [ORDER],
        out_specs=[VMEM] * 2,
        out_shape=[
            jax.ShapeDtypeStruct((groups, 2 * 4 * FACTOR_WIDTH, seqs), BF16),
            jax.ShapeDtypeStruct((4 * FACTOR_WIDTH, seqs), BF16),
        ],
        scratch_shapes=[
            pltpu.VMEM((2, tokens, depth // 2), F32),
            pltpu.VMEM((4, seqs, depth), F32),
            pltpu.VMEM((4, seqs, depth), BF16),
            pltpu.VMEM((4, 2, seqs, 256), BF16),
            pltpu.VMEM((4, seqs, depth), F32),
            pltpu.VMEM((4, seqs, depth), BF16),
        ],
        compiler_params=ROOM,
        cost_estimate=lasting(8),
        name="col_attention",
    )(y, valid, chain, w, wo, dyadic_t, after)


def assemble_kernel(*refs):
    pieces, (out_ref, d_s) = refs[:10], refs[11:]
    step = out_ref.shape[0]
    at = pl.program_id(0)

    def store(block, start, size, piece):
        d_s[block, start : start + size] = piece[...]

    @pl.when(at == 0)
    def _():
        place_halves(seq_index(), pieces, d_s.shape[1], store)

    upper = lax.broadcasted_iota(jnp.int32, (8, 8, 128), 1) < 4

    def line(one, carry):
        even, odd = [], []
        for pair in range(4):
            first = d_s[2 * pair, at * step + one].astype(F32).reshape(8, 8, 128)
            second = d_s[2 * pair + 1, at * step + one].astype(F32).reshape(8, 8, 128)
            even.append(jnp.where(upper, first, pltpu.roll(second, 4, 1)))
            odd.append(jnp.where(upper, pltpu.roll(first, 4, 1), second))
        both = jnp.stack([jnp.stack(even, 1), jnp.stack(odd, 1)], 1)
        out_ref[one] = both.reshape(512, 128).astype(BF16)
        return carry

    lax.fori_loop(0, step, line, 0, unroll=2)


def assemble(pieces, after):
    rows, columns, depth = pieces[0].shape
    step = ASSEMBLE_STEP
    return pl.pallas_call(
        assemble_kernel,
        grid=(rows // step,),
        in_specs=[VMEM] * len(pieces) + [ORDER],
        out_specs=pl.BlockSpec((step, 8 * columns, depth), lambda g: (g, 0, 0)),
        out_shape=jax.ShapeDtypeStruct((rows, 8 * columns, depth), BF16),
        scratch_shapes=[pltpu.VMEM((8, rows, columns, depth), BF16)],
        compiler_params=ROOM,
        cost_estimate=lasting(5),
        name="assemble",
    )(*pieces, after)


def spread_kernel(g_ref, w_ref, member_ref, _, out_ref, token_ref):
    token_ref[...] = jnp.zeros_like(token_ref)
    width = FACTOR_WIDTH
    scale = scale_of(member_ref[...])
    blank = jnp.zeros((64, 128), BF16)

    def pair(at, carry):
        parts = []
        for one in range(2):
            given = g_ref[2 * at + one]
            parts.append(jnp.concatenate([given, blank], 1))
            parts.append(jnp.concatenate([blank, given], 1))
        both = (nt(w_ref[...], jnp.concatenate(parts, 0)) * scale).astype(BF16)
        for one in range(2):
            here = pl.ds(pl.multiple_of((2 * at + one) * width, width), width)
            out_ref[here, :] = jnp.concatenate(
                [
                    both[width * e : width * e + width, 128 * one : 128 * one + 128]
                    for e in range(16)
                ],
                1,
            )
        return carry

    lax.fori_loop(0, g_ref.shape[0] // 2, pair, 0)


def spread_of(given, w, member, after):
    rows, columns, _ = given.shape
    return pl.pallas_call(
        spread_kernel,
        in_specs=[VMEM] * 3 + [ORDER],
        out_specs=[VMEM] * 2,
        out_shape=[
            jax.ShapeDtypeStruct((rows * FACTOR_WIDTH, columns * FACTOR_WIDTH), BF16),
            TOKEN,
        ],
        compiler_params=ROOM,
        cost_estimate=lasting(8),
        name="spread",
    )(given, w, member, after)


def couple_kernel(a_ref, bd_ref, w_ref, member_ref, out_ref, o_s):
    width = FACTOR_WIDTH
    rows, columns = o_s.shape
    for at in range(columns // 256):
        here = slice(256 * at, 256 * at + 256)
        o_s[:, here] = nt(a_ref[...], bd_ref[here, :]).astype(BF16)
    scale = scale_of(member_ref[...])
    w = w_ref[...].astype(F32).T.astype(BF16)
    low = lax.broadcasted_iota(jnp.int32, (128, 128), 1) < 64

    def pair(at, carry):
        outer = o_s[pl.ds(pl.multiple_of(at * 2 * width, 2 * width), 2 * width), :]
        stacks = []
        for one in range(2):
            part = outer[width * one : width * one + width]
            stacks.append(
                jnp.concatenate([part[:, 128 * e : 128 * e + 128] for e in range(16)], 0)
            )
        both = nn(w, jnp.concatenate(stacks, 1))
        top = jnp.where(low, both[:128, :128], pltpu.roll(both[:128, 128:], 64, 1))
        bottom = jnp.where(low, pltpu.roll(both[128:, :128], 64, 1), both[128:, 128:])
        delta = ((top + bottom) * scale).T
        out_ref[pl.ds(at * 2, 2)] = delta.reshape(2, 64, 128).astype(BF16)
        return carry

    lax.fori_loop(0, rows // (2 * width), pair, 0, unroll=PAIR_UNROLL)


def couple(a_all, bd, w, member):
    rows, columns = a_all.shape[0], bd.shape[0]
    return pl.pallas_call(
        couple_kernel,
        in_specs=[VMEM] * 4,
        out_specs=VMEM,
        out_shape=jax.ShapeDtypeStruct(
            (rows // FACTOR_WIDTH, columns // FACTOR_WIDTH, 128), BF16
        ),
        scratch_shapes=[pltpu.VMEM((rows, columns), BF16)],
        compiler_params=ROOM,
        cost_estimate=lasting(6),
        name="couple",
    )(a_all, bd, w, member)


def grads_kernel(both_ref, s_ref, *refs):
    b_pieces, (a_ref, bd_ref, ga_ref, own_ref, other_ref, turned_s) = refs[:4], refs[4:]
    width = FACTOR_WIDTH
    blocks = own_ref.shape[0]
    columns = turned_s.shape[1] // width
    core = lax.axis_index("core")
    x_lo, y = res_index()
    near, far = (0, 1, 3, 4), (2, 5, 6, 7)
    for other in range(2):
        for part, piece in zip((near, far), b_pieces[2 * other : 2 * other + 2]):
            for at, block in enumerate(part):
                to = ((y + block) & 3) * 2 + (x_lo ^ (block // 4))
                to = pl.multiple_of((to * 2 + (core ^ other)) * 128, 128)
                lines = piece[128 * at : 128 * at + 128, :]
                put(turned_s, pl.ds(to, 128), lines.astype(F32))
    for at in range(width):
        here = slice(at * columns, at * columns + columns)
        bd_ref[here, :] = take(turned_s, pl.ds(at, columns, stride=width)).astype(BF16)
    a_ref[...] = both_ref[:, 128:].reshape(a_ref.shape)
    left = a_ref[...].astype(F32).T.astype(BF16)
    for at in range(columns * width // 256):
        here = slice(256 * at, 256 * at + 256)
        put(turned_s, here, nn(left, s_ref[:, here]).T)
    for other, out_ref in ((1, other_ref), (0, own_ref)):
        for block in range(blocks):
            for part in range(4):
                column = (2 * block + (core ^ other)) * 4 + part
                lines = take(turned_s, pl.ds(column, width, stride=columns))
                out_ref[block, width * part : width * part + width, :] = lines.astype(BF16)
    for at in range(4):
        here = slice(256 * at, 256 * at + 256)
        ga_ref[:, here] = nn(s_ref[here, :], bd_ref[...]).T.astype(BF16)


def factor_grads(both, spread, b_pieces):
    seqs = both.shape[2]
    rows, columns = spread.shape
    shape = jax.ShapeDtypeStruct((columns // 256, 128, seqs), BF16)
    return pl.pallas_call(
        grads_kernel,
        in_specs=[VMEM] * 6,
        out_specs=[VMEM] * 5,
        out_shape=[
            jax.ShapeDtypeStruct((rows, seqs), BF16),
            jax.ShapeDtypeStruct((columns, seqs), BF16),
            jax.ShapeDtypeStruct((seqs, rows), BF16),
            shape,
            shape,
        ],
        scratch_shapes=[pltpu.VMEM((2, columns, seqs // 2), F32)],
        compiler_params=ROOM,
        cost_estimate=lasting(9),
        name="factor_grads",
    )(both, spread, *b_pieces)


def fold_kernel(own_ref, other_ref, out_ref):
    out_ref[...] = (own_ref[...].astype(F32) + other_ref[...].astype(F32)).astype(BF16)


def fold(own, other):
    return pl.pallas_call(
        fold_kernel,
        in_specs=[VMEM] * 2,
        out_specs=VMEM,
        out_shape=jax.ShapeDtypeStruct(own.shape, BF16),
        compiler_params=ROOM,
        cost_estimate=lasting(1),
        name="fold",
    )(own, other)


def pack_kernel(ga_ref, gb_ref, out_ref):
    groups, members, _ = out_ref.shape
    wide = ga_ref.shape[1]
    total = gb_ref[0].astype(F32)
    for at in range(1, gb_ref.shape[0]):
        total = total + gb_ref[at].astype(F32)
    out_ref[:, :, :wide] = ga_ref[...].reshape(groups, members, wide)
    out_ref[:, :, wide:] = total.T.reshape(groups, members, total.shape[0]).astype(BF16)


def pack_grads(ga, gb, groups):
    seqs, wide = ga.shape
    return pl.pallas_call(
        pack_kernel,
        in_specs=[VMEM] * 2,
        out_specs=VMEM,
        out_shape=jax.ShapeDtypeStruct((groups, seqs // groups, wide + gb.shape[1]), BF16),
        compiler_params=ROOM,
        cost_estimate=lasting(3),
        name="pack_grads",
    )(ga, gb)


def home_kernel(gf_ref, w_ref, x_ref, member_ref, chain_ref, x_out_ref, ct_ref, token_ref, x_s, ct_s, live_s):
    token_ref[...] = jnp.zeros_like(token_ref)
    width = FACTOR_WIDTH
    groups, rows, depth = x_ref.shape
    parts = 4
    seqs = rows // 2 // parts
    residues = groups * parts
    wide = residues * width
    x_hi, z = seq_index()
    x_lo, y = res_index()
    first = ((y * 2 + x_lo) * 2 + lax.axis_index("core")) * residues
    live_s[...] = jnp.broadcast_to(column_of(member_ref[...]), live_s.shape)
    member = live_s[pl.ds(pl.multiple_of((x_hi * 4 + z) * seqs, seqs), seqs), :1]
    total = gf_ref[0, :, :wide].astype(F32)
    for at in range(1, groups):
        total = total + gf_ref[at, :, :wide].astype(F32)
    lane = lax.broadcasted_iota(jnp.int32, (1, 128), 1) // width
    lines = []
    for group in range(groups):
        live = jnp.zeros((1, 128), F32)
        for at in range(parts):
            here = chain_ref[first + group * parts + at].astype(F32)
            live = jnp.where(lane == at, here, live)
        live = live * member
        left = total[:, 128 * group : 128 * group + 128] * live
        right = gf_ref[group, :, wide:].astype(F32) * live
        lines.append(jnp.concatenate([left, right], 1))
    given = jnp.concatenate(lines, 0)
    lane = lax.broadcasted_iota(jnp.int32, (1, depth), 1) // width % parts
    back = jnp.concatenate([w_ref[:width, :]] * parts + [w_ref[width:, :]] * parts, 0)
    for at in range(parts):
        upstream = nn(jnp.where(lane == at, given, 0.0).astype(BF16), back)
        x = x_ref[:, seqs * at : seqs * at + seqs]
        x = x.reshape(groups * seqs, depth).astype(F32)
        center = x - jnp.mean(x, -1, keepdims=True)
        inverse = lax.rsqrt(jnp.mean(center * center, -1, keepdims=True) + 1e-05)
        scaled = center * inverse
        cotangent = inverse * (
            upstream
            - jnp.mean(upstream, -1, keepdims=True)
            - scaled * jnp.mean(upstream * scaled, -1, keepdims=True)
        )
        for group in range(groups):
            here = pl.ds(group * parts + at, seqs, stride=residues)
            put(x_s, here, x[group * seqs : group * seqs + seqs])
            put(ct_s, here, cotangent[group * seqs : group * seqs + seqs])
    x_out_ref[...] = take(x_s, slice(None)).reshape(seqs, residues, depth).astype(BF16)
    ct_ref[...] = take(ct_s, slice(None)).reshape(seqs, residues, depth).astype(BF16)


def finish_home(gf, w, both, member, chain):
    groups, rows, depth = both.shape
    seqs, residues = rows // 8, groups * 4
    shape = (seqs, residues, depth)
    return pl.pallas_call(
        home_kernel,
        in_specs=[VMEM] * 4 + [SMEM],
        out_specs=[VMEM] * 3,
        out_shape=[jax.ShapeDtypeStruct(shape, BF16)] * 2 + [TOKEN],
        scratch_shapes=[pltpu.VMEM((2, seqs * residues, depth // 2), F32)] * 2
        + [pltpu.VMEM((member.shape[1], 128), F32)],
        compiler_params=ROOM,
        cost_estimate=lasting(6),
        name="finish_home",
    )(gf, w, both, member, chain)


def hold_kernel(*refs):
    pass


def hold(arrays, after):
    count = len(arrays)
    return pl.pallas_call(
        hold_kernel,
        in_specs=[ORDER] * (count + 1),
        out_specs=[ORDER] * count,
        out_shape=[jax.ShapeDtypeStruct(one.shape, one.dtype) for one in arrays],
        input_output_aliases={at: at for at in range(count)},
        cost_estimate=lasting(0.1),
        name="hold",
    )(*arrays, after)


def turn_by(steps):
    return [(at, (at + steps) % 4) for at in range(4)]


SWAP = [(0, 1), (1, 0)]


def ring(x, along, across, after=None):
    partner = lax.ppermute(x, across, SWAP)
    below = lax.ppermute(x, along, turn_by(1))
    above = lax.ppermute(x, along, turn_by(3))
    far = lax.ppermute(x, along, turn_by(2))
    if after is not None:
        partner, far = hold([partner, far], after)
    partner_below = lax.ppermute(partner, along, turn_by(1))
    partner_above = lax.ppermute(partner, along, turn_by(3))
    partner_far = lax.ppermute(far, across, SWAP)
    return [x, above, far, below, partner, partner_above, partner_far, partner_below]


def ring_halves(x, along, across):
    half = x.shape[0] // 2
    partner = lax.ppermute(x, across, SWAP)
    below = lax.ppermute(x, along, turn_by(1))
    above = lax.ppermute(x, along, turn_by(3))
    far_low = lax.ppermute(below[:half], along, turn_by(1))
    far_high = lax.ppermute(above[half:], along, turn_by(3))
    partner_below = lax.ppermute(partner, along, turn_by(1))
    partner_above = lax.ppermute(partner, along, turn_by(3))
    partner_low = lax.ppermute(far_low, across, SWAP)
    partner_high = lax.ppermute(far_high, across, SWAP)
    return [
        x, above, far_low, far_high, below,
        partner, partner_above, partner_low, partner_high, partner_below,
    ]


def per_device(
    multiple_alignment_rep,
    pair_rep,
    aligned_member_valid,
    chain_position_valid,
    horizontal_entry_matrices,
    horizontal_exit_matrix,
    bias_proj,
    vertical_entry_matrices,
    vertical_exit_matrix,
    dyadic_projection_matrices,
    outer_out,
    pair_grad,
):
    seqs_here, res_here, depth = multiple_alignment_rep.shape
    residues = pair_rep.shape[1]
    pair_width = outer_out.shape[1]
    q_size, b_size, r_size = 8, 8, 16
    width = FACTOR_WIDTH
    q_at = lax.axis_index("x_hi") * 4 + lax.axis_index("z")
    member = aligned_member_valid.reshape(1, -1)
    chain_row = chain_position_valid.reshape(1, residues)

    dyadic_t = dyadic_projection_matrices.T
    cube = outer_out.reshape(width, width // 2, 2, pair_width)
    w_outer = cube.transpose(1, 0, 2, 3).reshape(16 * width, 2 * pair_width)
    grad_here = lax.dynamic_index_in_dim(
        pair_grad.reshape(res_here, r_size, q_size, 4, pair_width), q_at, 2, keepdims=False
    ).reshape(res_here, r_size * 4, pair_width)

    bias, bias_token = pair_bias(pair_rep, bias_proj.T, chain_row)
    x_rows = lax.all_to_all(
        multiple_alignment_rep.reshape(b_size, seqs_here // b_size, res_here, depth),
        ("y", "x_lo"), 0, 0, tiled=True,
    )
    (x_rows,) = hold([x_rows], bias_token)
    x_other = lax.ppermute(x_rows, "core", SWAP)
    q, k, v, g, entry_token = row_entry(x_rows, x_other, chain_row, horizontal_entry_matrices)
    bias_pieces = ring(bias, "y", "x_lo", after=entry_token)
    near, far = (0, 1, 3, 4), (2, 5, 6, 7)
    after_row = ()
    for part in (near, far):
        after_row = row_attention(
            [(at // 4, at % 4) for at in part], q, k, v, g, x_rows, horizontal_exit_matrix,
            [bias_pieces[at] for at in part], after_row,
        )
        after_row = [after_row]
    (after_row,) = after_row

    spread, spread_token = spread_of(grad_here, w_outer, member, after_row)
    columns = lax.all_to_all(
        after_row.reshape(q_size * b_size, 16, depth),
        ("x_hi", "z", "y", "x_lo"), 0, 0, tiled=True,
    )
    going, factor_b = col_attention(
        columns, member, chain_position_valid,
        vertical_entry_matrices, vertical_exit_matrix, dyadic_t, q_size, spread_token,
    )
    b_ring = ring(factor_b, "y", "x_lo")
    b_pieces = [jnp.concatenate([b_ring[at] for at in part], 0) for part in (near, far)]
    b_pieces += [lax.ppermute(piece, "core", SWAP) for piece in b_pieces]
    back = lax.all_to_all(going, ("x_hi", "z"), 0, 0, tiled=True)

    a_all, bd, ga, gb, gb_other = factor_grads(back, spread, b_pieces)
    gb_other = lax.ppermute(gb_other, "core", SWAP)
    delta = couple(a_all, bd, w_outer, member)
    deltas = ring_halves(delta, "z", "x_hi")
    gb = fold(gb, gb_other)
    gb = lax.all_to_all(gb, ("y", "x_lo"), 0, 0, tiled=True)
    factors = lax.all_to_all(pack_grads(ga, gb, q_size), ("x_hi", "z"), 0, 0, tiled=True)
    alignment_refreshed, cotangent, home_token = finish_home(
        factors, dyadic_t, back, member, chain_position_valid
    )
    couple_delta = assemble(deltas, home_token)
    return (alignment_refreshed, couple_delta, cotangent)


def solution(mesh):
    torus = jax.sharding.Mesh(
        mesh.devices.reshape(2, 4, 4, 2, 2), ("x_hi", "z", "y", "x_lo", "core")
    )
    seq, res = ("x_hi", "z"), ("y", "x_lo", "core")
    placed = (
        P(seq, res, None),
        P(res, None, None),
        P(),
        P(),
        P(),
        P(),
        P(),
        P(),
        P(),
        P(),
        P(),
        P(res, None, None),
    )
    return jax.shard_map(
        per_device,
        mesh=torus,
        in_specs=placed,
        out_specs=(P(seq, res, None), P(res, None, None), P(seq, res, None)),
        check_vma=False,
    )
```
